32 devices in a mesh: section: 2 (over y), dp: 16 (over z, x, core).
Axes of the slice: x: 2, y: 2, z: 4, core: 2. Of those that a mesh axis runs over, the one named last changes fastest.
Arguments:
- phonemes: bfloat16 [64, 160, 256], P('dp'), may hold values from -6 to 6
- phone_lengths: int32 [64], P('dp'), may hold values from 80 to 160, as said below
- durations: int32 [64, 160], P('dp'), may hold values from 0 to 95, as said below
- pitch_bins: int32 [64, 1024], P('dp'), may hold values from 0 to 255
- energy_bins: int32 [64, 1024], P('dp'), may hold values from 0 to 255
- joint_weight: bfloat16 [2, 256, 768], P('section'), may hold values from -0.375 to 0.375
- output_weight: bfloat16 [2, 256, 256], P('section'), may hold values from -1.5 to 1.5
- widen_weight: bfloat16 [2, 2304, 1024], P('section'), may hold values from -0.125 to 0.125
- narrow_weight: bfloat16 [2, 1024, 256], P('section'), may hold values from -0.1875 to 0.1875
- block_scales: float32 [2, 2, 256], P('section'), may hold values from 0.25 to 1.75
- block_shifts: float32 [2, 2, 256], P('section'), may hold values from -3 to 3
- predictor_convs: bfloat16 [3, 2, 768, 256], replicated, may hold values from -0.21875 to 0.21875
- predictor_scales: float32 [3, 2, 256], replicated, may hold values from 0.25 to 1.75
- predictor_shifts: float32 [3, 2, 256], replicated, may hold values from -3 to 3
- predictor_outputs: float32 [3, 256], replicated, may hold values from -0.375 to 0.375
- pitch_table: bfloat16 [256, 256], replicated, may hold values from -3 to 3
- energy_table: bfloat16 [256, 256], replicated, may hold values from -3 to 3
- mel_weight: bfloat16 [256, 80], replicated, may hold values from -0.375 to 0.375
- mel_cotangent: bfloat16 [64, 1024, 80], P('dp'), may hold values from -6 to 6
- duration_cotangent: float32 [64, 160], P('dp'), may hold values from -6 to 6
- pitch_cotangent: float32 [64, 1024], P('dp'), may hold values from -6 to 6
- energy_cotangent: float32 [64, 1024], P('dp'), may hold values from -6 to 6
Outputs:
- mel_out: float32 [64, 1024, 80], P('dp', 'section')
- duration_pred: float32 [64, 160], P('dp', 'section')
- pitch_pred: float32 [64, 1024], P('dp', 'section')
- energy_pred: float32 [64, 1024], P('dp', 'section')
- input_grad: float32 [64, 160, 256], P('dp', 'section')
- grad_joint: float32 [2, 256, 768], P('section', 'dp')
- grad_output: float32 [2, 256, 256], P('section', 'dp')
- grad_widen: float32 [2, 2304, 1024], P('section', 'dp')
- grad_narrow: float32 [2, 1024, 256], P('section', 'dp')
- grad_block_scales: float32 [2, 2, 256], P('section', None, 'dp')
- grad_block_shifts: float32 [2, 2, 256], P('section', None, 'dp')
- grad_predictor_convs: float32 [3, 2, 768, 256], P(None, None, None, 'dp')
- grad_predictor_scales: float32 [3, 2, 256], P(None, None, 'dp')
- grad_predictor_shifts: float32 [3, 2, 256], P(None, None, 'dp')
- grad_predictor_outputs: float32 [3, 256], P(None, 'dp')
- grad_pitch_table: float32 [256, 256], P(None, 'dp')
- grad_energy_table: float32 [256, 256], P(None, 'dp')
- grad_mel_weight: float32 [256, 80], P('dp')
The draws below stay inside these ranges and needn't reach their ends.
Inputs may be any that keep to these rules, and one draw needn't show every extreme that they name: `phone_lengths`: some sequence has exactly 160 phonemes. Positions at or past a sequence's phoneme count have duration 0; a sequence's durations sum to 512 to 1024, and those of the sequence with 160 phonemes to exactly 1024; some phoneme of that sequence has the largest duration.
All inputs are finite; a program needn't handle non-finite values.
Results may differ from the reference program's by a relative error of at most 0.02.
Values may be sent and summed in bfloat16 or wider, within the bound.
A program may use at most 384 MiB of HBM per device.

```python
import jax
import jax.numpy as jnp
from jax import lax

D = 256
HEADS = 2
HEAD = 128
FF = 1024
BINS = 256
MELS = 80
KERNEL = 9
PHONES = 160
FRAMES = 1024
SEQS = 64


def lengths_and_durations(key):
    subkeys = jax.random.split(key, 5)
    longest_step = 8 * FRAMES // (PHONES // 2 + 7) + 1
    counts = jax.random.randint(subkeys[0], (SEQS,), PHONES // 2, PHONES + 1)
    frame_totals = jax.random.randint(subkeys[1], (SEQS,), FRAMES // 2, FRAMES + 1)
    longest = jax.random.randint(subkeys[2], (), 0, SEQS)
    chosen = jnp.arange(SEQS) == longest
    counts = jnp.where(chosen, PHONES, counts)
    frame_totals = jnp.where(chosen, FRAMES - longest_step, frame_totals)
    position = jax.random.randint(subkeys[4], (), 0, PHONES)
    marked = chosen[:, None] & (jnp.arange(PHONES)[None, :] == position)
    shares = jax.random.randint(subkeys[3], (SEQS, PHONES), 1, 9)
    shares = shares * (jnp.arange(PHONES)[None, :] < counts[:, None]).astype(shares.dtype)
    shares = jnp.where(marked, 0, shares)
    running = jnp.cumsum(shares, axis=1)
    bounds = frame_totals[:, None] * running // running[:, -1:]
    before = jnp.concatenate([jnp.zeros((SEQS, 1), bounds.dtype), bounds[:, :-1]], axis=1)
    spans = bounds - before + jnp.where(marked, longest_step, 0)
    return (counts.astype(jnp.int32), spans.astype(jnp.int32))


def draw_phone_lengths(key, part):
    shared = lengths_and_durations(key)
    return shared[0]


def draw_durations(key, part):
    shared = lengths_and_durations(key)
    return shared[1]


def touch_ends(drawn, own_key, smallest, top_value):
    index_at = [jax.random.randint(jax.random.fold_in(own_key, axis), (), 0, length) for axis, length in enumerate(drawn.shape)]
    widest = drawn.shape.index(max(drawn.shape))
    beside = index_at[:widest] + [(index_at[widest] + 1) % drawn.shape[widest]] + index_at[widest + 1:]
    return drawn.at[tuple(index_at)].set(smallest).at[tuple(beside)].set(top_value)


def steps_of(own_key, extent, cuts, least, largest):
    loudness = 1.0
    for axis_at, shards_of in cuts:
        steps = jax.random.uniform(jax.random.fold_in(jax.random.fold_in(own_key, 6), axis_at), (shards_of,), jnp.float32, least / len(cuts), largest / len(cuts))
        loudness = loudness * jnp.repeat(jnp.exp(steps), extent[axis_at] // shards_of).reshape((-1,) + (1,) * (len(extent) - 1 - axis_at))
    return loudness


def normal_values(rng, extent, deviation, most, shards=(), kind=jnp.bfloat16):
    entries = jax.random.normal(rng, extent, jnp.float32) * deviation
    if len(shards) > 0:
        entries = steps_of(rng, extent, shards, -0.22, 0.18) * entries
    return jnp.clip(entries, min=-most, max=most).astype(kind)


def setup_inputs(seed: int = 0) -> dict:
    seeds = jax.random.split(jax.random.key(seed), 23)
    phonemes = normal_values(seeds[0], (SEQS, PHONES, D), 1.0, 6.0, ((0, 16),))
    phone_lengths = draw_phone_lengths(jax.random.fold_in(seeds[22], 71), 0)
    durations = draw_durations(jax.random.fold_in(seeds[22], 71), 0)
    pitch_bins = touch_ends(jax.random.randint(seeds[3], (SEQS, FRAMES), 0, BINS), jax.random.fold_in(seeds[3], 1), 0, BINS - 1).astype(jnp.int32)
    energy_bins = touch_ends(jax.random.randint(seeds[4], (SEQS, FRAMES), 0, BINS), jax.random.fold_in(seeds[4], 1), 0, BINS - 1).astype(jnp.int32)
    joint_weight = normal_values(seeds[5], (2, D, 3 * D), D ** -0.5, 0.375, ((0, 2),))
    output_weight = normal_values(seeds[6], (2, D, D), (D // 16) ** -0.5, 1.5, ((0, 2),))
    widen_weight = normal_values(seeds[7], (2, KERNEL * D, FF), (KERNEL * D) ** -0.5, 0.125, ((0, 2),))
    narrow_weight = normal_values(seeds[8], (2, FF, D), FF ** -0.5, 0.1875, ((0, 2),))
    block_scales = jnp.clip(1.0 + 0.15 * jax.random.normal(seeds[9], (2, 2, D), jnp.float32), 0.25, 1.75)
    block_shifts = normal_values(seeds[10], (2, 2, D), 0.3, 3.0, ((0, 2),), jnp.float32)
    predictor_convs = normal_values(seeds[11], (3, 2, 3 * D, D), (3 * D) ** -0.5, 0.21875)
    predictor_scales = jnp.clip(1.0 + 0.15 * jax.random.normal(seeds[12], (3, 2, D), jnp.float32), 0.25, 1.75)
    predictor_shifts = normal_values(seeds[13], (3, 2, D), 0.3, 3.0, (), jnp.float32)
    predictor_outputs = normal_values(seeds[14], (3, D), D ** -0.5, 0.375, (), jnp.float32)
    pitch_table = normal_values(seeds[15], (BINS, D), 0.5, 3.0)
    energy_table = normal_values(seeds[16], (BINS, D), 0.5, 3.0)
    mel_weight = normal_values(seeds[17], (D, MELS), D ** -0.5, 0.375)
    mel_cotangent = normal_values(seeds[18], (SEQS, FRAMES, MELS), 1.0, 6.0, ((0, 16),))
    duration_cotangent = normal_values(seeds[19], (SEQS, PHONES), 1.0, 6.0, ((0, 16),), jnp.float32)
    pitch_cotangent = normal_values(seeds[20], (SEQS, FRAMES), 1.0, 6.0, ((0, 16),), jnp.float32)
    energy_cotangent = normal_values(seeds[21], (SEQS, FRAMES), 1.0, 6.0, ((0, 16),), jnp.float32)
    return {"phonemes": phonemes, "phone_lengths": phone_lengths, "durations": durations, "pitch_bins": pitch_bins, "energy_bins": energy_bins, "joint_weight": joint_weight, "output_weight": output_weight, "widen_weight": widen_weight, "narrow_weight": narrow_weight, "block_scales": block_scales, "block_shifts": block_shifts, "predictor_convs": predictor_convs, "predictor_scales": predictor_scales, "predictor_shifts": predictor_shifts, "predictor_outputs": predictor_outputs, "pitch_table": pitch_table, "energy_table": energy_table, "mel_weight": mel_weight, "mel_cotangent": mel_cotangent, "duration_cotangent": duration_cotangent, "pitch_cotangent": pitch_cotangent, "energy_cotangent": energy_cotangent}


@jax.custom_vjp
def low(v):
    return lax.optimization_barrier(v.astype(jnp.bfloat16)).astype(jnp.float32)

@jax.custom_vjp
def low_back(v):
    return v

def low_keep(v):
    return (low(v), None)

def low_pass(kept, grad):
    return (grad,)

def back_keep(v):
    return (v, None)

def back_low(kept, grad):
    return (low(grad),)
low.defvjp(low_keep, low_pass)
low_back.defvjp(back_keep, back_low)
highest = lax.Precision.HIGHEST
norm_eps = 1e-05

def matmul(left_side, right_side):
    return jnp.dot(left_side, right_side, precision=highest, preferred_element_type=jnp.float32)

def both_ways(values):
    return low_back(low(values))

def layer_norm(values, scale_row, shift_row):
    average = lax.optimization_barrier(jnp.mean(values, axis=-1, keepdims=True))
    centred = values - average
    variance = lax.optimization_barrier(jnp.mean(centred * centred, axis=-1, keepdims=True))
    return centred * lax.rsqrt(variance + norm_eps) * scale_row + shift_row

def unfold(values, kernel_width):
    length = values.shape[0]
    margin = kernel_width // 2
    padded = jnp.pad(values, ((margin, margin), (0, 0)))
    return jnp.concatenate([padded[offset:offset + length] for offset in range(kernel_width)], axis=1)

def fft_block(hidden, keep_mask, joint_matrix, output_matrix, widen_matrix, narrow_matrix, scale_pair, shift_pair):
    length = hidden.shape[0]
    joint_proj = both_ways(matmul(low(hidden), joint_matrix))
    query_heads = joint_proj[:, :D].reshape(length, HEADS, HEAD)
    key_heads = joint_proj[:, D:2 * D].reshape(length, HEADS, HEAD)
    value_heads = joint_proj[:, 2 * D:].reshape(length, HEADS, HEAD)
    penalty = jnp.where(keep_mask > 0.5, 0.0, -1000000000.0)
    scores = jnp.einsum('qhd,khd->hqk', query_heads, key_heads, precision=highest) * HEAD ** (-0.5) + penalty[None, None, :]
    scores = low_back(scores)
    weights = jax.nn.softmax(scores, axis=-1)
    mixed_heads = jnp.einsum('hqk,khd->qhd', low(weights), value_heads, precision=highest).reshape(length, D)
    mixed_heads = both_ways(mixed_heads)
    attended = low_back(matmul(mixed_heads, output_matrix))
    first_out = layer_norm(hidden + attended, scale_pair[0], shift_pair[0]) * keep_mask[:, None]
    widened = low_back(matmul(unfold(low(first_out), KERNEL), widen_matrix))
    activated = low(jax.nn.gelu(widened))
    narrowed = low_back(matmul(activated, narrow_matrix))
    return layer_norm(first_out + narrowed, scale_pair[1], shift_pair[1]) * keep_mask[:, None]

def predictor(hidden, keep_mask, conv_pair, scale_pair, shift_pair, readout):
    before_a = low_back(matmul(unfold(low(hidden), 3), conv_pair[0]))
    after_a = layer_norm(jax.nn.gelu(before_a), scale_pair[0], shift_pair[0]) * keep_mask[:, None]
    before_b = low_back(matmul(unfold(low(after_a), 3), conv_pair[1]))
    after_b = layer_norm(jax.nn.gelu(before_b), scale_pair[1], shift_pair[1])
    return matmul(after_b, readout) * keep_mask

def regulate_matrix(duration_row):
    end_points = jnp.cumsum(duration_row)
    starts = end_points - duration_row
    frame_index = jnp.arange(FRAMES, dtype=jnp.int32)
    inside = (frame_index[:, None] >= starts[None, :]) & (frame_index[:, None] < end_points[None, :])
    return inside.astype(jnp.float32)

def sequence_forward(phoneme_values, params, count_value, duration_row, pitch_row, energy_row):
    joint_sets, output_sets, widen_sets, narrow_sets, block_scale_sets, block_shift_sets, conv_sets, scale_sets, shift_sets, readout_sets, pitch_values, energy_values, mel_values = params
    keep_phones = (jnp.arange(PHONES, dtype=jnp.int32) < count_value).astype(jnp.float32)
    expand = regulate_matrix(duration_row)
    keep_frames = lax.optimization_barrier(jnp.sum(expand, axis=1))
    encoded = fft_block(phoneme_values, keep_phones, joint_sets[0], output_sets[0], widen_sets[0], narrow_sets[0], block_scale_sets[0], block_shift_sets[0])
    duration_estimate = predictor(encoded, keep_phones, conv_sets[0], scale_sets[0], shift_sets[0], readout_sets[0])
    frames = matmul(expand, encoded)
    pitch_estimate = predictor(frames, keep_frames, conv_sets[1], scale_sets[1], shift_sets[1], readout_sets[1])
    frames = frames + jnp.take(pitch_values, pitch_row, axis=0) * keep_frames[:, None]
    energy_estimate = predictor(frames, keep_frames, conv_sets[2], scale_sets[2], shift_sets[2], readout_sets[2])
    frames = frames + jnp.take(energy_values, energy_row, axis=0) * keep_frames[:, None]
    decoded = fft_block(both_ways(frames), keep_frames, joint_sets[1], output_sets[1], widen_sets[1], narrow_sets[1], block_scale_sets[1], block_shift_sets[1])
    spectrum = matmul(low(decoded), mel_values)
    return (spectrum, duration_estimate, pitch_estimate, energy_estimate)

def reference(phonemes, phone_lengths, durations, pitch_bins, energy_bins, joint_weight, output_weight, widen_weight, narrow_weight, block_scales, block_shifts, predictor_convs, predictor_scales, predictor_shifts, predictor_outputs, pitch_table, energy_table, mel_weight, mel_cotangent, duration_cotangent, pitch_cotangent, energy_cotangent):
    weights = tuple((weight_item.astype(jnp.float32) for weight_item in (joint_weight, output_weight, widen_weight, narrow_weight, block_scales, block_shifts, predictor_convs, predictor_scales, predictor_shifts, predictor_outputs, pitch_table, energy_table, mel_weight)))

    def one_sequence(totals, inputs):
        phoneme_row, count_value, duration_row, pitch_row, energy_row, mel_grad_row, duration_grad_row, pitch_grad_row, energy_grad_row = inputs

        def forward(phoneme_values, *params):
            return sequence_forward(phoneme_values, params, count_value, duration_row, pitch_row, energy_row)
        outputs, pullback = jax.vjp(forward, phoneme_row.astype(jnp.float32), *weights)
        gradients = pullback((mel_grad_row.astype(jnp.float32), duration_grad_row, pitch_grad_row, energy_grad_row))
        totals = jax.tree.map(jnp.add, totals, tuple(gradients[1:]))
        return (totals, (outputs[0], outputs[1], outputs[2], outputs[3], gradients[0]))
    initial = tuple((jnp.zeros(weight_item.shape, jnp.float32) for weight_item in weights))
    totals, stacked = lax.scan(one_sequence, initial, (phonemes, phone_lengths, durations, pitch_bins, energy_bins, mel_cotangent, duration_cotangent, pitch_cotangent, energy_cotangent))
    return (stacked[0], stacked[1], stacked[2], stacked[3], stacked[4], totals[0], totals[1], totals[2], totals[3], totals[4], totals[5], totals[6], totals[7], totals[8], totals[9], totals[10], totals[11], totals[12])
```

```python
import functools
import math

import jax
import jax.numpy as jnp
from jax import lax
from jax.experimental import pallas as pl
from jax.experimental.pallas import tpu as pltpu
from jax.sharding import PartitionSpec as P

D = 256
HEAD = 128
FF = 1024
BINS = 256
MELS = 80
TAPS = 9
PHONES = 160
FRAMES = 1024
SLOT = 192
WIDE = TAPS * D
EPS = 1e-5
AT_TABLES = 6 * 3 * D
AT_MEL = AT_TABLES + 2 * BINS
AT_VECTORS = AT_MEL + 128
PACK = AT_VECTORS + 128
C1 = math.sqrt(2.0 / math.pi)
C2 = C1 * 0.044715
SCALE = HEAD**-0.5
LOG2E = math.log2(math.e)
F32 = jnp.float32
BF16 = jnp.bfloat16


def dot(a, b):
    return jnp.dot(a, b, preferred_element_type=F32)


def dot_nt(a, b):
    return lax.dot_general(a, b, (((1,), (1,)), ((), ())), preferred_element_type=F32)


def dot_tn(a, b):
    return lax.dot_general(a, b, (((0,), (0,)), ((), ())), preferred_element_type=F32)


def iota(shape, dim):
    return lax.broadcasted_iota(jnp.int32, shape, dim)


def gelu_pair(x):
    x2 = x * x
    h = 0.5 + 0.5 * jnp.tanh(x * (C1 + C2 * x2))
    value = x * h
    slope = h + value * (1.0 - h) * (2.0 * C1 + 6.0 * C2 * x2)
    return value, slope


def normed(r):
    mean = jnp.mean(r, axis=-1, keepdims=True)
    centred = r - mean
    rstd = lax.rsqrt(jnp.mean(centred * centred, axis=-1, keepdims=True) + EPS)
    return centred * rstd, rstd


def norm_back(t, n, rstd):
    return (
        t - jnp.mean(t, axis=-1, keepdims=True) - n * jnp.mean(t * n, axis=-1, keepdims=True)
    ) * rstd


def column_sum(x):
    return jnp.sum(x, axis=0, keepdims=True)


def aligned(i, size):
    return pl.ds(pl.multiple_of(i * size, size), size)


def each(count, body):
    def step(i, carry):
        body(i)
        return carry

    lax.fori_loop(0, count, step, 0)


class Layout:
    def __init__(self, segments, span, query):
        self.segments, self.span, self.query = segments, span, query
        self.rows = segments * span
        self.fewest = span // 2


ENC = Layout(4, SLOT, SLOT)
DEC = Layout(1, FRAMES, 256)
T = 256
LENGTHS = ((FRAMES, 0),)


def pieces(length, size):
    return [(at, min(size, length - at)) for at in range(0, length, size)]


def block_scratch(layout, backward):
    L, S, n = layout.rows, layout.span, layout.segments
    shapes = dict(
        h_lo=pltpu.VMEM((L, D), BF16),
        joint=pltpu.VMEM((L, 3 * D), BF16),
        jointT=pltpu.VMEM((n, 3 * D, S), BF16),
        mixedT=pltpu.VMEM((n, D, S), BF16),
        first=pltpu.VMEM((L + 16, D), F32),
        cols=pltpu.VMEM((L, WIDE), BF16),
        slope=pltpu.VMEM((L, FF), F32),
        wide=pltpu.VMEM((2, T, D), F32),
        second=pltpu.VMEM((L, D), F32),
        widen=pltpu.VMEM((WIDE, FF), BF16),
        narrow=pltpu.VMEM((FF, D), BF16),
        sem=pltpu.SemaphoreType.DMA((6,)),
    )
    if backward:
        shapes.update(
            expo=pltpu.VMEM((n, 2, S, S), BF16),
            rinv=pltpu.VMEM((n, 2, 8, S), F32),
            n1=pltpu.VMEM((L, D), F32),
            r1=pltpu.VMEM((L, 1), F32),
            act=pltpu.VMEM((L, FF), BF16),
            spare=pltpu.VMEM((WIDE - 2 * L, FF), BF16),
            dnar=pltpu.VMEM((max(L, FF), D), BF16),
            dwid=pltpu.VMEM((L, FF), BF16),
            dcols=pltpu.VMEM((T + 32, WIDE), F32),
            dfirst=pltpu.VMEM((L + 16, D), F32),
            datt=pltpu.VMEM((L, D), BF16),
            dmixT=pltpu.VMEM((n, D, S), BF16),
            inner=pltpu.VMEM((n, 2, 8, S), F32),
            djointT=pltpu.VMEM((n, 3 * D, S), BF16),
            a_joint=pltpu.VMEM((3 * D, D), F32),
            a_output=pltpu.VMEM((D, D), F32),
            a_widen=pltpu.VMEM((WIDE, FF), F32),
            a_narrow=pltpu.VMEM((FF, D), F32),
            a_vec=pltpu.VMEM((8, D), F32),
        )
    return shapes


def start_block(layout, b):
    edge = jnp.zeros((8, D), F32)
    b.first[0:8, :] = edge
    b.first[layout.rows + 8 : layout.rows + 16, :] = edge


def zero_accumulators(b):
    b.a_joint[...] = jnp.zeros_like(b.a_joint)
    b.a_output[...] = jnp.zeros_like(b.a_output)
    b.a_narrow[...] = jnp.zeros_like(b.a_narrow)
    b.a_vec[...] = jnp.zeros_like(b.a_vec)

    def body(t, _):
        b.a_widen[aligned(t, D), :] = jnp.zeros((D, FF), F32)
        return 0

    lax.fori_loop(0, TAPS, body, 0)
    edge = jnp.zeros((16, WIDE), F32)
    b.dcols[0:16, :] = edge


def heads(h):
    return tuple(slice(k * D + h * HEAD, k * D + (h + 1) * HEAD) for k in range(3))


def attention_forward(layout, b, w, counts, length):
    S, save = layout.span, hasattr(b, "expo")
    blocks = [(s, at, q) for s in range(layout.segments) for at, q in pieces(length, layout.query)]
    for s, at, q in blocks:
        rows = slice(s * S + at, s * S + at + q)
        value = dot(b.h_lo[rows, :], w.joint[...]).astype(BF16)
        b.joint[rows, :] = value
        b.jointT[s, :, at : at + q] = value.T
    chunks = pieces(length, D)
    items = [block + (h,) for block in blocks for h in range(2)]

    def score(i):
        s, at, q, h = items[i]
        query_at, key_at, _ = heads(h)
        side = slice((i % 2) * D, (i % 2) * D + q)
        top = None
        for c, size in chunks:
            scores = dot(
                b.joint[s * S + c : s * S + c + size, key_at], b.jointT[s, query_at, at : at + q]
            )
            if c + size > layout.fewest:
                scores = jnp.where(iota((size, q), 0) + c < counts[s], scores, -1e30)
            b.slope[c : c + size, side] = scores
            part = jnp.max(scores.reshape(size // 8, 8, q), axis=0)
            top = part if top is None else jnp.maximum(top, part)
        return jnp.max(top, axis=0, keepdims=True)

    tops = {0: score(0)}
    for i, (s, at, q, h) in enumerate(items):
        if i + 1 < len(items):
            tops[i + 1] = score(i + 1)
        query_at, _, value_at = heads(h)
        side = slice((i % 2) * D, (i % 2) * D + q)
        sums = mixed = None
        for c, size in chunks:
            expo = jnp.exp2((b.slope[c : c + size, side] - tops[i]) * (SCALE * LOG2E))
            part = jnp.sum(expo.reshape(size // 8, 8, q), axis=0)
            sums = part if sums is None else sums + part
            expo = expo.astype(BF16)
            if save:
                b.expo[s, h, c : c + size, at : at + q] = expo
            part = dot(b.jointT[s, value_at, c : c + size], expo)
            mixed = part if mixed is None else mixed + part
        rinv = 1.0 / column_sum(sums)
        b.mixedT[s, query_at, at : at + q] = (mixed * rinv).astype(BF16)
        if save:
            b.rinv[s, h, :, at : at + q] = jnp.broadcast_to(rinv, (8, q))
    for s, at, q in blocks:
        r0 = s * S + at
        attended = dot_tn(b.mixedT[s, :, at : at + q], w.output[...])
        n, rstd = normed(b.h_lo[r0 : r0 + q, :].astype(F32) + attended)
        keep = (iota((q, 1), 0) + at < counts[s]).astype(F32)
        b.first[r0 + 8 : r0 + 8 + q, :] = (n * w.scales[0:1, :] + w.shifts[0:1, :]) * keep
        if save:
            b.n1[r0 : r0 + q, :] = n
            b.r1[r0 : r0 + q, :] = rstd


def ffn_forward(b, w, length):
    save = hasattr(b, "expo")
    tiles = pieces(length, T)
    items = [(k, j) for k in range(len(tiles)) for j in range(4)]

    def unfold(k):
        r0, size = tiles[k]
        v = b.first[r0 : r0 + size + 16, :]
        for t in range(TAPS):
            b.cols[r0 : r0 + size, t * D : (t + 1) * D] = v[4 + t : 4 + t + size].astype(BF16)

    def widen(i):
        k, j = items[i]
        r0, size = tiles[k]
        b.wide[i % 2, 0:size, :] = dot(b.cols[r0 : r0 + size, :], b.widen[:, j * D : (j + 1) * D])

    unfold(0)
    widen(0)
    for i, (k, j) in enumerate(items):
        if j == 1 and k + 1 < len(tiles):
            unfold(k + 1)
        if i + 1 < len(items):
            widen(i + 1)
        r0, size = tiles[k]
        rows, at = slice(r0, r0 + size), slice(j * D, (j + 1) * D)
        value, slope = gelu_pair(b.wide[i % 2, 0:size, :])
        value = value.astype(BF16)
        if save:
            b.act[rows, at] = value
            b.slope[rows, at] = slope
        narrowed = dot(value, b.narrow[at, :])
        before = b.second[rows, :] if j else b.first[r0 + 8 : r0 + 8 + size, :]
        b.second[rows, :] = before + narrowed


def ffn_backward(b, w, length):
    b.dfirst[0 : length + 16, :] = jnp.zeros((length + 16, D), F32)
    for r0, size in pieces(length, T):
        rows = slice(r0, r0 + size)
        b.dcols[16 + size : 32 + size, :] = jnp.zeros((16, WIDE), F32)
        for j in range(4):
            at = slice(j * D, (j + 1) * D)
            b.dwid[rows, at] = (
                dot_nt(b.dnar[rows, :], b.narrow[at, :]) * b.slope[rows, at]
            ).astype(BF16)
        for t in range(TAPS):
            at = slice(t * D, (t + 1) * D)
            b.dcols[16 : 16 + size, at] = dot_nt(b.dwid[rows, :], b.widen[at, :])
        total = b.dcols[12 : 28 + size, 0:D]
        for t in range(1, TAPS):
            total = total + b.dcols[12 - t : 28 - t + size, t * D : (t + 1) * D]
        b.dfirst[r0 : r0 + size + 16, :] += total
        b.dfirst[r0 + 8 : r0 + 8 + size, :] += b.second[rows, :]


def ffn_weight_grads(b, length):
    def widen(t, _):
        at = aligned(t, 3 * D)
        b.a_widen[at, :] += dot_tn(b.cols[0:length, at], b.dwid[0:length, :])
        return 0

    lax.fori_loop(0, 3, widen, 0)
    b.a_narrow[...] += dot_tn(b.act[0:length, :], b.dnar[0:length, :])


def attention_backward(layout, b, w, counts, length, finish):
    S = layout.span
    blocks = [(s, at, q) for s in range(layout.segments) for at, q in pieces(length, layout.query)]
    chunks = pieces(length, D)
    for s, at, q in blocks:
        r0 = s * S + at
        rows, pad_rows, lanes = slice(r0, r0 + q), slice(r0 + 8, r0 + 8 + q), slice(at, at + q)
        keep = (iota((q, 1), 0) + at < counts[s]).astype(F32)
        dy = b.dfirst[pad_rows, :] * keep
        n = b.n1[rows, :]
        b.a_vec[0:1, :] += column_sum(dy * n)
        b.a_vec[1:2, :] += column_sum(dy)
        dsum = norm_back(dy * w.scales[0:1, :], n, b.r1[rows, :])
        b.dfirst[pad_rows, :] = dsum
        datt = dsum.astype(BF16)
        b.datt[rows, :] = datt
        dmix = dot_nt(w.output[...], datt)
        for h in range(2):
            head = heads(h)[0]
            part = (dmix[head, :] * b.rinv[s, h, 0:1, lanes]).astype(BF16)
            b.dmixT[s, head, lanes] = part
            inner = column_sum(part.astype(F32) * b.mixedT[s, head, lanes].astype(F32))
            b.inner[s, h, :, lanes] = jnp.broadcast_to(inner, (8, q))
    items = [block + (h,) for block in blocks for h in range(2)]

    def score(i):
        s, at, q, h = items[i]
        side = slice((i % 2) * D, (i % 2) * D + q)
        b.slope[0:length, side] = dot(
            b.joint[s * S : s * S + length, heads(h)[2]], b.dmixT[s, heads(h)[0], at : at + q]
        )

    score(0)
    for i, (s, at, q, h) in enumerate(items):
        if i + 1 < len(items):
            score(i + 1)
        query_at, key_at, _ = heads(h)
        lanes, side = slice(at, at + q), slice((i % 2) * D, (i % 2) * D + q)
        dquery = None
        for c, size in chunks:
            expo = b.expo[s, h, c : c + size, lanes].astype(F32)
            ds = expo * (b.slope[c : c + size, side] - b.inner[s, h, 0:1, lanes])
            ds = ds.astype(BF16)
            part = dot(b.jointT[s, key_at, c : c + size], ds)
            dquery = part if dquery is None else dquery + part
            b.cols[s * S + at : s * S + at + q, h * FRAMES + c : h * FRAMES + c + size] = ds.T
        b.djointT[s, query_at, lanes] = (dquery * SCALE).astype(BF16)
    for s in range(layout.segments):
        rows = slice(s * S, s * S + length)
        for h in range(2):
            query_at, key_at, value_at = heads(h)
            for c, size in chunks:
                lanes = slice(c, c + size)
                dkey = dot(
                    b.jointT[s, query_at, 0:length],
                    b.cols[rows, h * FRAMES + c : h * FRAMES + c + size],
                )
                b.djointT[s, key_at, lanes] = (dkey * SCALE).astype(BF16)
                dvalue = dot_nt(b.dmixT[s, query_at, 0:length], b.expo[s, h, lanes, 0:length])
                b.djointT[s, value_at, lanes] = dvalue.astype(BF16)
        b.a_output[...] += dot(b.mixedT[s, :, 0:length], b.datt[rows, :])
        b.a_joint[...] += dot(b.djointT[s, :, 0:length], b.h_lo[rows, :])
    for s, at, q in blocks:
        dh = dot_tn(b.djointT[s, :, at : at + q], w.jointT[...])
        finish(s, at, q, dh + b.dfirst[s * S + at + 8 : s * S + at + 8 + q, :])


def second_norm_back(b, w, r0, size, dy, n, rstd):
    b.a_vec[2:3, :] += column_sum(dy * n)
    b.a_vec[3:4, :] += column_sum(dy)
    dsecond = norm_back(dy * w.scales[1:2, :], n, rstd)
    b.second[r0 : r0 + size, :] = dsecond
    b.dnar[r0 : r0 + size, :] = dsecond.astype(BF16)


class Refs:
    def __init__(self, names, refs):
        for name, ref in zip(names, refs):
            setattr(self, name, ref)


WEIGHTS = ("joint", "jointT", "output", "widen_far", "narrow_far", "scales", "shifts")
FAR = ("w_widen_far", "w_narrow_far", "g_widen", "g_narrow")


def send_large_grads(b, o):
    b.dnar[0:FF, :] = b.a_narrow[...].astype(BF16)
    pltpu.make_async_copy(b.dnar.at[pl.ds(0, FF)], o.g_narrow, b.sem.at[2]).start()
    at = 0
    for k, (buffer, size) in enumerate(large_parts(b)):
        buffer[0:size, :] = b.a_widen[at : at + size, :].astype(BF16)
        pltpu.make_async_copy(
            buffer.at[pl.ds(0, size)], o.g_widen.at[pl.ds(at, size)], b.sem.at[3 + k]
        ).start()
        at += size


def large_parts(b):
    size = b.act.shape[0]
    left = WIDE - 2 * size
    return ((b.act, size), (b.dwid, size), (b.spare, left))


def store_block_grads(b, o):
    o.g_joint[...] = b.a_joint[...].T.astype(BF16)
    o.g_output[...] = b.a_output[...].astype(BF16)
    rows = jnp.concatenate([b.a_vec[...], jnp.zeros((120, D), F32)], axis=0)
    o.g_vec[...] = rows.T.astype(BF16)
    pltpu.make_async_copy(b.dnar.at[pl.ds(0, FF)], o.g_narrow, b.sem.at[2]).wait()
    at = 0
    for k, (buffer, size) in enumerate(large_parts(b)):
        pltpu.make_async_copy(
            buffer.at[pl.ds(0, size)], o.g_widen.at[pl.ds(at, size)], b.sem.at[3 + k]
        ).wait()
        at += size


def start_weights(b, w):
    pltpu.make_async_copy(w.widen_far, b.widen, b.sem.at[0]).start()
    pltpu.make_async_copy(w.narrow_far, b.narrow, b.sem.at[1]).start()


def wait_weights(b, w):
    pltpu.make_async_copy(w.widen_far, b.widen, b.sem.at[0]).wait()
    pltpu.make_async_copy(w.narrow_far, b.narrow, b.sem.at[1]).wait()


GRADS = (
    ("g_joint", (D, 3 * D), BF16),
    ("g_output", (D, D), BF16),
    ("g_widen", (WIDE, FF), BF16),
    ("g_narrow", (FF, D), BF16),
    ("g_vec", (D, 128), BF16),
)


def expansion(start, stop, first_row, size):
    row = iota((size, 256), 0) + first_row
    return ((row >= start) & (row < stop)).astype(F32).astype(BF16)


def hot_columns(bins, count, first_lane, size):
    live = iota((1, size), 1) + first_lane < count
    return ((iota((BINS, size), 0) == bins) & live).astype(F32).astype(BF16)


def span_ends(durations):
    upper = (iota((256, 256), 0) <= iota((256, 256), 1)).astype(F32).astype(BF16)
    return dot(durations.astype(F32).astype(BF16), upper).astype(jnp.int32)


def decoder_kernel(sequences, names, *refs):
    r = Refs(names, refs)
    b, w, o = r, Refs(WEIGHTS, [getattr(r, "w_" + n) for n in WEIGHTS]), r
    layout = DEC
    start_weights(b, w)
    zero_accumulators(b)
    start_block(layout, b)
    r.a_mel[...] = jnp.zeros_like(r.a_mel)
    r.a_table[...] = jnp.zeros_like(r.a_table)
    r.durations_pad[...] = jnp.zeros_like(r.durations_pad)
    r.durations_pad[0:sequences, 0:PHONES] = r.durations[...]
    stop = span_ends(r.durations_pad[...])
    r.stop[...] = stop
    r.start[...] = stop - r.durations_pad[...]
    r.encoded_pad[...] = jnp.zeros_like(r.encoded_pad)

    def sequence(s, length):
        count = r.frames[s]
        counts = [count]
        r.encoded_pad[0:PHONES, :] = r.encoded[s]
        start, stop = r.start[pl.ds(s, 1), :], r.stop[pl.ds(s, 1), :]
        tiles = pieces(length, T)
        for r0, size in tiles:
            rows = slice(r0, r0 + size)
            expand = expansion(start, stop, r0, size)
            r.expand[rows, :] = expand
            hot_p = hot_columns(r.pitch_bins[pl.ds(s, 1), rows], count, r0, size)
            hot_e = hot_columns(r.energy_bins[pl.ds(s, 1), rows], count, r0, size)
            r.hot[0:BINS, rows] = hot_p
            r.hot[BINS:, rows] = hot_e
            adapted = dot(expand, r.encoded_pad[...])
            adapted = adapted + dot_tn(hot_p, r.pitch_table[...])
            adapted = adapted + dot_tn(hot_e, r.energy_table[...])
            b.h_lo[rows, :] = adapted.astype(BF16)
        attention_forward(layout, b, w, counts, length)
        b.first[length + 8 : length + 16, :] = jnp.zeros((8, D), F32)
        pl.when(s == 0)(lambda: wait_weights(b, w))
        ffn_forward(b, w, length)
        for r0, size in tiles:
            rows = slice(r0, r0 + size)
            n, rstd = normed(b.second[rows, :])
            keep = (iota((size, 1), 0) + r0 < count).astype(F32)
            decoded = ((n * w.scales[1:2, :] + w.shifts[1:2, :]) * keep).astype(BF16)
            o.mel[s, rows, :] = dot(decoded, r.mel_weight[...])
            cotangent = r.mel_cotangent[s, rows, :]
            r.a_mel[...] += dot_tn(decoded, cotangent)
            dy = dot_nt(cotangent, r.mel_weight[...]) * keep
            second_norm_back(b, w, r0, size, dy, n, rstd)
        if length < FRAMES:
            o.mel[s, length:, :] = jnp.zeros((FRAMES - length, MELS), F32)
        ffn_backward(b, w, length)
        ffn_weight_grads(b, length)
        pl.when(s == sequences - 1)(lambda: send_large_grads(b, o))

        def finish(_, at, q, dh):
            b.datt[at : at + q, :] = dh.astype(BF16)

        attention_backward(layout, b, w, counts, length, finish)
        dadapted = b.datt[0:length, :]
        r.a_table[...] += dot(r.hot[:, 0:length], dadapted)
        o.dencoded[s] = dot_tn(r.expand[0:length, :], dadapted)[0:PHONES]

    def one(s, _):
        count = r.frames[s]
        for length, before in LENGTHS:
            chosen = ((count > before) & (count <= length)).astype(jnp.int32)
            each(chosen, lambda _: sequence(s, length))
        return 0

    lax.fori_loop(0, sequences, one, 0)
    store_block_grads(b, o)
    r.pack[:, 0:AT_TABLES] = jnp.zeros((D, AT_TABLES), BF16)
    r.pack[:, AT_TABLES:AT_MEL] = r.a_table[...].T.astype(BF16)
    r.pack[:, AT_MEL:] = jnp.zeros((D, PACK - AT_MEL), BF16)
    r.pack[:, AT_MEL : AT_MEL + MELS] = r.a_mel[...].astype(BF16)


def build(kernel, name, inputs, outputs, scratch, smem=()):
    names = [n for n, _ in inputs] + [n for n, _, _ in outputs] + list(scratch)

    def place(n):
        space = pltpu.SMEM if n in smem else pl.ANY if n in FAR else pltpu.VMEM
        return pl.BlockSpec(memory_space=space)

    return pl.pallas_call(
        functools.partial(kernel, names),
        name=name,
        in_specs=[place(n) for n, _ in inputs],
        out_specs=[place(n) for n, _, _ in outputs],
        out_shape=[jax.ShapeDtypeStruct(shape, kind) for _, shape, kind in outputs],
        scratch_shapes=list(scratch.values()),
        compiler_params=pltpu.CompilerParams(vmem_limit_bytes=60 * 2**20),
    )(*[a for _, a in inputs])


def weight_inputs(weights):
    return [("w_" + n, a) for n, a in zip(WEIGHTS, weights)]


def decoder(encoded, durations, frames, pitch_bins, energy_bins, weights, pitch_table,
            energy_table, mel_weight, mel_cotangent):
    sequences = encoded.shape[0]
    scratch = dict(
        block_scratch(DEC, True),
        a_mel=pltpu.VMEM((D, MELS), F32),
        a_table=pltpu.VMEM((2 * BINS, D), F32),
        durations_pad=pltpu.VMEM((8, 256), jnp.int32),
        start=pltpu.VMEM((8, 256), jnp.int32),
        stop=pltpu.VMEM((8, 256), jnp.int32),
        encoded_pad=pltpu.VMEM((256, D), BF16),
        expand=pltpu.VMEM((FRAMES, 256), BF16),
        hot=pltpu.VMEM((2 * BINS, FRAMES), BF16),
    )
    return build(
        functools.partial(decoder_kernel, sequences),
        "decoder",
        [
            ("frames", frames),
            ("encoded", encoded),
            ("durations", durations),
            ("pitch_bins", pitch_bins),
            ("energy_bins", energy_bins),
            *weight_inputs(weights),
            ("pitch_table", pitch_table),
            ("energy_table", energy_table),
            ("mel_weight", mel_weight),
            ("mel_cotangent", mel_cotangent),
        ],
        [
            ("mel", (sequences, FRAMES, MELS), F32),
            ("dencoded", (sequences, PHONES, D), F32),
            *GRADS,
            ("pack", (D, PACK), BF16),
        ],
        scratch,
        smem=("frames",),
    )


def load_segments(b, phonemes):
    b.h_lo[...] = jnp.zeros_like(b.h_lo)
    for s in range(ENC.segments):
        b.h_lo[s * SLOT : s * SLOT + PHONES, :] = phonemes[s]


def slot_keep(counts, r0, size):
    row = iota((size, 1), 0) + r0
    kept = row < counts[0]
    for s in range(1, ENC.segments):
        kept = kept | ((row >= s * SLOT) & (row < s * SLOT + counts[s]))
    return kept.astype(F32)


def encoder_forward_kernel(names, *refs):
    r = Refs(names, refs)
    b, w = r, Refs(WEIGHTS, [getattr(r, "w_" + n) for n in WEIGHTS])
    start_weights(b, w)
    counts = [r.counts[s] for s in range(ENC.segments)]
    start_block(ENC, b)
    load_segments(b, r.phonemes)
    attention_forward(ENC, b, w, counts, SLOT)
    wait_weights(b, w)
    ffn_forward(b, w, ENC.rows)
    for r0, size in pieces(ENC.rows, T):
        n, _ = normed(b.second[r0 : r0 + size, :])
        encoded = (n * w.scales[1:2, :] + w.shifts[1:2, :]) * slot_keep(counts, r0, size)
        b.second[r0 : r0 + size, :] = encoded
    for s in range(ENC.segments):
        encoded = b.second[s * SLOT : s * SLOT + PHONES, :]
        r.encoded[s] = encoded
        r.encoded_lo[s] = encoded.astype(BF16)


def encoder_backward_kernel(names, *refs):
    r = Refs(names, refs)
    b, w, o = r, Refs(WEIGHTS, [getattr(r, "w_" + n) for n in WEIGHTS]), r
    start_weights(b, w)
    counts = [r.counts[s] for s in range(ENC.segments)]
    zero_accumulators(b)
    start_block(ENC, b)
    load_segments(b, r.phonemes)
    attention_forward(ENC, b, w, counts, SLOT)
    wait_weights(b, w)
    ffn_forward(b, w, ENC.rows)
    b.n1_grad[...] = jnp.zeros_like(b.n1_grad)
    for s in range(ENC.segments):
        b.n1_grad[s * SLOT : s * SLOT + PHONES, :] = r.grad_near[s] + r.grad_far[s].astype(F32)
    for r0, size in pieces(ENC.rows, T):
        n, rstd = normed(b.second[r0 : r0 + size, :])
        dy = b.n1_grad[r0 : r0 + size, :] * slot_keep(counts, r0, size)
        second_norm_back(b, w, r0, size, dy, n, rstd)
    ffn_backward(b, w, ENC.rows)
    ffn_weight_grads(b, ENC.rows)
    send_large_grads(b, o)

    def finish(s, at, q, dh):
        o.grad_input[s] = dh[0:PHONES]

    attention_backward(ENC, b, w, counts, SLOT, finish)
    store_block_grads(b, o)


def encoder_forward(phonemes, counts, weights):
    n = phonemes.shape[0]
    return build(
        encoder_forward_kernel,
        "encoder_forward",
        [("counts", counts), ("phonemes", phonemes), *weight_inputs(weights)],
        [("encoded", (n, PHONES, D), F32), ("encoded_lo", (n, PHONES, D), BF16)],
        block_scratch(ENC, False),
        smem=("counts",),
    )


def encoder_backward(phonemes, counts, weights, grad_near, grad_far):
    n = phonemes.shape[0]
    return build(
        encoder_backward_kernel,
        "encoder_backward",
        [
            ("counts", counts),
            ("phonemes", phonemes),
            *weight_inputs(weights),
            ("grad_near", grad_near),
            ("grad_far", grad_far),
        ],
        [("grad_input", (n, PHONES, D), F32), *GRADS],
        dict(block_scratch(ENC, True), n1_grad=pltpu.VMEM((ENC.rows, D), F32)),
        smem=("counts",),
    )


def halves(x):
    high = x.astype(BF16)
    return high, (x - high.astype(F32)).astype(BF16)


def predict(r, p, rows, keep, keep_row, hidden, cotangent, estimate):
    tiles = pieces(rows, T)
    conv_a, conv_b = r.convs.at[p, 0], r.convs.at[p, 1]
    scale_a, scale_b = r.scales[p, 0:1, :], r.scales[p, 1:2, :]
    shift_a, shift_b = r.shifts[p, 0:1, :], r.shifts[p, 1:2, :]
    readout = r.readouts[pl.ds(p, 1), :]
    edge = jnp.zeros((8, D), F32)
    r.after[0:8, :] = edge
    r.after[rows + 8 : rows + 16, :] = edge

    def unfold(source, target, r0, size):
        v = source[r0 : r0 + size + 16, :]
        for t in range(3):
            target[r0 : r0 + size, t * D : (t + 1) * D] = v[7 + t : 7 + t + size].astype(BF16)

    def fold(target, gradient, conv, r0, size):
        r.dcols3[16 : 16 + size, :] = dot_nt(gradient, conv[...])
        r.dcols3[16 + size : 32 + size, :] = jnp.zeros((16, 3 * D), F32)
        total = r.dcols3[9 : 25 + size, 0:D]
        for t in range(1, 3):
            total = total + r.dcols3[9 - t : 25 - t + size, t * D : (t + 1) * D]
        target[r0 : r0 + size + 16, :] += total

    for r0, size in tiles:
        at = slice(r0, r0 + size)
        unfold(hidden, r.cols_a, r0, size)
        value, slope = gelu_pair(dot(r.cols_a[at, :], conv_a[...]))
        n, rstd = normed(value)
        r.slope_a[at, :] = slope
        r.norm_a[at, :] = n
        r.rstd_a[at, :] = rstd
        r.after[r0 + 8 : r0 + 8 + size, :] = (n * scale_a + shift_a) * keep(r0, size)
    r.dafter[0 : rows + 16, :] = jnp.zeros((rows + 16, D), F32)
    weighted = readout * scale_b
    weighted_mean = jnp.mean(weighted, axis=1, keepdims=True)
    high, low = halves(readout)
    row = iota((16, D), 0)
    two = jnp.where(row == 0, high.astype(F32), jnp.where(row == 1, low.astype(F32), 0.0))
    two = two.astype(BF16)
    for r0, size in tiles:
        at = slice(r0, r0 + size)
        unfold(r.after, r.cols_b, r0, size)
        value, slope = gelu_pair(dot(r.cols_b[at, :], conv_b[...]))
        n, rstd = normed(value)
        after = n * scale_b + shift_b
        high, low = halves(after)
        with_high, with_low = dot_nt(two, high), dot_nt(two, low)
        guess = with_high[0:1] + with_high[1:2] + with_low[0:1]
        estimate[:, at] = guess * keep_row(r0, size)
        column = jnp.broadcast_to(cotangent[:, at], (128, size)).T
        column = jnp.concatenate([column, column], axis=1) * keep(r0, size)
        r.a_vec[p, 2:3, :] += readout * column_sum(column * n)
        r.a_vec[p, 3:4, :] += readout * column_sum(column)
        r.a_vec[p, 4:5, :] += column_sum(column * after)
        inner = jnp.mean(weighted * n, axis=1, keepdims=True)
        gradient = (column * (weighted - weighted_mean - n * inner) * rstd * slope).astype(BF16)
        r.grad_b[at, :] = gradient
        fold(r.dafter, gradient, conv_b, r0, size)
    hidden[0 : rows + 16, :] = jnp.zeros((rows + 16, D), F32)
    for r0, size in tiles:
        at = slice(r0, r0 + size)
        dy = r.dafter[r0 + 8 : r0 + 8 + size, :] * keep(r0, size)
        n = r.norm_a[at, :]
        r.a_vec[p, 0:1, :] += column_sum(dy * n)
        r.a_vec[p, 1:2, :] += column_sum(dy)
        gradient = norm_back(dy * scale_a, n, r.rstd_a[at, :]) * r.slope_a[at, :]
        gradient = gradient.astype(BF16)
        r.grad_a[at, :] = gradient
        fold(hidden, gradient, conv_a, r0, size)
    r.a_conv[p, 0] += dot_tn(r.grad_a[0:rows, :], r.cols_a[0:rows, :])
    r.a_conv[p, 1] += dot_tn(r.grad_b[0:rows, :], r.cols_b[0:rows, :])


def predictor_kernel(sequences, names, *refs):
    r = Refs(names, refs)
    r.a_conv[...] = jnp.zeros_like(r.a_conv)
    r.a_vec[...] = jnp.zeros_like(r.a_vec)
    r.a_table[...] = jnp.zeros_like(r.a_table)
    r.dcols3[0:16, :] = jnp.zeros((16, 3 * D), F32)
    r.durations_pad[...] = jnp.zeros_like(r.durations_pad)
    r.durations_pad[0:sequences, 0:PHONES] = r.durations[...]
    stop = span_ends(r.durations_pad[...])
    r.stop[...] = stop
    r.start[...] = stop - r.durations_pad[...]
    counts = [r.counts[s] for s in range(sequences)]
    slots = sequences * SLOT
    r.hidden[0, 0 : slots + 16, :] = jnp.zeros((slots + 16, D), F32)
    for s in range(sequences):
        r.hidden[0, s * SLOT + 8 : s * SLOT + 8 + PHONES, :] = r.encoded[s]

    def keep_slots(r0, size):
        return slot_keep(counts, r0, size)

    def keep_slots_row(r0, size):
        lane = iota((1, size), 1) + r0
        kept = lane < counts[0]
        for s in range(1, sequences):
            kept = kept | ((lane >= s * SLOT) & (lane < s * SLOT + counts[s]))
        return kept.astype(F32)

    predict(
        r, 0, slots, keep_slots, keep_slots_row, r.hidden.at[0], r.cot_duration, r.duration_pred
    )
    for s in range(sequences):
        r.dencoded[s] = r.hidden[0, s * SLOT + 8 : s * SLOT + 8 + PHONES, :]
    r.encoded_high[...] = jnp.zeros_like(r.encoded_high)
    r.encoded_low[...] = jnp.zeros_like(r.encoded_low)

    def one(s):
        count = r.frames[s]
        high, low = halves(r.encoded[s])
        r.encoded_high[0:PHONES, :] = high
        r.encoded_low[0:PHONES, :] = low
        start, stop = r.start[pl.ds(s, 1), :], r.stop[pl.ds(s, 1), :]
        edge = jnp.zeros((8, D), F32)
        for k in range(2):
            r.hidden[k, 0:8, :] = edge
            r.hidden[k, FRAMES + 8 : FRAMES + 16, :] = edge
        for r0, size in pieces(FRAMES, T):
            at = slice(r0, r0 + size)
            expand = expansion(start, stop, r0, size)
            r.expand[at, :] = expand
            hot = hot_columns(r.pitch_bins[pl.ds(s, 1), at], count, r0, size)
            r.hot[:, at] = hot
            frames = dot(expand, r.encoded_high[...]) + dot(expand, r.encoded_low[...])
            r.hidden[0, r0 + 8 : r0 + 8 + size, :] = frames
            pitched = frames + dot_tn(hot, r.pitch_table[...])
            r.hidden[1, r0 + 8 : r0 + 8 + size, :] = pitched

        def keep(r0, size):
            return (iota((size, 1), 0) + r0 < count).astype(F32)

        def keep_row(r0, size):
            return (iota((1, size), 1) + r0 < count).astype(F32)

        def both(k):
            line = pl.ds(k * sequences + s, 1)
            predict(
                r, k + 1, FRAMES, keep, keep_row, r.hidden.at[k],
                r.cot_frames.at[line], r.frame_preds.at[line],
            )

        each(2, both)
        high, low = halves(r.hidden[1, 8 : FRAMES + 8, :])
        r.a_table[...] += dot(r.hot[...], high) + dot(r.hot[...], low)
        high, low = halves(r.hidden[0, 8 : FRAMES + 8, :] + r.hidden[1, 8 : FRAMES + 8, :])
        dencoded = dot_tn(r.expand[...], high) + dot_tn(r.expand[...], low)
        r.dencoded[s] = r.dencoded[s] + dencoded[0:PHONES]

    each(sequences, one)
    for p in range(3):
        for k in range(2):
            at = (2 * p + k) * 3 * D
            r.pack[:, at : at + 3 * D] = r.a_conv[p, k].astype(BF16)
    r.pack[:, AT_TABLES : AT_TABLES + BINS] = r.a_table[...].T.astype(BF16)
    r.pack[:, AT_TABLES + BINS : AT_VECTORS] = jnp.zeros((D, AT_VECTORS - AT_TABLES - BINS), BF16)
    rows = jnp.concatenate([r.a_vec[p] for p in range(3)] + [jnp.zeros((104, D), F32)], axis=0)
    r.pack[:, AT_VECTORS:] = rows.T.astype(BF16)


def predictors(encoded, durations, frames, counts, pitch_bins, convs, scales, shifts, readouts,
               pitch_table, cot_duration, cot_frames):
    n = encoded.shape[0]
    return build(
        functools.partial(predictor_kernel, n),
        "predictors",
        [
            ("frames", frames),
            ("counts", counts),
            ("encoded", encoded),
            ("durations", durations),
            ("pitch_bins", pitch_bins),
            ("convs", convs),
            ("scales", scales),
            ("shifts", shifts),
            ("readouts", readouts),
            ("pitch_table", pitch_table),
            ("cot_duration", cot_duration),
            ("cot_frames", cot_frames),
        ],
        [
            ("duration_pred", (1, n * SLOT), F32),
            ("frame_preds", (2 * n, FRAMES), F32),
            ("dencoded", (n, PHONES, D), F32),
            ("pack", (D, PACK), BF16),
        ],
        dict(
            a_conv=pltpu.VMEM((3, 2, D, 3 * D), F32),
            a_vec=pltpu.VMEM((3, 8, D), F32),
            a_table=pltpu.VMEM((BINS, D), F32),
            durations_pad=pltpu.VMEM((8, 256), jnp.int32),
            start=pltpu.VMEM((8, 256), jnp.int32),
            stop=pltpu.VMEM((8, 256), jnp.int32),
            encoded_high=pltpu.VMEM((256, D), BF16),
            encoded_low=pltpu.VMEM((256, D), BF16),
            expand=pltpu.VMEM((FRAMES, 256), BF16),
            hot=pltpu.VMEM((BINS, FRAMES), BF16),
            hidden=pltpu.VMEM((2, FRAMES + 16, D), F32),
            after=pltpu.VMEM((FRAMES + 16, D), F32),
            dafter=pltpu.VMEM((FRAMES + 16, D), F32),
            cols_a=pltpu.VMEM((FRAMES, 3 * D), BF16),
            cols_b=pltpu.VMEM((FRAMES, 3 * D), BF16),
            slope_a=pltpu.VMEM((FRAMES, D), F32),
            norm_a=pltpu.VMEM((FRAMES, D), F32),
            rstd_a=pltpu.VMEM((FRAMES, 1), F32),
            grad_a=pltpu.VMEM((FRAMES, D), BF16),
            grad_b=pltpu.VMEM((FRAMES, D), BF16),
            dcols3=pltpu.VMEM((T + 32, 3 * D), F32),
        ),
        smem=("frames", "counts"),
    )


def unwritten(outputs):
    def kernel(*refs):
        del refs

    return pl.pallas_call(
        kernel,
        name="unwritten",
        out_specs=[pl.BlockSpec(memory_space=pl.ANY)] * len(outputs),
        out_shape=[jax.ShapeDtypeStruct(shape, kind) for _, shape, kind in outputs],
    )()


def swapped(array):
    return lax.ppermute(array, "section", [(0, 1), (1, 0)])


def scattered(arrays):
    ways = lax.axis_size("dp")
    shares = [a.shape[0] // ways for a in arrays]
    flat = jnp.concatenate([a.reshape(ways, -1) for a in arrays], axis=1)
    flat = lax.psum_scatter(flat, "dp", scatter_dimension=0, tiled=True)[0]
    out, at = [], 0
    for a, share in zip(arrays, shares):
        size = share * a.shape[1]
        out.append(flat[at : at + size].reshape(share, a.shape[1]).astype(F32))
        at += size
    return out


def body(phonemes, phone_lengths, durations, pitch_bins, energy_bins, joint_weight, output_weight,
         widen_weight, narrow_weight, block_scales, block_shifts, predictor_convs,
         predictor_scales, predictor_shifts, predictor_outputs, pitch_table, energy_table,
         mel_weight, mel_cotangent, duration_cotangent, pitch_cotangent, energy_cotangent):
    section = lax.axis_index("section")
    first = section == 0
    n = phonemes.shape[0]
    frames = jnp.sum(durations, axis=1)
    weights = (joint_weight[0], joint_weight[0].T, output_weight[0], widen_weight[0],
               narrow_weight[0], block_scales[0], block_shifts[0])
    cot_duration = jnp.pad(duration_cotangent, ((0, 0), (0, SLOT - PHONES))).reshape(1, n * SLOT)
    cot_frames = jnp.concatenate([pitch_cotangent, energy_cotangent])
    encoded_outs = [("encoded", (n, PHONES, D), F32), ("encoded_lo", (n, PHONES, D), BF16)]
    encoded, encoded_lo = lax.cond(
        first,
        lambda: tuple(encoder_forward(phonemes, phone_lengths, weights)),
        lambda: tuple(unwritten(encoded_outs)),
    )
    arrived = lax.ppermute(encoded_lo, "section", [(0, 1)])
    blank_preds = [("d", (1, n * SLOT), F32), ("f", (2 * n, FRAMES), F32)]
    blank_mel = [("mel", (n, FRAMES, MELS), F32)]

    def near(_):
        duration, preds, dencoded, pack = predictors(
            encoded, durations, frames, phone_lengths, pitch_bins, predictor_convs,
            predictor_scales, predictor_shifts, predictor_outputs, pitch_table, cot_duration,
            cot_frames,
        )
        return (duration, preds, *unwritten(blank_mel), dencoded, *unwritten(GRADS), pack)

    def far(sent):
        mel, dencoded, *grads, pack = decoder(
            sent, durations, frames, pitch_bins, energy_bins, weights, pitch_table, energy_table,
            mel_weight, mel_cotangent,
        )
        return (*unwritten(blank_preds), mel, dencoded, *grads, pack)

    duration, preds, mel, dencoded, *grads = lax.cond(first, near, far, arrived)
    grads, pack = grads[:-1], grads[-1]
    returned = lax.ppermute(dencoded, "section", [(1, 0)])

    def finish(returned):
        return tuple(encoder_backward(phonemes, phone_lengths, weights, dencoded, returned))

    blank_input = [("grad_input", (n, PHONES, D), F32)]
    grad_input, *grads = lax.cond(
        first, finish, lambda _: (*unwritten(blank_input), *grads), returned
    )
    g_joint, g_output, g_widen, g_narrow, g_vec = grads
    g_joint, g_output, g_widen, g_narrow, g_vec, pack = scattered(
        [g_joint, g_output, g_widen, g_narrow, g_vec, pack]
    )
    pack = pack + swapped(pack.astype(BF16)).astype(F32)
    half, some = FRAMES // 2, PHONES // 2
    duration = duration.reshape(n, SLOT)[:, :PHONES]
    away = swapped(
        jnp.where(
            first,
            jnp.concatenate(
                [
                    preds[:, half:].reshape(-1),
                    duration[:, some:].reshape(-1),
                    grad_input[:, some:].reshape(-1),
                ]
            ).astype(BF16),
            jnp.zeros((1,), BF16),
        )
    ).astype(F32)
    a = 2 * n * half
    b = a + n * some
    away_preds, away_duration, away_input = (
        away[:a].reshape(2 * n, half), away[a:b].reshape(n, some), away[b:].reshape(n, some, D),
    )
    away_mel = swapped(mel[:, :half].astype(BF16)).astype(F32)
    mel_out = jnp.where(first, away_mel, mel[:, half:])
    preds = jnp.where(first, preds[:, :half], away_preds)
    duration = jnp.where(first, duration[:, :some], away_duration)
    grad_input = jnp.where(first, grad_input[:, :some], away_input)
    vec = pack[:, AT_VECTORS : AT_VECTORS + 24].reshape(-1, 3, 8)
    return (
        mel_out,
        duration,
        preds[:n],
        preds[n:],
        grad_input,
        g_joint[None],
        g_output[None],
        g_widen[None],
        g_narrow[None],
        g_vec[:, 0:4:2].T[None],
        g_vec[:, 1:4:2].T[None],
        pack[:, :AT_TABLES].reshape(-1, 3, 2, 3 * D).transpose(1, 2, 3, 0),
        vec[:, :, 0:4:2].transpose(1, 2, 0),
        vec[:, :, 1:4:2].transpose(1, 2, 0),
        vec[:, :, 4].T,
        pack[:, AT_TABLES : AT_TABLES + BINS].T,
        pack[:, AT_TABLES + BINS : AT_MEL].T,
        pack[:, AT_MEL : AT_MEL + MELS],
    )


def solution(mesh):
    rows = P("dp", None)
    table = P("section", None, None)
    return jax.shard_map(
        body,
        mesh=mesh,
        in_specs=(
            P("dp", None, None), P("dp"), rows, rows, rows,
            table, table, table, table, table, table,
            P(), P(), P(), P(), P(), P(), P(),
            P("dp", None, None), rows, rows, rows,
        ),
        out_specs=(
            P("dp", "section", None),
            P("dp", "section"),
            P("dp", "section"),
            P("dp", "section"),
            P("dp", "section", None),
            P("section", "dp", None),
            P("section", "dp", None),
            P("section", "dp", None),
            P("section", "dp", None),
            P("section", None, "dp"),
            P("section", None, "dp"),
            P(None, None, None, "dp"),
            P(None, None, "dp"),
            P(None, None, "dp"),
            P(None, "dp"),
            P(None, "dp"),
            P(None, "dp"),
            P("dp", None),
        ),
        check_vma=False,
    )
```

```python
import functools
import itertools
import math

import jax
import jax.numpy as jnp
from jax import lax
from jax.experimental import pallas as pl
from jax.experimental.pallas import tpu as pltpu
from jax.sharding import PartitionSpec as P

D = 256
HEAD = 128
FF = 1024
BINS = 256
MELS = 80
TAPS = 9
PHONES = 160
FRAMES = 1024
SLOT = 192
WIDE = TAPS * D
EPS = 1e-5
AT_VECTORS = 6 * 3 * D
AT_TABLES = AT_VECTORS + 128
AT_MEL = AT_TABLES + 2 * BINS
PACK = AT_MEL + 128
NEAR_PACK = AT_TABLES + BINS
C1 = math.sqrt(2.0 / math.pi)
C2 = C1 * 0.044715
SCALE = HEAD**-0.5
SECTION = "section"
DP = "dp"
LOG2E = math.log2(math.e)
F32 = jnp.float32
BF16 = jnp.bfloat16


def names(**kept):
    return tuple(kept)


def dot(a, b):
    return jnp.dot(a, b, preferred_element_type=F32)


def dot_nt(a, b):
    return lax.dot_general(a, b, (((1,), (1,)), ((), ())), preferred_element_type=F32)


def dot_tn(a, b):
    return lax.dot_general(a, b, (((0,), (0,)), ((), ())), preferred_element_type=F32)


def iota(shape, dim):
    return lax.broadcasted_iota(jnp.int32, shape, dim)


def gelu_pair(x):
    x2 = x * x
    h = 0.5 + 0.5 * jnp.tanh(x * (C1 + C2 * x2))
    value = x * h
    slope = h + value * (1.0 - h) * (2.0 * C1 + 6.0 * C2 * x2)
    return value, slope


def normed(r):
    mean = jnp.mean(r, axis=-1, keepdims=True)
    centred = r - mean
    rstd = lax.rsqrt(jnp.mean(centred * centred, axis=-1, keepdims=True) + EPS)
    return centred * rstd, rstd


def norm_back(t, n, rstd):
    return (
        t - jnp.mean(t, axis=-1, keepdims=True) - n * jnp.mean(t * n, axis=-1, keepdims=True)
    ) * rstd


def column_sum(x):
    return jnp.sum(x, axis=0, keepdims=True)


def aligned(i, size):
    return pl.ds(pl.multiple_of(i * size, size), size)


def each(count, body):
    def step(i, carry):
        body(i)
        return carry

    lax.fori_loop(0, count, step, 0)


class Layout:
    def __init__(self, segments, span, query):
        self.segments, self.span, self.query = segments, span, query
        self.rows = segments * span
        self.fewest = span // 2


ENC = Layout(4, SLOT, SLOT)
DEC = Layout(1, FRAMES, 256)
T = 256
AHEAD = 2


def pieces(length, size):
    return [(at, min(size, length - at)) for at in range(0, length, size)]


def block_scratch(layout, backward):
    L, S, n = layout.rows, layout.span, layout.segments
    shapes = dict(
        h_lo=pltpu.VMEM((L, D), BF16),
        joint=pltpu.VMEM((L, 3 * D), BF16),
        jointT=pltpu.VMEM((n, 3 * D, S), BF16),
        mixedT=pltpu.VMEM((n, D, S), BF16),
        first=pltpu.VMEM((L + 16, D), F32),
        cols=pltpu.VMEM((L, WIDE), BF16),
        slope=pltpu.VMEM((L, FF), F32),
        wide=pltpu.VMEM((2, T, D), F32),
        second=pltpu.VMEM((L, D), F32),
        widen=pltpu.VMEM((WIDE, FF), BF16),
        narrow=pltpu.VMEM((FF, D), BF16),
        sem=pltpu.SemaphoreType.DMA((6,)),
    )
    if backward:
        shapes.update(
            expo=pltpu.VMEM((n, 2, S, S), BF16),
            rinv=pltpu.VMEM((n, 2, 8, S), F32),
            n1=pltpu.VMEM((L, D), F32),
            r1=pltpu.VMEM((L, 1), F32),
            act=pltpu.VMEM((L, FF), BF16),
            spare=pltpu.VMEM((WIDE - 2 * L, FF), BF16),
            dnar=pltpu.VMEM((max(L, FF), D), BF16),
            dwid=pltpu.VMEM((L, FF), BF16),
            dcols=pltpu.VMEM((T + 32, WIDE), F32),
            dfirst=pltpu.VMEM((L + 16, D), F32),
            datt=pltpu.VMEM((L, D), BF16),
            dmixT=pltpu.VMEM((n, D, S), BF16),
            inner=pltpu.VMEM((n, 2, 8, S), F32),
            djointT=pltpu.VMEM((n, 3 * D, S), BF16),
            joint_turned=pltpu.VMEM((3 * D, D), BF16),
            a_joint=pltpu.VMEM((3 * D, D), F32),
            a_output=pltpu.VMEM((D, D), F32),
            a_widen=pltpu.VMEM((WIDE, FF), F32),
            a_narrow=pltpu.VMEM((FF, D), F32),
            a_vec=pltpu.VMEM((8, D), F32),
        )
    return shapes


def start_block(layout, b):
    edge = jnp.zeros((8, D), F32)
    b.first[0:8, :] = edge
    b.first[layout.rows + 8 : layout.rows + 16, :] = edge


def zero_accumulators(b, w):
    b.joint_turned[...] = w.joint[...].T
    b.a_joint[...] = jnp.zeros_like(b.a_joint)
    b.a_output[...] = jnp.zeros_like(b.a_output)
    b.a_narrow[...] = jnp.zeros_like(b.a_narrow)
    b.a_vec[...] = jnp.zeros_like(b.a_vec)

    def body(t, _):
        b.a_widen[aligned(t, D), :] = jnp.zeros((D, FF), F32)
        return 0

    lax.fori_loop(0, TAPS, body, 0)
    edge = jnp.zeros((16, WIDE), F32)
    b.dcols[0:16, :] = edge


def heads(h):
    return tuple(slice(k * D + h * HEAD, k * D + (h + 1) * HEAD) for k in range(3))


def span(start, size):
    if isinstance(start, int):
        return slice(start, start + size)
    return pl.ds(pl.multiple_of(start, math.gcd(size, 256)), size)


def tile_rows(k, extra=0, first=0):
    return pl.ds(pl.multiple_of(k * T + first, 8), T + extra)


def attention_forward(layout, b, w, counts, length):
    S, save = layout.span, hasattr(b, "expo")
    blocks = [(s, at, q) for s in range(layout.segments) for at, q in pieces(length, layout.query)]
    for s, at, q in blocks:
        rows = slice(s * S + at, s * S + at + q)
        value = dot(b.h_lo[rows, :], w.joint[...]).astype(BF16)
        b.joint[rows, :] = value
        b.jointT[s, :, at : at + q] = value.T
    chunks = pieces(length, D)
    items = [block + (h,) for block in blocks for h in range(2)]

    def score(i):
        s, at, q, h = items[i]
        query_at, key_at, _ = heads(h)
        side = slice((i % 2) * D, (i % 2) * D + q)
        top = None
        for c, size in chunks:
            scores = dot(
                b.joint[s * S + c : s * S + c + size, key_at], b.jointT[s, query_at, at : at + q]
            )
            if c + size > layout.fewest:
                scores = jnp.where(iota((size, q), 0) + c < counts[s], scores, -1e30)
            b.slope[c : c + size, side] = scores
            part = jnp.max(scores.reshape(size // 8, 8, q), axis=0)
            top = part if top is None else jnp.maximum(top, part)
        return jnp.max(top, axis=0, keepdims=True)

    tops = {0: score(0)}
    for i, (s, at, q, h) in enumerate(items):
        if i + 1 < len(items):
            tops[i + 1] = score(i + 1)
        query_at, _, value_at = heads(h)
        side = slice((i % 2) * D, (i % 2) * D + q)
        sums = mixed = None
        for c, size in chunks:
            expo = jnp.exp2((b.slope[c : c + size, side] - tops[i]) * (SCALE * LOG2E))
            part = jnp.sum(expo.reshape(size // 8, 8, q), axis=0)
            sums = part if sums is None else sums + part
            expo = expo.astype(BF16)
            if save:
                b.expo[s, h, c : c + size, at : at + q] = expo
            part = dot(b.jointT[s, value_at, c : c + size], expo)
            mixed = part if mixed is None else mixed + part
        rinv = 1.0 / column_sum(sums)
        b.mixedT[s, query_at, at : at + q] = (mixed * rinv).astype(BF16)
        if save:
            b.rinv[s, h, :, at : at + q] = jnp.broadcast_to(rinv, (8, q))
    for s, at, q in blocks:
        r0 = s * S + at
        attended = dot_tn(b.mixedT[s, :, at : at + q], w.output[...])
        n, rstd = normed(b.h_lo[r0 : r0 + q, :].astype(F32) + attended)
        keep = (iota((q, 1), 0) + at < counts[s]).astype(F32)
        b.first[r0 + 8 : r0 + 8 + q, :] = (n * w.scales[0:1, :] + w.shifts[0:1, :]) * keep
        if save:
            b.n1[r0 : r0 + q, :] = n
            b.r1[r0 : r0 + q, :] = rstd


def ffn_forward(b, w, length):
    save = hasattr(b, "expo")
    tiles = pieces(length, T)
    items = [(k, j) for k in range(len(tiles)) for j in range(4)]

    def unfold(k):
        r0, size = tiles[k]
        v = b.first[r0 : r0 + size + 16, :]
        for t in range(TAPS):
            b.cols[r0 : r0 + size, t * D : (t + 1) * D] = v[4 + t : 4 + t + size].astype(BF16)

    def widen(i):
        k, j = items[i]
        r0, size = tiles[k]
        b.wide[i % 2, 0:size, :] = dot(b.cols[r0 : r0 + size, :], b.widen[:, j * D : (j + 1) * D])

    unfold(0)
    widen(0)
    for i, (k, j) in enumerate(items):
        if j == 1 and k + 1 < len(tiles):
            unfold(k + 1)
        if i + 1 < len(items):
            widen(i + 1)
        r0, size = tiles[k]
        rows, at = slice(r0, r0 + size), slice(j * D, (j + 1) * D)
        value, slope = gelu_pair(b.wide[i % 2, 0:size, :])
        value = value.astype(BF16)
        if save:
            b.act[rows, at] = value
            b.slope[rows, at] = slope
        narrowed = dot(value, b.narrow[at, :])
        before = b.second[rows, :] if j else b.first[r0 + 8 : r0 + 8 + size, :]
        b.second[rows, :] = before + narrowed


def ffn_backward(b, w, length):
    b.dfirst[0 : length + 16, :] = jnp.zeros((length + 16, D), F32)
    for r0, size in pieces(length, T):
        rows = slice(r0, r0 + size)
        b.dcols[16 + size : 32 + size, :] = jnp.zeros((16, WIDE), F32)
        for j in range(4):
            at = slice(j * D, (j + 1) * D)
            b.dwid[rows, at] = (
                dot_nt(b.dnar[rows, :], b.narrow[at, :]) * b.slope[rows, at]
            ).astype(BF16)
        for t in range(TAPS):
            at = slice(t * D, (t + 1) * D)
            b.dcols[16 : 16 + size, at] = dot_nt(b.dwid[rows, :], b.widen[at, :])
        total = b.dcols[12 : 28 + size, 0:D]
        for t in range(1, TAPS):
            total = total + b.dcols[12 - t : 28 - t + size, t * D : (t + 1) * D]
        b.dfirst[r0 : r0 + size + 16, :] += total
        b.dfirst[r0 + 8 : r0 + 8 + size, :] += b.second[rows, :]


def ffn_weight_grads(b, length):
    def widen(t, _):
        at = aligned(t, 3 * D)
        b.a_widen[at, :] += dot_tn(b.cols[0:length, at], b.dwid[0:length, :])
        return 0

    lax.fori_loop(0, 3, widen, 0)
    b.a_narrow[...] += dot_tn(b.act[0:length, :], b.dnar[0:length, :])


def attention_backward(layout, b, w, counts, length, finish):
    S = layout.span
    blocks = [(s, at, q) for s in range(layout.segments) for at, q in pieces(length, layout.query)]
    chunks = pieces(length, D)
    for s, at, q in blocks:
        r0 = s * S + at
        rows, pad_rows, lanes = slice(r0, r0 + q), slice(r0 + 8, r0 + 8 + q), slice(at, at + q)
        keep = (iota((q, 1), 0) + at < counts[s]).astype(F32)
        dy = b.dfirst[pad_rows, :] * keep
        n = b.n1[rows, :]
        b.a_vec[0:1, :] += column_sum(dy * n)
        b.a_vec[1:2, :] += column_sum(dy)
        dsum = norm_back(dy * w.scales[0:1, :], n, b.r1[rows, :])
        b.dfirst[pad_rows, :] = dsum
        datt = dsum.astype(BF16)
        b.datt[rows, :] = datt
        dmix = dot_nt(w.output[...], datt)
        for h in range(2):
            head = heads(h)[0]
            part = (dmix[head, :] * b.rinv[s, h, 0:1, lanes]).astype(BF16)
            b.dmixT[s, head, lanes] = part
            inner = column_sum(part.astype(F32) * b.mixedT[s, head, lanes].astype(F32))
            b.inner[s, h, :, lanes] = jnp.broadcast_to(inner, (8, q))
    items = [block + (h,) for block in blocks for h in range(2)]

    def score(i):
        s, at, q, h = items[i]
        side = slice((i % 2) * D, (i % 2) * D + q)
        b.slope[0:length, side] = dot(
            b.joint[s * S : s * S + length, heads(h)[2]], b.dmixT[s, heads(h)[0], at : at + q]
        )

    score(0)
    for i, (s, at, q, h) in enumerate(items):
        if i + 1 < len(items):
            score(i + 1)
        query_at, key_at, _ = heads(h)
        lanes, side = slice(at, at + q), slice((i % 2) * D, (i % 2) * D + q)
        dquery = None
        for c, size in chunks:
            expo = b.expo[s, h, c : c + size, lanes].astype(F32)
            ds = expo * (b.slope[c : c + size, side] - b.inner[s, h, 0:1, lanes])
            ds = ds.astype(BF16)
            part = dot(b.jointT[s, key_at, c : c + size], ds)
            dquery = part if dquery is None else dquery + part
            b.cols[s * S + at : s * S + at + q, h * FRAMES + c : h * FRAMES + c + size] = ds.T
        b.djointT[s, query_at, lanes] = (dquery * SCALE).astype(BF16)
    for s in range(layout.segments):
        rows = slice(s * S, s * S + length)
        for h in range(2):
            query_at, key_at, value_at = heads(h)
            for c, size in chunks:
                lanes = slice(c, c + size)
                dkey = dot(
                    b.jointT[s, query_at, 0:length],
                    b.cols[rows, h * FRAMES + c : h * FRAMES + c + size],
                )
                b.djointT[s, key_at, lanes] = (dkey * SCALE).astype(BF16)
                dvalue = dot_nt(b.dmixT[s, query_at, 0:length], b.expo[s, h, lanes, 0:length])
                b.djointT[s, value_at, lanes] = dvalue.astype(BF16)
        b.a_output[...] += dot(b.mixedT[s, :, 0:length], b.datt[rows, :])
        b.a_joint[...] += dot(b.djointT[s, :, 0:length], b.h_lo[rows, :])
    for s, at, q in blocks:
        dh = dot_tn(b.djointT[s, :, at : at + q], b.joint_turned[...])
        finish(s, at, q, dh + b.dfirst[s * S + at + 8 : s * S + at + 8 + q, :])


def second_norm_back(b, w, r0, size, dy, n, rstd):
    b.a_vec[2:3, :] += column_sum(dy * n)
    b.a_vec[3:4, :] += column_sum(dy)
    dsecond = norm_back(dy * w.scales[1:2, :], n, rstd)
    b.second[r0 : r0 + size, :] = dsecond
    b.dnar[r0 : r0 + size, :] = dsecond.astype(BF16)


class Refs:
    def __init__(self, names, refs):
        for name, ref in zip(names, refs):
            setattr(self, name, ref)


WEIGHTS = names(joint=1, output=1, widen_far=1, narrow_far=1, scales=1, shifts=1)
FAR = names(w_widen_far=1, w_narrow_far=1, g_widen=1, g_narrow=1)


def send_large_grads(b, o):
    b.dnar[0:FF, :] = b.a_narrow[...].astype(BF16)
    pltpu.make_async_copy(b.dnar.at[pl.ds(0, FF)], o.g_narrow, b.sem.at[2]).start()
    at = 0
    for k, (buffer, size) in enumerate(large_parts(b)):
        buffer[0:size, :] = b.a_widen[at : at + size, :].astype(BF16)
        pltpu.make_async_copy(
            buffer.at[pl.ds(0, size)], o.g_widen.at[pl.ds(at, size)], b.sem.at[3 + k]
        ).start()
        at += size


def large_parts(b):
    size = b.act.shape[0]
    left = WIDE - 2 * size
    return ((b.act, size), (b.dwid, size), (b.spare, left))


def store_block_grads(b, o):
    o.g_joint[...] = b.a_joint[...].T.astype(BF16)
    o.g_output[...] = b.a_output[...].astype(BF16)
    rows = jnp.concatenate([b.a_vec[...], jnp.zeros((120, D), F32)], axis=0)
    o.g_vec[...] = rows.T.astype(BF16)
    pltpu.make_async_copy(b.dnar.at[pl.ds(0, FF)], o.g_narrow, b.sem.at[2]).wait()
    at = 0
    for k, (buffer, size) in enumerate(large_parts(b)):
        pltpu.make_async_copy(
            buffer.at[pl.ds(0, size)], o.g_widen.at[pl.ds(at, size)], b.sem.at[3 + k]
        ).wait()
        at += size


def start_weights(b, w):
    pltpu.make_async_copy(w.widen_far, b.widen, b.sem.at[0]).start()
    pltpu.make_async_copy(w.narrow_far, b.narrow, b.sem.at[1]).start()


def wait_weights(b, w):
    pltpu.make_async_copy(w.widen_far, b.widen, b.sem.at[0]).wait()
    pltpu.make_async_copy(w.narrow_far, b.narrow, b.sem.at[1]).wait()


GRADS = dict(
    g_joint=((D, 3 * D), BF16),
    g_output=((D, D), BF16),
    g_widen=((WIDE, FF), BF16),
    g_narrow=((FF, D), BF16),
    g_vec=((D, 128), BF16),
)


def expansion(start, stop, first_row, size):
    row = iota((size, 256), 0) + first_row
    return ((row >= start) & (row < stop)).astype(F32).astype(BF16)


def hot_columns(bins, count, first_lane, size):
    live = iota((1, size), 1) + first_lane < count
    return ((iota((BINS, size), 0) == bins) & live).astype(F32).astype(BF16)


def span_ends(durations):
    upper = (iota((256, 256), 0) <= iota((256, 256), 1)).astype(F32).astype(BF16)
    return dot(durations.astype(F32).astype(BF16), upper).astype(jnp.int32)


def decoder_kernel(sequences, r):
    b, w, o = r, Refs(WEIGHTS, [getattr(r, "w_" + n) for n in WEIGHTS]), r
    layout = DEC
    start_weights(b, w)
    zero_accumulators(b, w)
    start_block(layout, b)
    r.a_mel[...] = jnp.zeros_like(r.a_mel)
    r.a_table[...] = jnp.zeros_like(r.a_table)
    r.durations_pad[...] = jnp.zeros_like(r.durations_pad)
    r.durations_pad[0:sequences, 0:PHONES] = r.durations[...]
    stop = span_ends(r.durations_pad[...])
    r.stop[...] = stop
    r.start[...] = stop - r.durations_pad[...]
    r.encoded_pad[...] = jnp.zeros_like(r.encoded_pad)

    def sequence(s, length):
        count = r.frames[s]
        counts = [count]
        r.encoded_pad[0:PHONES, :] = r.arrived[s]
        start, stop = r.start[pl.ds(s, 1), :], r.stop[pl.ds(s, 1), :]
        tiles = pieces(length, T)
        for r0, size in tiles:
            rows = slice(r0, r0 + size)
            expand = expansion(start, stop, r0, size)
            r.expand[rows, :] = expand
            hot_p = hot_columns(r.pitch_bins[pl.ds(s, 1), rows], count, r0, size)
            hot_e = hot_columns(r.energy_bins[pl.ds(s, 1), rows], count, r0, size)
            r.hot[0:BINS, rows] = hot_p
            r.hot[BINS:, rows] = hot_e
            adapted = dot(expand, r.encoded_pad[...])
            adapted = adapted + dot_tn(hot_p, r.pitch_table[...])
            adapted = adapted + dot_tn(hot_e, r.energy_table[...])
            b.h_lo[rows, :] = adapted.astype(BF16)
        attention_forward(layout, b, w, counts, length)
        b.first[length + 8 : length + 16, :] = jnp.zeros((8, D), F32)
        pl.when(s == 0)(lambda: wait_weights(b, w))
        ffn_forward(b, w, length)
        for r0, size in tiles:
            rows = slice(r0, r0 + size)
            n, rstd = normed(b.second[rows, :])
            keep = (iota((size, 1), 0) + r0 < count).astype(F32)
            decoded = ((n * w.scales[1:2, :] + w.shifts[1:2, :]) * keep).astype(BF16)
            spectrum = dot_nt(r.mel_turned[...], decoded)
            if r0 < FRAMES // 2:
                o.mel_away[s, :, rows] = spectrum.astype(BF16)
            else:
                o.mel_own[s, :, r0 - FRAMES // 2 : r0 - FRAMES // 2 + size] = spectrum
            cotangent = r.mel_cotangent[s, :, rows]
            r.a_mel[...] += dot(cotangent, decoded)
            dy = dot_tn(cotangent, r.mel_turned[...]) * keep
            second_norm_back(b, w, r0, size, dy, n, rstd)
        ffn_backward(b, w, length)
        ffn_weight_grads(b, length)
        pl.when(s == sequences - 1)(lambda: send_large_grads(b, o))

        def finish(_, at, q, dh):
            b.datt[at : at + q, :] = dh.astype(BF16)

        attention_backward(layout, b, w, counts, length, finish)
        dadapted = b.datt[0:length, :]
        r.a_table[...] += dot(r.hot[:, 0:length], dadapted)
        o.dsent[s] = dot_tn(r.expand[0:length, :], dadapted)[0:PHONES].astype(BF16)

    def one(s):
        sequence(s, FRAMES)

    each(sequences, one)
    store_block_grads(b, o)
    r.pack_far[:, 0 : 2 * BINS] = r.a_table[...].T.astype(BF16)
    r.pack_far[:, 2 * BINS :] = jnp.zeros((D, 128), BF16)
    r.pack_far[:, 2 * BINS : 2 * BINS + MELS] = r.a_mel[...].T.astype(BF16)


def section_call(name, inputs, outputs, branches, smem=(), kept=()):
    shapes = {n: (a.shape, a.dtype) for n, a in inputs.items()}

    def kernel(*refs):
        place = dict(zip(inputs, refs))
        target = dict(zip(outputs, refs[len(inputs) :]))

        def run(body, ins, outs, scratch):
            near_ins = [n for n in ins if n not in FAR and n not in smem]
            near_outs = [n for n in outs if n not in FAR]
            local = {n: pltpu.VMEM(*shapes[n]) for n in near_ins}
            local.update({n: pltpu.VMEM(*outputs[n]) for n in near_outs})
            local.update(scratch)
            local.update(
                sem_in=pltpu.SemaphoreType.DMA((len(near_ins),)),
                sem_out=pltpu.SemaphoreType.DMA((len(near_outs),)),
            )

            def scoped(*values):
                r = Refs(list(local), values)
                for n in ins:
                    if n not in near_ins:
                        setattr(r, n, place[n])
                for n in outs:
                    if n not in near_outs:
                        setattr(r, n, target[n])
                copies = [
                    pltpu.make_async_copy(place[n], getattr(r, n), r.sem_in.at[k])
                    for k, n in enumerate(near_ins)
                ]
                for copy in copies:
                    copy.start()
                for copy in copies:
                    copy.wait()
                body(r)
                copies = [
                    pltpu.make_async_copy(getattr(r, n), target[n], r.sem_out.at[k])
                    for k, n in enumerate(near_outs)
                ]
                for copy in copies:
                    copy.start()
                for copy in copies:
                    copy.wait()

            pl.run_scoped(scoped, *local.values())

        for section, branch in enumerate(branches):
            if branch is not None:
                here = (lax.axis_index(SECTION) == section).astype(jnp.int32)
                each(here, lambda _: run(*branch))

    index_in = list(inputs)
    return pl.pallas_call(
        kernel,
        name=name,
        in_specs=[
            pl.BlockSpec(memory_space=pltpu.SMEM if n in smem else pl.ANY) for n in inputs
        ],
        out_specs=[pl.BlockSpec(memory_space=pl.ANY)] * len(outputs),
        out_shape=[jax.ShapeDtypeStruct(*outputs[n]) for n in outputs],
        input_output_aliases={index_in.index(n): k for k, n in enumerate(outputs) if n in kept},
        compiler_params=pltpu.CompilerParams(vmem_limit_bytes=61 * 2**20),
    )(*inputs.values())


W_NAMES = tuple("w_" + n for n in WEIGHTS)
G_NAMES = tuple(GRADS)


def decoder_branch(sequences):
    scratch = dict(
        block_scratch(DEC, True),
        a_mel=pltpu.VMEM((MELS, D), F32),
        a_table=pltpu.VMEM((2 * BINS, D), F32),
        durations_pad=pltpu.VMEM((8, 256), jnp.int32),
        start=pltpu.VMEM((8, 256), jnp.int32),
        stop=pltpu.VMEM((8, 256), jnp.int32),
        encoded_pad=pltpu.VMEM((256, D), BF16),
        expand=pltpu.VMEM((FRAMES, 256), BF16),
        hot=pltpu.VMEM((2 * BINS, FRAMES), BF16),
    )
    ins = names(frames=1, arrived=1, durations=1, pitch_bins=1, energy_bins=1, pitch_table=1,
                energy_table=1, mel_turned=1, mel_cotangent=1)
    outs = names(mel_own=1, mel_away=1, dsent=1, pack_far=1)
    return functools.partial(decoder_kernel, sequences), ins + W_NAMES, outs + G_NAMES, scratch


def load_segments(b, phonemes):
    b.h_lo[...] = jnp.zeros_like(b.h_lo)
    for s in range(ENC.segments):
        b.h_lo[s * SLOT : s * SLOT + PHONES, :] = phonemes[s]


def slot_keep(counts, r0, size):
    row = iota((size, 1), 0) + r0
    kept = row < counts[0]
    for s in range(1, ENC.segments):
        kept = kept | ((row >= s * SLOT) & (row < s * SLOT + counts[s]))
    return kept.astype(F32)


def encoder_forward_kernel(r):
    b, w = r, Refs(WEIGHTS, [getattr(r, "w_" + n) for n in WEIGHTS])
    start_weights(b, w)
    counts = [r.counts[s] for s in range(ENC.segments)]
    start_block(ENC, b)
    load_segments(b, r.phonemes)
    attention_forward(ENC, b, w, counts, SLOT)
    wait_weights(b, w)
    ffn_forward(b, w, ENC.rows)
    for r0, size in pieces(ENC.rows, T):
        n, _ = normed(b.second[r0 : r0 + size, :])
        encoded = (n * w.scales[1:2, :] + w.shifts[1:2, :]) * slot_keep(counts, r0, size)
        b.second[r0 : r0 + size, :] = encoded
    for s in range(ENC.segments):
        encoded = b.second[s * SLOT : s * SLOT + PHONES, :]
        r.encoded[s] = encoded
        r.encoded_lo[s] = encoded.astype(BF16)


def encoder_backward_kernel(r):
    b, w, o = r, Refs(WEIGHTS, [getattr(r, "w_" + n) for n in WEIGHTS]), r
    start_weights(b, w)
    counts = [r.counts[s] for s in range(ENC.segments)]
    zero_accumulators(b, w)
    start_block(ENC, b)
    load_segments(b, r.phonemes)
    attention_forward(ENC, b, w, counts, SLOT)
    wait_weights(b, w)
    ffn_forward(b, w, ENC.rows)
    b.n1_grad[...] = jnp.zeros_like(b.n1_grad)
    for s in range(ENC.segments):
        b.n1_grad[s * SLOT : s * SLOT + PHONES, :] = r.grad_near[s] + r.grad_far[s].astype(F32)
    for r0, size in pieces(ENC.rows, T):
        n, rstd = normed(b.second[r0 : r0 + size, :])
        dy = b.n1_grad[r0 : r0 + size, :] * slot_keep(counts, r0, size)
        second_norm_back(b, w, r0, size, dy, n, rstd)
    ffn_backward(b, w, ENC.rows)
    ffn_weight_grads(b, ENC.rows)
    send_large_grads(b, o)

    def finish(s, at, q, dh):
        o.input_own[s] = dh[0 : PHONES // 2]
        o.input_away[s] = dh[PHONES // 2 : PHONES].astype(BF16)

    attention_backward(ENC, b, w, counts, SLOT, finish)
    store_block_grads(b, o)


def encoder_forward_branch():
    return (
        encoder_forward_kernel,
        names(counts=1, phonemes=1) + W_NAMES,
        names(encoded=1, encoded_lo=1),
        block_scratch(ENC, False),
    )


def encoder_backward_branch():
    return (
        encoder_backward_kernel,
        names(counts=1, phonemes=1, grad_near=1, grad_far=1) + W_NAMES,
        names(input_own=1, input_away=1) + G_NAMES,
        dict(block_scratch(ENC, True), n1_grad=pltpu.VMEM((ENC.rows, D), F32)),
    )


def halves(x):
    high = x.astype(BF16)
    return high, (x - high.astype(F32)).astype(BF16)


def predict(r, p, rows, keep, keep_row, hidden, cotangent, estimate):
    tiles = rows // T
    conv_a, conv_b = r.convs.at[p, 0], r.convs.at[p, 1]
    scale_a, scale_b = r.scales[p, 0:1, :], r.scales[p, 1:2, :]
    shift_a, shift_b = r.shifts[p, 0:1, :], r.shifts[p, 1:2, :]
    readout = r.readouts[pl.ds(p, 1), :]
    edge = jnp.zeros((8, D), F32)
    r.after[0:8, :] = edge
    r.after[rows + 8 : rows + 16, :] = edge

    def unfold(source, target, k):
        v = source[tile_rows(k, 16), :]
        for t in range(3):
            target[tile_rows(k), t * D : (t + 1) * D] = v[7 + t : 7 + t + T].astype(BF16)

    def fold(target, gradient, conv, k):
        r.dcols3[16 : 16 + T, :] = dot_nt(gradient, conv[...])
        total = r.dcols3[9 : 25 + T, 0:D]
        for t in range(1, 3):
            total = total + r.dcols3[9 - t : 25 - t + T, t * D : (t + 1) * D]
        target[tile_rows(k, 16), :] += total

    def clear(target):
        def body(k):
            target[tile_rows(k), :] = jnp.zeros((T, D), F32)

        each(tiles, body)
        target[rows : rows + 16, :] = jnp.zeros((16, D), F32)

    def first_half(k):
        at = tile_rows(k)
        unfold(hidden, r.cols_a, k)
        value, slope = gelu_pair(dot(r.cols_a[at, :], conv_a[...]))
        n, rstd = normed(value)
        r.slope_a[at, :] = slope
        r.norm_a[at, :] = n
        r.rstd_a[at, :] = rstd
        r.after[tile_rows(k, 0, 8), :] = (n * scale_a + shift_a) * keep(k * T, T)

    each(tiles, first_half)
    clear(r.dafter)
    weighted = readout * scale_b
    weighted_mean = jnp.mean(weighted, axis=1, keepdims=True)
    high, low = halves(readout)
    row = iota((16, D), 0)
    two = jnp.where(row == 0, high.astype(F32), jnp.where(row == 1, low.astype(F32), 0.0))
    two = two.astype(BF16)

    def second_half(k):
        at = span(k * T, T)
        unfold(r.after, r.cols_b, k)
        value, slope = gelu_pair(dot(r.cols_b[at, :], conv_b[...]))
        n, rstd = normed(value)
        after = n * scale_b + shift_b
        high, low = halves(after)
        with_high, with_low = dot_nt(two, high), dot_nt(two, low)
        guess = with_high[0:1] + with_high[1:2] + with_low[0:1]
        estimate[:, at] = guess * keep_row(k * T, T)
        column = jnp.broadcast_to(cotangent[:, at], (128, T)).T
        column = jnp.concatenate([column, column], axis=1) * keep(k * T, T)
        r.a_vec[p, 2:3, :] += readout * column_sum(column * n)
        r.a_vec[p, 3:4, :] += readout * column_sum(column)
        r.a_vec[p, 4:5, :] += column_sum(column * after)
        inner = jnp.mean(weighted * n, axis=1, keepdims=True)
        gradient = (column * (weighted - weighted_mean - n * inner) * rstd * slope).astype(BF16)
        r.grad_b[at, :] = gradient
        fold(r.dafter, gradient, conv_b, k)

    each(tiles, second_half)
    clear(hidden)

    def back(k):
        at = tile_rows(k)
        dy = r.dafter[tile_rows(k, 0, 8), :] * keep(k * T, T)
        n = r.norm_a[at, :]
        r.a_vec[p, 0:1, :] += column_sum(dy * n)
        r.a_vec[p, 1:2, :] += column_sum(dy)
        gradient = norm_back(dy * scale_a, n, r.rstd_a[at, :]) * r.slope_a[at, :]
        gradient = gradient.astype(BF16)
        r.grad_a[at, :] = gradient
        fold(hidden, gradient, conv_a, k)

    each(tiles, back)
    r.a_conv[p, 0] += dot_tn(r.grad_a[0:rows, :], r.cols_a[0:rows, :])
    r.a_conv[p, 1] += dot_tn(r.grad_b[0:rows, :], r.cols_b[0:rows, :])


def predictor_kernel(sequences, r):
    r.a_conv[...] = jnp.zeros_like(r.a_conv)
    r.a_vec[...] = jnp.zeros_like(r.a_vec)
    r.a_table[...] = jnp.zeros_like(r.a_table)
    r.dcols3[0:16, :] = jnp.zeros((16, 3 * D), F32)
    r.dcols3[16 + T :, :] = jnp.zeros((16, 3 * D), F32)
    r.durations_pad[...] = jnp.zeros_like(r.durations_pad)
    r.durations_pad[0:sequences, 0:PHONES] = r.durations[...]
    stop = span_ends(r.durations_pad[...])
    r.stop[...] = stop
    r.start[...] = stop - r.durations_pad[...]
    counts = [r.counts[s] for s in range(sequences)]
    slots = sequences * SLOT
    r.hidden[0, 0 : slots + 16, :] = jnp.zeros((slots + 16, D), F32)
    for s in range(sequences):
        r.hidden[0, s * SLOT + 8 : s * SLOT + 8 + PHONES, :] = r.encoded[s]

    def keep_slots(r0, size):
        return slot_keep(counts, r0, size)

    def keep_slots_row(r0, size):
        lane = iota((1, size), 1) + r0
        kept = lane < counts[0]
        for s in range(1, sequences):
            kept = kept | ((lane >= s * SLOT) & (lane < s * SLOT + counts[s]))
        return kept.astype(F32)

    predict(
        r, 0, slots, keep_slots, keep_slots_row, r.hidden.at[0], r.cot_duration, r.duration_pred
    )
    for s in range(sequences):
        r.dencoded[s] = r.hidden[0, s * SLOT + 8 : s * SLOT + 8 + PHONES, :]
    r.encoded_high[...] = jnp.zeros_like(r.encoded_high)
    r.encoded_low[...] = jnp.zeros_like(r.encoded_low)

    def one(s):
        count = r.frames[s]
        high, low = halves(r.encoded[s])
        r.encoded_high[0:PHONES, :] = high
        r.encoded_low[0:PHONES, :] = low
        start, stop = r.start[pl.ds(s, 1), :], r.stop[pl.ds(s, 1), :]
        edge = jnp.zeros((8, D), F32)
        for k in range(2):
            r.hidden[k, 0:8, :] = edge
            r.hidden[k, FRAMES + 8 : FRAMES + 16, :] = edge

        def embed(k):
            at = span(k * T, T)
            expand = expansion(start, stop, k * T, T)
            r.expand[at, :] = expand
            hot = hot_columns(r.pitch_bins[pl.ds(s, 1), at], count, k * T, T)
            r.hot[:, at] = hot
            frames = dot(expand, r.encoded_high[...]) + dot(expand, r.encoded_low[...])
            r.hidden[0, tile_rows(k, 0, 8), :] = frames
            pitched = frames + dot_tn(hot, r.pitch_table[...])
            r.hidden[1, tile_rows(k, 0, 8), :] = pitched

        each(FRAMES // T, embed)

        def keep(r0, size):
            return (iota((size, 1), 0) + r0 < count).astype(F32)

        def keep_row(r0, size):
            return (iota((1, size), 1) + r0 < count).astype(F32)

        def both(k):
            line = pl.ds(k * sequences + s, 1)
            predict(
                r, k + 1, FRAMES, keep, keep_row, r.hidden.at[k],
                r.cot_frames.at[line], r.frame_preds.at[line],
            )

        each(2, both)
        high, low = halves(r.hidden[1, 8 : FRAMES + 8, :])
        r.a_table[...] += dot(r.hot[...], high) + dot(r.hot[...], low)
        high, low = halves(r.hidden[0, 8 : FRAMES + 8, :] + r.hidden[1, 8 : FRAMES + 8, :])
        dencoded = dot_tn(r.expand[...], high) + dot_tn(r.expand[...], low)
        r.dencoded[s] = r.dencoded[s] + dencoded[0:PHONES]

    each(sequences, one)
    for p in range(3):
        for k in range(2):
            at = (2 * p + k) * 3 * D
            r.pack[:, at : at + 3 * D] = r.a_conv[p, k].astype(BF16)
    rows = jnp.concatenate([r.a_vec[p] for p in range(3)] + [jnp.zeros((104, D), F32)], axis=0)
    r.pack[:, AT_VECTORS:AT_TABLES] = rows.T.astype(BF16)
    r.pack[:, AT_TABLES : AT_TABLES + BINS] = r.a_table[...].T.astype(BF16)


def predictors_branch(sequences):
    return (
        functools.partial(predictor_kernel, sequences),
        names(frames=1, counts=1, encoded=1, durations=1, pitch_bins=1, convs=1, scales=1,
              shifts=1, readouts=1, pitch_table=1, cot_duration=1, cot_frames=1),
        names(duration_pred=1, frame_preds=1, dencoded=1, pack=1),
        dict(
            a_conv=pltpu.VMEM((3, 2, D, 3 * D), F32),
            a_vec=pltpu.VMEM((3, 8, D), F32),
            a_table=pltpu.VMEM((BINS, D), F32),
            durations_pad=pltpu.VMEM((8, 256), jnp.int32),
            start=pltpu.VMEM((8, 256), jnp.int32),
            stop=pltpu.VMEM((8, 256), jnp.int32),
            encoded_high=pltpu.VMEM((256, D), BF16),
            encoded_low=pltpu.VMEM((256, D), BF16),
            expand=pltpu.VMEM((FRAMES, 256), BF16),
            hot=pltpu.VMEM((BINS, FRAMES), BF16),
            hidden=pltpu.VMEM((2, FRAMES + 16, D), F32),
            after=pltpu.VMEM((FRAMES + 16, D), F32),
            dafter=pltpu.VMEM((FRAMES + 16, D), F32),
            cols_a=pltpu.VMEM((FRAMES, 3 * D), BF16),
            cols_b=pltpu.VMEM((FRAMES, 3 * D), BF16),
            slope_a=pltpu.VMEM((FRAMES, D), F32),
            norm_a=pltpu.VMEM((FRAMES, D), F32),
            rstd_a=pltpu.VMEM((FRAMES, 1), F32),
            grad_a=pltpu.VMEM((FRAMES, D), BF16),
            grad_b=pltpu.VMEM((FRAMES, D), BF16),
            dcols3=pltpu.VMEM((T + 32, 3 * D), F32),
        ),
    )


def swapped(array):
    return lax.ppermute(array, SECTION, [(0, 1), (1, 0)])


def scattered_anyhow(arrays):
    ways = lax.axis_size(DP)
    shares = [a.shape[0] // ways for a in arrays]
    flat = jnp.concatenate([a.reshape(ways, -1) for a in arrays], axis=1)
    flat = lax.psum_scatter(flat, DP, scatter_dimension=0, tiled=True)[0]
    out, at = [], 0
    for a, share in zip(arrays, shares):
        size = share * a.shape[1]
        out.append(flat[at : at + size].reshape(share, a.shape[1]).astype(F32))
        at += size
    return out


def scatter_kernel(steps, cuts, count, lists, trades, *refs):
    n, m = len(cuts), len(trades)
    given = max(m - 1, 0)
    sources, refs = refs[:count], refs[count:]
    traded, refs = refs[:given], refs[given:]
    outs, refs = refs[:count], refs[count:]
    arrived, refs = refs[:m], refs[m:]
    mine, landed = refs[:n], refs[n : n * (1 + steps)]
    load_sem, send_sem, recv_sem, *rest = refs[n * (1 + steps) :]
    if m:
        rounded, trade_send, trade_recv = rest
        traded = traded + (rounded,)
    me = lax.axis_index(DP)
    bits = [lax.rem(lax.div(me, 1 << k), 2) for k in range(steps)]
    partners = [me + (1 << k) * (1 - 2 * bits[k]) for k in range(steps)]
    def trade(i):
        return pltpu.make_async_remote_copy(
            src_ref=traded[i],
            dst_ref=arrived[i],
            send_sem=trade_send.at[i],
            recv_sem=trade_recv.at[i],
            device_id={SECTION: 1 - lax.axis_index(SECTION)},
            device_id_type=pl.DeviceIdType.MESH,
        )

    def every(k):
        return (slice(None),) * (steps - 1 - k)

    def source(i, bit):
        array, first, size = cuts[i]
        return sources[array].at[every(0) + (bit, slice(None), pl.ds(first, size))]

    def load(i):
        return pltpu.make_async_copy(source(i, bits[0]), mine[i], load_sem.at[i])

    def copy(i, k):
        if k == 0:
            out = source(i, 1 - bits[0])
        else:
            out = landed[i * steps + k - 1].at[every(k) + (1 - bits[k],)]
        return pltpu.make_async_remote_copy(
            src_ref=out,
            dst_ref=landed[i * steps + k],
            send_sem=send_sem.at[i, k],
            recv_sem=recv_sem.at[i, k],
            device_id={DP: partners[k]},
            device_id_type=pl.DeviceIdType.MESH,
        )

    def finish(i, k):
        copy(i, k).wait_recv()
        if k == 0:
            load(i).wait()
        there = landed[i * steps + k]
        for index in itertools.product(range(2), repeat=steps - 1 - k):
            if k == 0:
                stayed = mine[i][index]
            else:
                stayed = landed[i * steps + k - 1][index + (bits[k],)]
            total = there[index].astype(F32) + stayed.astype(F32)
            if k == steps - 1:
                array, first, size = cuts[i]
                outs[array][:, first : first + size] = total
            else:
                there[index] = total.astype(BF16)
        if k < steps - 1:
            copy(i, k + 1).start()

    def begin(i):
        copy(i, 0).start()
        load(i).start()

    def run(section, chosen):
        barrier = pltpu.get_barrier_semaphore()
        for partner in partners:
            pl.semaphore_signal(
                barrier, inc=1, device_id={DP: partner}, device_id_type=pl.DeviceIdType.MESH
            )
        if m:
            pl.semaphore_signal(
                barrier,
                inc=1,
                device_id={SECTION: 1 - lax.axis_index(SECTION)},
                device_id_type=pl.DeviceIdType.MESH,
            )
        pl.semaphore_wait(barrier, steps + (1 if m else 0))
        size = len(chosen)
        for i in range(given):
            if trades[i] == section:
                trade(i).start()
        last = [x for x, i in enumerate(chosen) if cuts[i][0] == count - 1]
        for turn in range(-AHEAD, size + steps - 1):
            if turn + AHEAD < size:
                begin(chosen[turn + AHEAD])
            for k in range(steps):
                at = turn - k
                if 0 <= at < size:
                    finish(chosen[at], k)
                    if m and trades[-1] == section and k == steps - 1 and at == last[-1]:
                        rounded[...] = outs[count - 1][...].astype(BF16)
                        trade(m - 1).start()
        for i in chosen:
            for k in range(steps):
                copy(i, k).wait_send()
        for i in range(m):
            if trades[i] == section:
                trade(i).wait_send()
            else:
                trade(i).wait_recv()

    for section, chosen in enumerate(lists):
        if chosen:
            here = (lax.axis_index(SECTION) == section).astype(jnp.int32)
            each(here, functools.partial(one_time, run, section, chosen))


def one_time(run, section, chosen, _):
    run(section, chosen)


def scattered(arrays, name, collective, width, parts, traded=(), trades=()):
    ways = lax.axis_size(DP)
    steps = ways.bit_length() - 1
    if ways != 1 << steps or any(a.shape[0] // ways % 16 for a in arrays):
        sums = scattered_anyhow(arrays)
        traded = [*traded, sums[-1].astype(BF16)] if trades else []
        return sums + [
            lax.ppermute(a, SECTION, [(s, 1 - s)]) for a, s in zip(traded, trades)
        ]
    shares = [a.shape[0] // ways for a in arrays]
    cuts = [
        (k, at, size)
        for k, a in enumerate(arrays)
        for at, size in pieces(a.shape[1], width if a.shape[0] > 1024 else 768)
    ]
    lists = [[i for k in part for i, cut in enumerate(cuts) if cut[0] == k] for part in parts]
    landed = [
        pltpu.VMEM((2,) * (steps - 1 - k) + (shares[array], size), BF16)
        for array, _, size in cuts
        for k in range(steps)
    ]
    mine = [pltpu.VMEM((2,) * (steps - 1) + (shares[array], size), BF16) for array, _, size in cuts]
    scratch = [
        *mine,
        *landed,
        pltpu.SemaphoreType.DMA((len(cuts),)),
        pltpu.SemaphoreType.DMA((len(cuts), steps)),
        pltpu.SemaphoreType.DMA((len(cuts), steps)),
    ]
    outs = [jax.ShapeDtypeStruct((share, a.shape[1]), F32) for share, a in zip(shares, arrays)]
    far, near = pl.BlockSpec(memory_space=pl.ANY), pl.BlockSpec(memory_space=pltpu.VMEM)
    out_specs = [near] * len(outs)
    if trades:
        sums = jax.ShapeDtypeStruct(outs[-1].shape, BF16)
        scratch.append(pltpu.VMEM(sums.shape, BF16))
        scratch += [pltpu.SemaphoreType.DMA((len(trades),))] * 2
        outs += [jax.ShapeDtypeStruct(a.shape, a.dtype) for a in traded] + [sums]
        out_specs += [far] * len(traded) + [near]
    return pl.pallas_call(
        functools.partial(scatter_kernel, steps, cuts, len(arrays), lists, tuple(trades)),
        name=name,
        in_specs=[far] * (len(arrays) + len(traded)),
        out_specs=out_specs,
        out_shape=outs,
        scratch_shapes=scratch,
        compiler_params=pltpu.CompilerParams(
            collective_id=collective, has_side_effects=True, vmem_limit_bytes=60 * 2**20
        ),
    )(
        *[a.reshape((2,) * steps + (share, a.shape[1])) for share, a in zip(shares, arrays)],
        *traded,
    )


def body(phonemes, phone_lengths, durations, pitch_bins, energy_bins, joint_weight, output_weight,
         widen_weight, narrow_weight, block_scales, block_shifts, predictor_convs,
         predictor_scales, predictor_shifts, predictor_outputs, pitch_table, energy_table,
         mel_weight, mel_cotangent, duration_cotangent, pitch_cotangent, energy_cotangent):
    first = lax.axis_index(SECTION) == 0
    n = phonemes.shape[0]
    frames = jnp.sum(durations, axis=1)
    block_weights = (joint_weight[0], output_weight[0], widen_weight[0], narrow_weight[0],
                     block_scales[0], block_shifts[0])
    weights = dict(zip(W_NAMES, block_weights))
    cot_duration = jnp.pad(duration_cotangent, ((0, 0), (0, SLOT - PHONES))).reshape(1, n * SLOT)
    cot_frames = jnp.concatenate([pitch_cotangent, energy_cotangent])
    encoded, encoded_lo = section_call(
        "encoder_forward",
        dict(counts=phone_lengths, phonemes=phonemes, **weights),
        dict(encoded=((n, PHONES, D), F32), encoded_lo=((n, PHONES, D), BF16)),
        (encoder_forward_branch(), None),
        smem=names(counts=1),
    )
    arrived = lax.ppermute(encoded_lo, SECTION, [(0, 1)])
    duration, preds, mel_own, mel_away, dencoded, dsent, *grads, pack, pack_far = section_call(
        "predictors_or_decoder",
        dict(
            frames=frames,
            counts=phone_lengths,
            encoded=encoded,
            arrived=arrived,
            durations=durations,
            pitch_bins=pitch_bins,
            energy_bins=energy_bins,
            convs=predictor_convs,
            scales=predictor_scales,
            shifts=predictor_shifts,
            readouts=predictor_outputs,
            pitch_table=pitch_table,
            energy_table=energy_table,
            mel_turned=mel_weight.T,
            mel_cotangent=mel_cotangent.transpose(0, 2, 1),
            cot_duration=cot_duration,
            cot_frames=cot_frames,
            **weights,
        ),
        dict(
            duration_pred=((1, n * SLOT), F32),
            frame_preds=((2 * n, FRAMES), F32),
            mel_own=((n, MELS, FRAMES // 2), F32),
            mel_away=((n, MELS, FRAMES // 2), BF16),
            dencoded=((n, PHONES, D), F32),
            dsent=((n, PHONES, D), BF16),
            **GRADS,
            pack=((D, NEAR_PACK), BF16),
            pack_far=((D, PACK - AT_TABLES), BF16),
        ),
        (predictors_branch(n), decoder_branch(n)),
        smem=names(frames=1, counts=1),
    )
    (pack,) = scattered([pack], "pack_sums", 1, 768, ((0,), ()))
    pack, dsent = lax.optimization_barrier((pack, dsent))
    returned = lax.ppermute(dsent, SECTION, [(1, 0)])
    input_own, input_away, *grads = section_call(
        "encoder_backward",
        dict(
            counts=phone_lengths,
            phonemes=phonemes,
            grad_near=dencoded,
            grad_far=returned,
            **weights,
            **dict(zip(G_NAMES, grads)),
        ),
        dict(
            input_own=((n, PHONES // 2, D), F32),
            input_away=((n, PHONES // 2, D), BF16),
            **GRADS,
        ),
        (encoder_backward_branch(), None),
        smem=names(counts=1),
        kept=G_NAMES,
    )
    sums = dict(zip(G_NAMES, grads))
    order = names(g_widen=1, g_narrow=1, g_joint=1, g_output=1, g_vec=1)
    half, some = FRAMES // 2, PHONES // 2
    duration = duration.reshape(n, SLOT)[:, :PHONES]
    small = jnp.concatenate(
        [
            preds[:, half:],
            jnp.pad(duration[:, some:], ((0, 16 - 3 * n), (0, half - some))),
        ]
    ).astype(BF16)
    sums = scattered(
        [sums[n] for n in order] + [pack_far],
        "block_sums",
        2,
        256,
        (range(5), (5, 0, 1, 2, 3, 4)),
        (pack.astype(BF16), small, input_away, mel_away),
        (0, 0, 0, 1, 1),
    )
    near_pack, small, input_away, mel_away, far_pack = sums[6:]
    own = dict(zip(order, sums))
    return assembled(
        n,
        sums[0].shape[0],
        dict(
            **own,
            pack=pack,
            pack_far=sums[5],
            duration=duration,
            preds=preds,
            mel_own=mel_own,
            input_own=input_own,
            near_pack=near_pack,
            small=small,
            input_away=input_away,
            mel_away=mel_away,
            far_pack=far_pack,
        ),
    )


def assemble_kernel(n, ins, outs, *refs):
    far, refs = refs[: len(ins)], refs[len(ins) :]
    outs_refs, (*near, sem) = refs[: len(outs)], refs[len(outs) :]
    copies = [
        pltpu.make_async_copy(a, b, sem.at[k]) for k, (a, b) in enumerate(zip(far, near))
    ]
    for copy in copies:
        copy.start()
    for copy in copies:
        copy.wait()
    r = Refs(ins + outs, [*near, *outs_refs])
    first = lax.axis_index(SECTION) == 0
    half, some = FRAMES // 2, PHONES // 2

    def choose(near, far):
        return jnp.where(first, near.astype(F32), far.astype(F32))

    for s in range(n):
        r.o_mel[s] = choose(r.mel_away[s], r.mel_own[s])
        r.o_input[s] = choose(r.input_own[s], r.input_away[s])
    preds = choose(r.preds[:, 0:half], r.small[0 : 2 * n, :])
    r.o_pitch[...] = preds[0:n]
    r.o_energy[...] = preds[n : 2 * n]
    r.o_duration[...] = choose(r.duration[:, 0:some], r.small[2 * n : 3 * n, 0:some])
    r.o_joint[0] = r.g_joint[...]
    r.o_output[0] = r.g_output[...]
    r.o_widen[0] = r.g_widen[...]
    r.o_narrow[0] = r.g_narrow[...]
    share = r.pack.shape[0]
    block_vec = r.g_vec[...].T
    vec = choose(r.pack[:, AT_VECTORS:AT_TABLES], r.near_pack[:, AT_VECTORS:AT_TABLES]).T
    for k in range(2):
        r.o_block_scales[0, k : k + 1, :] = block_vec[2 * k : 2 * k + 1, 0:share]
        r.o_block_shifts[0, k : k + 1, :] = block_vec[2 * k + 1 : 2 * k + 2, 0:share]
        for p in range(3):
            at = (2 * p + k) * 3 * D
            r.o_convs[p, k] = choose(
                r.pack[:, at : at + 3 * D], r.near_pack[:, at : at + 3 * D]
            )
            row = 8 * p + 2 * k
            r.o_scales[p, k : k + 1, :] = vec[row : row + 1, 0:share]
            r.o_shifts[p, k : k + 1, :] = vec[row + 1 : row + 2, 0:share]
    for p in range(3):
        r.o_readouts[p : p + 1, :] = vec[8 * p + 4 : 8 * p + 5, 0:share]
    near = choose(r.pack[:, AT_TABLES:], r.near_pack[:, AT_TABLES:])
    far = choose(r.far_pack[...], r.pack_far[...])
    r.o_pitch_table[...] = near + far[:, 0:BINS]
    r.o_energy_table[...] = far[:, BINS : 2 * BINS]
    r.o_mel_weight[...] = far[:, 2 * BINS : 2 * BINS + MELS]


def assembled(n, widen_rows, ins):
    share = ins[names(pack=1)[0]].shape[0]
    narrow_rows = FF * share // D
    outs = dict(
        o_mel=(n, MELS, FRAMES // 2),
        o_duration=(n, PHONES // 2),
        o_pitch=(n, FRAMES // 2),
        o_energy=(n, FRAMES // 2),
        o_input=(n, PHONES // 2, D),
        o_joint=(1, share, 3 * D),
        o_output=(1, share, D),
        o_widen=(1, widen_rows, FF),
        o_narrow=(1, narrow_rows, D),
        o_block_scales=(1, 2, share),
        o_block_shifts=(1, 2, share),
        o_convs=(3, 2, share, 3 * D),
        o_scales=(3, 2, share),
        o_shifts=(3, 2, share),
        o_readouts=(3, share),
        o_pitch_table=(share, BINS),
        o_energy_table=(share, BINS),
        o_mel_weight=(share, MELS),
    )
    whole = pl.BlockSpec(memory_space=pltpu.VMEM)
    results = pl.pallas_call(
        functools.partial(assemble_kernel, n, list(ins), list(outs)),
        name="assemble",
        in_specs=[pl.BlockSpec(memory_space=pl.ANY)] * len(ins),
        out_specs=[whole] * len(outs),
        out_shape=[jax.ShapeDtypeStruct(shape, F32) for shape in outs.values()],
        scratch_shapes=[
            *[pltpu.VMEM(a.shape, a.dtype) for a in ins.values()],
            pltpu.SemaphoreType.DMA((len(ins),)),
        ],
        compiler_params=pltpu.CompilerParams(vmem_limit_bytes=61 * 2**20),
    )(*ins.values())
    results = list(results)
    results[0] = results[0].transpose(0, 2, 1)
    results[11] = results[11].transpose(0, 1, 3, 2)
    results[15], results[16] = results[15].T, results[16].T
    return tuple(results)


def solution(mesh):
    halves_of_rows = P(DP, SECTION)
    row, rows, blocks = P(DP), P(DP, None), P(DP, None, None)
    table, block_sums = P(SECTION, None, None), P(SECTION, DP, None)
    block_vectors, vectors, columns = P(SECTION, None, DP), P(None, None, DP), P(None, DP)
    return jax.shard_map(
        body,
        mesh=mesh,
        in_specs=(blocks, row, rows, rows, rows) + (table,) * 6 + (P(),) * 7
        + (blocks, rows, rows, rows),
        out_specs=(
            P(DP, SECTION, None),
            halves_of_rows,
            halves_of_rows,
            halves_of_rows,
            P(DP, SECTION, None),
            *(block_sums,) * 4,
            block_vectors,
            block_vectors,
            P(None, None, None, DP),
            vectors,
            vectors,
            columns,
            columns,
            columns,
            rows,
        ),
        check_vma=False,
    )
```

```python
import functools
import itertools
import math

import jax
import jax.numpy as jnp
from jax import lax
from jax.experimental import pallas as pl
from jax.experimental.pallas import tpu as pltpu
from jax.sharding import PartitionSpec as P

D = 256
HEAD = 128
FF = 1024
BINS = 256
MELS = 80
TAPS = 9
PHONES = 160
FRAMES = 1024
SLOT = 192
WIDE = TAPS * D
EPS = 1e-5
AT_VECTORS = 6 * 3 * D
AT_TABLES = AT_VECTORS + 128
AT_MEL = AT_TABLES + 2 * BINS
PACK = AT_MEL + 128
NEAR_PACK = AT_TABLES + BINS
C1 = math.sqrt(2.0 / math.pi)
C2 = C1 * 0.044715
SCALE = HEAD**-0.5
SECTION = "section"
DP = "dp"
LOG2E = math.log2(math.e)
F32 = jnp.float32
BF16 = jnp.bfloat16


def names(**kept):
    return tuple(kept)


def dot(a, b):
    return jnp.dot(a, b, preferred_element_type=F32)


def dot_nt(a, b):
    return lax.dot_general(a, b, (((1,), (1,)), ((), ())), preferred_element_type=F32)


def dot_tn(a, b):
    return lax.dot_general(a, b, (((0,), (0,)), ((), ())), preferred_element_type=F32)


def iota(shape, dim):
    return lax.broadcasted_iota(jnp.int32, shape, dim)


def gelu_pair(x):
    x2 = x * x
    h = 0.5 + 0.5 * jnp.tanh(x * (C1 + C2 * x2))
    value = x * h
    slope = h + value * (1.0 - h) * (2.0 * C1 + 6.0 * C2 * x2)
    return value, slope


def normed(r):
    mean = jnp.mean(r, axis=-1, keepdims=True)
    centred = r - mean
    rstd = lax.rsqrt(jnp.mean(centred * centred, axis=-1, keepdims=True) + EPS)
    return centred * rstd, rstd


def norm_back(t, n, rstd):
    return (
        t - jnp.mean(t, axis=-1, keepdims=True) - n * jnp.mean(t * n, axis=-1, keepdims=True)
    ) * rstd


def column_sum(x):
    return jnp.sum(x, axis=0, keepdims=True)


def aligned(i, size):
    return pl.ds(pl.multiple_of(i * size, size), size)


def each(count, body):
    def step(i, carry):
        body(i)
        return carry

    lax.fori_loop(0, count, step, 0)


class Layout:
    def __init__(self, segments, span, query):
        self.segments, self.span, self.query = segments, span, query
        self.rows = segments * span
        self.fewest = span // 2


ENC = Layout(4, SLOT, SLOT)
DEC = Layout(1, FRAMES, 256)
T = 256
AHEAD = 2


def pieces(length, size):
    return [(at, min(size, length - at)) for at in range(0, length, size)]


def block_scratch(layout, backward):
    L, S, n = layout.rows, layout.span, layout.segments
    shapes = dict(
        h_lo=pltpu.VMEM((L, D), BF16),
        joint=pltpu.VMEM((L, 3 * D), BF16),
        jointT=pltpu.VMEM((n, 3 * D, S), BF16),
        mixedT=pltpu.VMEM((n, D, S), BF16),
        first=pltpu.VMEM((L + 16, D), F32),
        cols=pltpu.VMEM((L, WIDE), BF16),
        slope=pltpu.VMEM((L, FF), F32),
        wide=pltpu.VMEM((2, T, D), F32),
        second=pltpu.VMEM((L, D), F32),
        widen=pltpu.VMEM((WIDE, FF), BF16),
        narrow=pltpu.VMEM((FF, D), BF16),
        sem=pltpu.SemaphoreType.DMA((6,)),
    )
    if backward:
        shapes.update(
            expo=pltpu.VMEM((n, 2, S, S), BF16),
            rinv=pltpu.VMEM((n, 2, 8, S), F32),
            n1=pltpu.VMEM((L, D), F32),
            r1=pltpu.VMEM((L, 1), F32),
            act=pltpu.VMEM((L, FF), BF16),
            spare=pltpu.VMEM((WIDE - 2 * L, FF), BF16),
            dnar=pltpu.VMEM((max(L, FF), D), BF16),
            dwid=pltpu.VMEM((L, FF), BF16),
            dcols=pltpu.VMEM((T + 32, WIDE), F32),
            dfirst=pltpu.VMEM((L + 16, D), F32),
            datt=pltpu.VMEM((L, D), BF16),
            dmixT=pltpu.VMEM((n, D, S), BF16),
            inner=pltpu.VMEM((n, 2, 8, S), F32),
            djointT=pltpu.VMEM((n, 3 * D, S), BF16),
            joint_turned=pltpu.VMEM((3 * D, D), BF16),
            a_joint=pltpu.VMEM((3 * D, D), F32),
            a_output=pltpu.VMEM((D, D), F32),
            a_widen=pltpu.VMEM((WIDE, FF), F32),
            a_narrow=pltpu.VMEM((FF, D), F32),
            a_vec=pltpu.VMEM((8, D), F32),
        )
    return shapes


def start_block(layout, b):
    edge = jnp.zeros((8, D), F32)
    b.first[0:8, :] = edge
    b.first[layout.rows + 8 : layout.rows + 16, :] = edge


def zero_accumulators(b, w):
    b.joint_turned[...] = w.joint[...].T
    b.a_joint[...] = jnp.zeros_like(b.a_joint)
    b.a_output[...] = jnp.zeros_like(b.a_output)
    b.a_narrow[...] = jnp.zeros_like(b.a_narrow)
    b.a_vec[...] = jnp.zeros_like(b.a_vec)

    def body(t, _):
        b.a_widen[aligned(t, D), :] = jnp.zeros((D, FF), F32)
        return 0

    lax.fori_loop(0, TAPS, body, 0)
    edge = jnp.zeros((16, WIDE), F32)
    b.dcols[0:16, :] = edge


def heads(h):
    return tuple(slice(k * D + h * HEAD, k * D + (h + 1) * HEAD) for k in range(3))


def span(start, size):
    if isinstance(start, int):
        return slice(start, start + size)
    return pl.ds(pl.multiple_of(start, math.gcd(size, 256)), size)


def tile_rows(k, extra=0, first=0):
    return pl.ds(pl.multiple_of(k * T + first, 8), T + extra)


def attention_forward(layout, b, w, counts, length):
    S, save = layout.span, hasattr(b, "expo")
    blocks = [(s, at, q) for s in range(layout.segments) for at, q in pieces(length, layout.query)]
    for s, at, q in blocks:
        rows = slice(s * S + at, s * S + at + q)
        value = dot(b.h_lo[rows, :], w.joint[...]).astype(BF16)
        b.joint[rows, :] = value
        b.jointT[s, :, at : at + q] = value.T
    chunks = pieces(length, D)
    items = [block + (h,) for block in blocks for h in range(2)]

    def score(i):
        s, at, q, h = items[i]
        query_at, key_at, _ = heads(h)
        side = slice((i % 2) * D, (i % 2) * D + q)
        top = None
        for c, size in chunks:
            scores = dot(
                b.joint[s * S + c : s * S + c + size, key_at], b.jointT[s, query_at, at : at + q]
            )
            if c + size > layout.fewest:
                scores = jnp.where(iota((size, q), 0) + c < counts[s], scores, -1e30)
            b.slope[c : c + size, side] = scores
            part = jnp.max(scores.reshape(size // 8, 8, q), axis=0)
            top = part if top is None else jnp.maximum(top, part)
        return jnp.max(top, axis=0, keepdims=True)

    tops = {0: score(0)}
    for i, (s, at, q, h) in enumerate(items):
        if i + 1 < len(items):
            tops[i + 1] = score(i + 1)
        query_at, _, value_at = heads(h)
        side = slice((i % 2) * D, (i % 2) * D + q)
        sums = mixed = None
        for c, size in chunks:
            expo = jnp.exp2((b.slope[c : c + size, side] - tops[i]) * (SCALE * LOG2E))
            part = jnp.sum(expo.reshape(size // 8, 8, q), axis=0)
            sums = part if sums is None else sums + part
            expo = expo.astype(BF16)
            if save:
                b.expo[s, h, c : c + size, at : at + q] = expo
            part = dot(b.jointT[s, value_at, c : c + size], expo)
            mixed = part if mixed is None else mixed + part
        rinv = 1.0 / column_sum(sums)
        b.mixedT[s, query_at, at : at + q] = (mixed * rinv).astype(BF16)
        if save:
            b.rinv[s, h, :, at : at + q] = jnp.broadcast_to(rinv, (8, q))
    for s, at, q in blocks:
        r0 = s * S + at
        attended = dot_tn(b.mixedT[s, :, at : at + q], w.output[...])
        n, rstd = normed(b.h_lo[r0 : r0 + q, :].astype(F32) + attended)
        keep = (iota((q, 1), 0) + at < counts[s]).astype(F32)
        b.first[r0 + 8 : r0 + 8 + q, :] = (n * w.scales[0:1, :] + w.shifts[0:1, :]) * keep
        if save:
            b.n1[r0 : r0 + q, :] = n
            b.r1[r0 : r0 + q, :] = rstd


def ffn_forward(b, w, length):
    save = hasattr(b, "expo")
    tiles = pieces(length, T)
    items = [(k, j) for k in range(len(tiles)) for j in range(4)]

    def unfold(k):
        r0, size = tiles[k]
        v = b.first[r0 : r0 + size + 16, :]
        for t in range(TAPS):
            b.cols[r0 : r0 + size, t * D : (t + 1) * D] = v[4 + t : 4 + t + size].astype(BF16)

    def widen(i):
        k, j = items[i]
        r0, size = tiles[k]
        b.wide[i % 2, 0:size, :] = dot(b.cols[r0 : r0 + size, :], b.widen[:, j * D : (j + 1) * D])

    unfold(0)
    widen(0)
    for i, (k, j) in enumerate(items):
        if j == 1 and k + 1 < len(tiles):
            unfold(k + 1)
        if i + 1 < len(items):
            widen(i + 1)
        r0, size = tiles[k]
        rows, at = slice(r0, r0 + size), slice(j * D, (j + 1) * D)
        value, slope = gelu_pair(b.wide[i % 2, 0:size, :])
        value = value.astype(BF16)
        if save:
            b.act[rows, at] = value
            b.slope[rows, at] = slope
        narrowed = dot(value, b.narrow[at, :])
        before = b.second[rows, :] if j else b.first[r0 + 8 : r0 + 8 + size, :]
        b.second[rows, :] = before + narrowed


def ffn_backward(b, w, length):
    b.dfirst[0 : length + 16, :] = jnp.zeros((length + 16, D), F32)
    for r0, size in pieces(length, T):
        rows = slice(r0, r0 + size)
        b.dcols[16 + size : 32 + size, :] = jnp.zeros((16, WIDE), F32)
        for j in range(4):
            at = slice(j * D, (j + 1) * D)
            b.dwid[rows, at] = (
                dot_nt(b.dnar[rows, :], b.narrow[at, :]) * b.slope[rows, at]
            ).astype(BF16)
        for t in range(TAPS):
            at = slice(t * D, (t + 1) * D)
            b.dcols[16 : 16 + size, at] = dot_nt(b.dwid[rows, :], b.widen[at, :])
        total = b.dcols[12 : 28 + size, 0:D]
        for t in range(1, TAPS):
            total = total + b.dcols[12 - t : 28 - t + size, t * D : (t + 1) * D]
        b.dfirst[r0 : r0 + size + 16, :] += total
        b.dfirst[r0 + 8 : r0 + 8 + size, :] += b.second[rows, :]


def ffn_weight_grads(b, length):
    for t in range(3):
        at = slice(t * 3 * D, (t + 1) * 3 * D)
        b.a_widen[at, :] += dot_tn(b.cols[0:length, at], b.dwid[0:length, :])
    b.a_narrow[...] += dot_tn(b.act[0:length, :], b.dnar[0:length, :])


def attention_backward(layout, b, w, counts, length, finish):
    S = layout.span
    blocks = [(s, at, q) for s in range(layout.segments) for at, q in pieces(length, layout.query)]
    chunks = pieces(length, D)
    for s, at, q in blocks:
        r0 = s * S + at
        rows, pad_rows, lanes = slice(r0, r0 + q), slice(r0 + 8, r0 + 8 + q), slice(at, at + q)
        keep = (iota((q, 1), 0) + at < counts[s]).astype(F32)
        dy = b.dfirst[pad_rows, :] * keep
        n = b.n1[rows, :]
        b.a_vec[0:1, :] += column_sum(dy * n)
        b.a_vec[1:2, :] += column_sum(dy)
        dsum = norm_back(dy * w.scales[0:1, :], n, b.r1[rows, :])
        b.dfirst[pad_rows, :] = dsum
        datt = dsum.astype(BF16)
        b.datt[rows, :] = datt
        dmix = dot_nt(w.output[...], datt)
        for h in range(2):
            head = heads(h)[0]
            part = (dmix[head, :] * b.rinv[s, h, 0:1, lanes]).astype(BF16)
            b.dmixT[s, head, lanes] = part
            inner = column_sum(part.astype(F32) * b.mixedT[s, head, lanes].astype(F32))
            b.inner[s, h, :, lanes] = jnp.broadcast_to(inner, (8, q))
    items = [block + (h,) for block in blocks for h in range(2)]

    def score(i):
        s, at, q, h = items[i]
        side = slice((i % 2) * D, (i % 2) * D + q)
        b.slope[0:length, side] = dot(
            b.joint[s * S : s * S + length, heads(h)[2]], b.dmixT[s, heads(h)[0], at : at + q]
        )

    score(0)
    for i, (s, at, q, h) in enumerate(items):
        if i + 1 < len(items):
            score(i + 1)
        query_at, key_at, _ = heads(h)
        lanes, side = slice(at, at + q), slice((i % 2) * D, (i % 2) * D + q)
        dquery = None
        for c, size in chunks:
            expo = b.expo[s, h, c : c + size, lanes].astype(F32)
            ds = expo * (b.slope[c : c + size, side] - b.inner[s, h, 0:1, lanes])
            ds = ds.astype(BF16)
            part = dot(b.jointT[s, key_at, c : c + size], ds)
            dquery = part if dquery is None else dquery + part
            b.cols[s * S + at : s * S + at + q, h * FRAMES + c : h * FRAMES + c + size] = ds.T
        b.djointT[s, query_at, lanes] = (dquery * SCALE).astype(BF16)
    for s in range(layout.segments):
        rows = slice(s * S, s * S + length)
        for h in range(2):
            query_at, key_at, value_at = heads(h)
            for c, size in chunks:
                lanes = slice(c, c + size)
                dkey = dot(
                    b.jointT[s, query_at, 0:length],
                    b.cols[rows, h * FRAMES + c : h * FRAMES + c + size],
                )
                b.djointT[s, key_at, lanes] = (dkey * SCALE).astype(BF16)
                dvalue = dot_nt(b.dmixT[s, query_at, 0:length], b.expo[s, h, lanes, 0:length])
                b.djointT[s, value_at, lanes] = dvalue.astype(BF16)
        b.a_output[...] += dot(b.mixedT[s, :, 0:length], b.datt[rows, :])
        b.a_joint[...] += dot(b.djointT[s, :, 0:length], b.h_lo[rows, :])
    for s, at, q in blocks:
        dh = dot_tn(b.djointT[s, :, at : at + q], b.joint_turned[...])
        finish(s, at, q, dh + b.dfirst[s * S + at + 8 : s * S + at + 8 + q, :])


def second_norm_back(b, w, r0, size, dy, n, rstd):
    b.a_vec[2:3, :] += column_sum(dy * n)
    b.a_vec[3:4, :] += column_sum(dy)
    dsecond = norm_back(dy * w.scales[1:2, :], n, rstd)
    b.second[r0 : r0 + size, :] = dsecond
    b.dnar[r0 : r0 + size, :] = dsecond.astype(BF16)


class Refs:
    def __init__(self, names, refs):
        for name, ref in zip(names, refs):
            setattr(self, name, ref)


WEIGHTS = names(joint=1, output=1, widen_far=1, narrow_far=1, scales=1, shifts=1)
FAR = names(w_widen_far=1, w_narrow_far=1, g_widen=1, g_narrow=1)


def send_large_grads(b, o):
    b.dnar[0:FF, :] = b.a_narrow[...].astype(BF16)
    pltpu.make_async_copy(b.dnar.at[pl.ds(0, FF)], o.g_narrow, b.sem.at[2]).start()
    at = 0
    for k, (buffer, size) in enumerate(large_parts(b)):
        buffer[0:size, :] = b.a_widen[at : at + size, :].astype(BF16)
        pltpu.make_async_copy(
            buffer.at[pl.ds(0, size)], o.g_widen.at[pl.ds(at, size)], b.sem.at[3 + k]
        ).start()
        at += size


def large_parts(b):
    size = b.act.shape[0]
    left = WIDE - 2 * size
    return ((b.act, size), (b.dwid, size), (b.spare, left))


def store_block_grads(b, o):
    o.g_joint[...] = b.a_joint[...].T.astype(BF16)
    o.g_output[...] = b.a_output[...].astype(BF16)
    rows = jnp.concatenate([b.a_vec[...], jnp.zeros((120, D), F32)], axis=0)
    o.g_vec[...] = rows.T.astype(BF16)
    pltpu.make_async_copy(b.dnar.at[pl.ds(0, FF)], o.g_narrow, b.sem.at[2]).wait()
    at = 0
    for k, (buffer, size) in enumerate(large_parts(b)):
        pltpu.make_async_copy(
            buffer.at[pl.ds(0, size)], o.g_widen.at[pl.ds(at, size)], b.sem.at[3 + k]
        ).wait()
        at += size


def start_weights(b, w):
    pltpu.make_async_copy(w.widen_far, b.widen, b.sem.at[0]).start()
    pltpu.make_async_copy(w.narrow_far, b.narrow, b.sem.at[1]).start()


def wait_weights(b, w):
    pltpu.make_async_copy(w.widen_far, b.widen, b.sem.at[0]).wait()
    pltpu.make_async_copy(w.narrow_far, b.narrow, b.sem.at[1]).wait()


GRADS = dict(
    g_joint=((D, 3 * D), BF16),
    g_output=((D, D), BF16),
    g_widen=((WIDE, FF), BF16),
    g_narrow=((FF, D), BF16),
    g_vec=((D, 128), BF16),
)


def expansion(start, stop, first_row, size):
    row = iota((size, 256), 0) + first_row
    return ((row >= start) & (row < stop)).astype(F32).astype(BF16)


def hot_columns(bins, count, first_lane, size):
    live = iota((1, size), 1) + first_lane < count
    return ((iota((BINS, size), 0) == bins) & live).astype(F32).astype(BF16)


def span_ends(durations):
    upper = (iota((256, 256), 0) <= iota((256, 256), 1)).astype(F32).astype(BF16)
    return dot(durations.astype(F32).astype(BF16), upper).astype(jnp.int32)


def decoder_kernel(sequences, r):
    b, w, o = r, Refs(WEIGHTS, [getattr(r, "w_" + n) for n in WEIGHTS]), r
    layout = DEC
    start_weights(b, w)
    zero_accumulators(b, w)
    start_block(layout, b)
    r.a_mel[...] = jnp.zeros_like(r.a_mel)
    r.a_table[...] = jnp.zeros_like(r.a_table)
    r.durations_pad[...] = jnp.zeros_like(r.durations_pad)
    r.durations_pad[0:sequences, 0:PHONES] = r.durations[...]
    stop = span_ends(r.durations_pad[...])
    r.stop[...] = stop
    r.start[...] = stop - r.durations_pad[...]
    r.encoded_pad[...] = jnp.zeros_like(r.encoded_pad)

    def sequence(s, length):
        count = r.frames[s]
        counts = [count]
        r.encoded_pad[0:PHONES, :] = r.arrived[s]
        start, stop = r.start[pl.ds(s, 1), :], r.stop[pl.ds(s, 1), :]
        tiles = pieces(length, T)
        for r0, size in tiles:
            rows = slice(r0, r0 + size)
            expand = expansion(start, stop, r0, size)
            r.expand[rows, :] = expand
            hot_p = hot_columns(r.pitch_bins[pl.ds(s, 1), rows], count, r0, size)
            hot_e = hot_columns(r.energy_bins[pl.ds(s, 1), rows], count, r0, size)
            r.hot[0:BINS, rows] = hot_p
            r.hot[BINS:, rows] = hot_e
            adapted = dot(expand, r.encoded_pad[...])
            adapted = adapted + dot_tn(hot_p, r.pitch_table[...])
            adapted = adapted + dot_tn(hot_e, r.energy_table[...])
            b.h_lo[rows, :] = adapted.astype(BF16)
        attention_forward(layout, b, w, counts, length)
        b.first[length + 8 : length + 16, :] = jnp.zeros((8, D), F32)
        ffn_forward(b, w, length)
        for r0, size in tiles:
            rows = slice(r0, r0 + size)
            n, rstd = normed(b.second[rows, :])
            keep = (iota((size, 1), 0) + r0 < count).astype(F32)
            decoded = ((n * w.scales[1:2, :] + w.shifts[1:2, :]) * keep).astype(BF16)
            spectrum = dot_nt(r.mel_turned[...], decoded)
            if r0 < FRAMES // 2:
                o.mel_away[s, :, rows] = spectrum.astype(BF16)
            else:
                o.mel_own[s, :, r0 - FRAMES // 2 : r0 - FRAMES // 2 + size] = spectrum
            cotangent = r.mel_cotangent[s, :, rows]
            r.a_mel[...] += dot(cotangent, decoded)
            dy = dot_tn(cotangent, r.mel_turned[...]) * keep
            second_norm_back(b, w, r0, size, dy, n, rstd)
        ffn_backward(b, w, length)
        ffn_weight_grads(b, length)

        def finish(_, at, q, dh):
            b.datt[at : at + q, :] = dh.astype(BF16)

        attention_backward(layout, b, w, counts, length, finish)
        dadapted = b.datt[0:length, :]
        r.a_table[...] += dot(r.hot[:, 0:length], dadapted)
        o.dsent[s] = dot_tn(r.expand[0:length, :], dadapted)[0:PHONES].astype(BF16)

    def one(s):
        sequence(s, FRAMES)

    wait_weights(b, w)
    each(sequences, one)
    send_large_grads(b, o)
    store_block_grads(b, o)
    r.pack_far[:, 0 : 2 * BINS] = r.a_table[...].T.astype(BF16)
    r.pack_far[:, 2 * BINS :] = jnp.zeros((D, 128), BF16)
    r.pack_far[:, 2 * BINS : 2 * BINS + MELS] = r.a_mel[...].T.astype(BF16)


def section_call(name, inputs, outputs, branches, smem=(), kept=()):
    shapes = {n: (a.shape, a.dtype) for n, a in inputs.items()}

    def kernel(*refs):
        place = dict(zip(inputs, refs))
        target = dict(zip(outputs, refs[len(inputs) :]))

        def run(body, ins, outs, scratch):
            near_ins = [n for n in ins if n not in FAR and n not in smem]
            near_outs = [n for n in outs if n not in FAR]
            local = {n: pltpu.VMEM(*shapes[n]) for n in near_ins}
            local.update({n: pltpu.VMEM(*outputs[n]) for n in near_outs})
            local.update(scratch)
            local.update(
                sem_in=pltpu.SemaphoreType.DMA((len(near_ins),)),
                sem_out=pltpu.SemaphoreType.DMA((len(near_outs),)),
            )

            def scoped(*values):
                r = Refs(list(local), values)
                for n in ins:
                    if n not in near_ins:
                        setattr(r, n, place[n])
                for n in outs:
                    if n not in near_outs:
                        setattr(r, n, target[n])
                copies = [
                    pltpu.make_async_copy(place[n], getattr(r, n), r.sem_in.at[k])
                    for k, n in enumerate(near_ins)
                ]
                for copy in copies:
                    copy.start()
                for copy in copies:
                    copy.wait()
                body(r)
                copies = [
                    pltpu.make_async_copy(getattr(r, n), target[n], r.sem_out.at[k])
                    for k, n in enumerate(near_outs)
                ]
                for copy in copies:
                    copy.start()
                for copy in copies:
                    copy.wait()

            pl.run_scoped(scoped, *local.values())

        for section, branch in enumerate(branches):
            if branch is not None:
                here = (lax.axis_index(SECTION) == section).astype(jnp.int32)
                each(here, lambda _: run(*branch))

    index_in = list(inputs)
    return pl.pallas_call(
        kernel,
        name=name,
        in_specs=[
            pl.BlockSpec(memory_space=pltpu.SMEM if n in smem else pl.ANY) for n in inputs
        ],
        out_specs=[pl.BlockSpec(memory_space=pl.ANY)] * len(outputs),
        out_shape=[jax.ShapeDtypeStruct(*outputs[n]) for n in outputs],
        input_output_aliases={index_in.index(n): k for k, n in enumerate(outputs) if n in kept},
        compiler_params=pltpu.CompilerParams(vmem_limit_bytes=61 * 2**20),
    )(*inputs.values())


W_NAMES = tuple("w_" + n for n in WEIGHTS)
G_NAMES = tuple(GRADS)


def decoder_branch(sequences):
    scratch = dict(
        block_scratch(DEC, True),
        a_mel=pltpu.VMEM((MELS, D), F32),
        a_table=pltpu.VMEM((2 * BINS, D), F32),
        durations_pad=pltpu.VMEM((8, 256), jnp.int32),
        start=pltpu.VMEM((8, 256), jnp.int32),
        stop=pltpu.VMEM((8, 256), jnp.int32),
        encoded_pad=pltpu.VMEM((256, D), BF16),
        expand=pltpu.VMEM((FRAMES, 256), BF16),
        hot=pltpu.VMEM((2 * BINS, FRAMES), BF16),
    )
    ins = names(frames=1, arrived=1, durations=1, pitch_bins=1, energy_bins=1, pitch_table=1,
                energy_table=1, mel_turned=1, mel_cotangent=1)
    outs = names(mel_own=1, mel_away=1, dsent=1, pack_far=1)
    return functools.partial(decoder_kernel, sequences), ins + W_NAMES, outs + G_NAMES, scratch


def load_segments(b, phonemes):
    b.h_lo[...] = jnp.zeros_like(b.h_lo)
    for s in range(ENC.segments):
        b.h_lo[s * SLOT : s * SLOT + PHONES, :] = phonemes[s]


def slot_keep(counts, r0, size):
    row = iota((size, 1), 0) + r0
    kept = row < counts[0]
    for s in range(1, ENC.segments):
        kept = kept | ((row >= s * SLOT) & (row < s * SLOT + counts[s]))
    return kept.astype(F32)


def encoder_forward_kernel(r):
    b, w = r, Refs(WEIGHTS, [getattr(r, "w_" + n) for n in WEIGHTS])
    start_weights(b, w)
    counts = [r.counts[s] for s in range(ENC.segments)]
    start_block(ENC, b)
    load_segments(b, r.phonemes)
    attention_forward(ENC, b, w, counts, SLOT)
    wait_weights(b, w)
    ffn_forward(b, w, ENC.rows)
    for r0, size in pieces(ENC.rows, T):
        n, _ = normed(b.second[r0 : r0 + size, :])
        encoded = (n * w.scales[1:2, :] + w.shifts[1:2, :]) * slot_keep(counts, r0, size)
        b.second[r0 : r0 + size, :] = encoded
    for s in range(ENC.segments):
        encoded = b.second[s * SLOT : s * SLOT + PHONES, :]
        r.encoded[s] = encoded
        r.encoded_lo[s] = encoded.astype(BF16)


def encoder_backward_kernel(r):
    b, w, o = r, Refs(WEIGHTS, [getattr(r, "w_" + n) for n in WEIGHTS]), r
    start_weights(b, w)
    counts = [r.counts[s] for s in range(ENC.segments)]
    zero_accumulators(b, w)
    start_block(ENC, b)
    load_segments(b, r.phonemes)
    attention_forward(ENC, b, w, counts, SLOT)
    wait_weights(b, w)
    ffn_forward(b, w, ENC.rows)
    b.n1_grad[...] = jnp.zeros_like(b.n1_grad)
    for s in range(ENC.segments):
        b.n1_grad[s * SLOT : s * SLOT + PHONES, :] = r.grad_near[s] + r.grad_far[s].astype(F32)
    for r0, size in pieces(ENC.rows, T):
        n, rstd = normed(b.second[r0 : r0 + size, :])
        dy = b.n1_grad[r0 : r0 + size, :] * slot_keep(counts, r0, size)
        second_norm_back(b, w, r0, size, dy, n, rstd)
    ffn_backward(b, w, ENC.rows)
    ffn_weight_grads(b, ENC.rows)
    send_large_grads(b, o)

    def finish(s, at, q, dh):
        o.input_own[s] = dh[0 : PHONES // 2]
        o.input_away[s] = dh[PHONES // 2 : PHONES].astype(BF16)

    attention_backward(ENC, b, w, counts, SLOT, finish)
    store_block_grads(b, o)


def encoder_forward_branch():
    return (
        encoder_forward_kernel,
        names(counts=1, phonemes=1) + W_NAMES,
        names(encoded=1, encoded_lo=1),
        block_scratch(ENC, False),
    )


def encoder_backward_branch():
    return (
        encoder_backward_kernel,
        names(counts=1, phonemes=1, grad_near=1, grad_far=1) + W_NAMES,
        names(input_own=1, input_away=1) + G_NAMES,
        dict(block_scratch(ENC, True), n1_grad=pltpu.VMEM((ENC.rows, D), F32)),
    )


def halves(x):
    high = x.astype(BF16)
    return high, (x - high.astype(F32)).astype(BF16)


def predict(r, p, rows, keep, keep_row, hidden, cotangent, estimate):
    tiles = rows // T
    conv_a, conv_b = r.convs.at[p, 0], r.convs.at[p, 1]
    scale_a, scale_b = r.scales[p, 0:1, :], r.scales[p, 1:2, :]
    shift_a, shift_b = r.shifts[p, 0:1, :], r.shifts[p, 1:2, :]
    readout = r.readouts[pl.ds(p, 1), :]
    edge = jnp.zeros((8, D), F32)
    r.after[0:8, :] = edge
    r.after[rows + 8 : rows + 16, :] = edge

    def unfold(source, target, k):
        v = source[tile_rows(k, 16), :]
        for t in range(3):
            target[tile_rows(k), t * D : (t + 1) * D] = v[7 + t : 7 + t + T].astype(BF16)

    def fold(target, gradient, conv, k):
        r.dcols3[16 : 16 + T, :] = dot_nt(gradient, conv[...])
        total = r.dcols3[9 : 25 + T, 0:D]
        for t in range(1, 3):
            total = total + r.dcols3[9 - t : 25 - t + T, t * D : (t + 1) * D]
        target[tile_rows(k, 16), :] += total

    def clear(target):
        def body(k):
            target[tile_rows(k), :] = jnp.zeros((T, D), F32)

        each(tiles, body)
        target[rows : rows + 16, :] = jnp.zeros((16, D), F32)

    def first_half(k):
        at = tile_rows(k)
        unfold(hidden, r.cols_a, k)
        value, slope = gelu_pair(dot(r.cols_a[at, :], conv_a[...]))
        n, rstd = normed(value)
        r.slope_a[at, :] = slope
        r.norm_a[at, :] = n
        r.rstd_a[at, :] = rstd
        r.after[tile_rows(k, 0, 8), :] = (n * scale_a + shift_a) * keep(k * T, T)

    each(tiles, first_half)
    clear(r.dafter)
    weighted = readout * scale_b
    weighted_mean = jnp.mean(weighted, axis=1, keepdims=True)
    high, low = halves(readout)
    row = iota((16, D), 0)
    two = jnp.where(row == 0, high.astype(F32), jnp.where(row == 1, low.astype(F32), 0.0))
    two = two.astype(BF16)

    def second_half(k):
        at = span(k * T, T)
        unfold(r.after, r.cols_b, k)
        value, slope = gelu_pair(dot(r.cols_b[at, :], conv_b[...]))
        n, rstd = normed(value)
        after = n * scale_b + shift_b
        high, low = halves(after)
        with_high, with_low = dot_nt(two, high), dot_nt(two, low)
        guess = with_high[0:1] + with_high[1:2] + with_low[0:1]
        estimate[:, at] = guess * keep_row(k * T, T)
        column = jnp.broadcast_to(cotangent[:, at], (128, T)).T
        column = jnp.concatenate([column, column], axis=1) * keep(k * T, T)
        r.a_vec[p, 2:3, :] += readout * column_sum(column * n)
        r.a_vec[p, 3:4, :] += readout * column_sum(column)
        r.a_vec[p, 4:5, :] += column_sum(column * after)
        inner = jnp.mean(weighted * n, axis=1, keepdims=True)
        gradient = (column * (weighted - weighted_mean - n * inner) * rstd * slope).astype(BF16)
        r.grad_b[at, :] = gradient
        fold(r.dafter, gradient, conv_b, k)

    each(tiles, second_half)
    clear(hidden)

    def back(k):
        at = tile_rows(k)
        dy = r.dafter[tile_rows(k, 0, 8), :] * keep(k * T, T)
        n = r.norm_a[at, :]
        r.a_vec[p, 0:1, :] += column_sum(dy * n)
        r.a_vec[p, 1:2, :] += column_sum(dy)
        gradient = norm_back(dy * scale_a, n, r.rstd_a[at, :]) * r.slope_a[at, :]
        gradient = gradient.astype(BF16)
        r.grad_a[at, :] = gradient
        fold(hidden, gradient, conv_a, k)

    each(tiles, back)
    r.a_conv[p, 0] += dot_tn(r.grad_a[0:rows, :], r.cols_a[0:rows, :])
    r.a_conv[p, 1] += dot_tn(r.grad_b[0:rows, :], r.cols_b[0:rows, :])


def predictor_kernel(sequences, r):
    r.a_conv[...] = jnp.zeros_like(r.a_conv)
    r.a_vec[...] = jnp.zeros_like(r.a_vec)
    r.a_table[...] = jnp.zeros_like(r.a_table)
    r.dcols3[0:16, :] = jnp.zeros((16, 3 * D), F32)
    r.dcols3[16 + T :, :] = jnp.zeros((16, 3 * D), F32)
    r.durations_pad[...] = jnp.zeros_like(r.durations_pad)
    r.durations_pad[0:sequences, 0:PHONES] = r.durations[...]
    stop = span_ends(r.durations_pad[...])
    r.stop[...] = stop
    r.start[...] = stop - r.durations_pad[...]
    counts = [r.counts[s] for s in range(sequences)]
    slots = sequences * SLOT
    r.hidden[0, 0 : slots + 16, :] = jnp.zeros((slots + 16, D), F32)
    for s in range(sequences):
        r.hidden[0, s * SLOT + 8 : s * SLOT + 8 + PHONES, :] = r.encoded[s]

    def keep_slots(r0, size):
        return slot_keep(counts, r0, size)

    def keep_slots_row(r0, size):
        lane = iota((1, size), 1) + r0
        kept = lane < counts[0]
        for s in range(1, sequences):
            kept = kept | ((lane >= s * SLOT) & (lane < s * SLOT + counts[s]))
        return kept.astype(F32)

    predict(
        r, 0, slots, keep_slots, keep_slots_row, r.hidden.at[0], r.cot_duration, r.duration_pred
    )
    for s in range(sequences):
        r.dencoded[s] = r.hidden[0, s * SLOT + 8 : s * SLOT + 8 + PHONES, :]
    r.encoded_high[...] = jnp.zeros_like(r.encoded_high)
    r.encoded_low[...] = jnp.zeros_like(r.encoded_low)

    def one(s):
        count = r.frames[s]
        high, low = halves(r.encoded[s])
        r.encoded_high[0:PHONES, :] = high
        r.encoded_low[0:PHONES, :] = low
        start, stop = r.start[pl.ds(s, 1), :], r.stop[pl.ds(s, 1), :]
        edge = jnp.zeros((8, D), F32)
        for k in range(2):
            r.hidden[k, 0:8, :] = edge
            r.hidden[k, FRAMES + 8 : FRAMES + 16, :] = edge

        def embed(k):
            at = span(k * T, T)
            expand = expansion(start, stop, k * T, T)
            r.expand[at, :] = expand
            hot = hot_columns(r.pitch_bins[pl.ds(s, 1), at], count, k * T, T)
            r.hot[:, at] = hot
            frames = dot(expand, r.encoded_high[...]) + dot(expand, r.encoded_low[...])
            r.hidden[0, tile_rows(k, 0, 8), :] = frames
            pitched = frames + dot_tn(hot, r.pitch_table[...])
            r.hidden[1, tile_rows(k, 0, 8), :] = pitched

        each(FRAMES // T, embed)

        def keep(r0, size):
            return (iota((size, 1), 0) + r0 < count).astype(F32)

        def keep_row(r0, size):
            return (iota((1, size), 1) + r0 < count).astype(F32)

        def both(k):
            line = pl.ds(k * sequences + s, 1)
            predict(
                r, k + 1, FRAMES, keep, keep_row, r.hidden.at[k],
                r.cot_frames.at[line], r.frame_preds.at[line],
            )

        each(2, both)
        high, low = halves(r.hidden[1, 8 : FRAMES + 8, :])
        r.a_table[...] += dot(r.hot[...], high) + dot(r.hot[...], low)
        high, low = halves(r.hidden[0, 8 : FRAMES + 8, :] + r.hidden[1, 8 : FRAMES + 8, :])
        dencoded = dot_tn(r.expand[...], high) + dot_tn(r.expand[...], low)
        r.dencoded[s] = r.dencoded[s] + dencoded[0:PHONES]

    each(sequences, one)
    some = PHONES // 2
    r.away[...] = jnp.zeros_like(r.away)
    r.away[0 : 2 * sequences, :] = r.frame_preds[:, FRAMES // 2 :]
    for s in range(sequences):
        line = r.duration_pred[:, s * SLOT + some : s * SLOT + PHONES]
        r.away[2 * sequences + s : 2 * sequences + s + 1, 0:some] = line
    r.small[...] = r.away[...].astype(BF16)
    for p in range(3):
        for k in range(2):
            at = (2 * p + k) * 3 * D
            r.pack[:, at : at + 3 * D] = r.a_conv[p, k].astype(BF16)
    rows = jnp.concatenate([r.a_vec[p] for p in range(3)] + [jnp.zeros((104, D), F32)], axis=0)
    r.pack[:, AT_VECTORS:AT_TABLES] = rows.T.astype(BF16)
    r.pack[:, AT_TABLES : AT_TABLES + BINS] = r.a_table[...].T.astype(BF16)


def predictors_branch(sequences):
    return (
        functools.partial(predictor_kernel, sequences),
        names(frames=1, counts=1, encoded=1, durations=1, pitch_bins=1, convs=1, scales=1,
              shifts=1, readouts=1, pitch_table=1, cot_duration=1, cot_frames=1),
        names(duration_pred=1, frame_preds=1, small=1, dencoded=1, pack=1),
        dict(
            away=pltpu.VMEM((16, FRAMES // 2), F32),
            a_conv=pltpu.VMEM((3, 2, D, 3 * D), F32),
            a_vec=pltpu.VMEM((3, 8, D), F32),
            a_table=pltpu.VMEM((BINS, D), F32),
            durations_pad=pltpu.VMEM((8, 256), jnp.int32),
            start=pltpu.VMEM((8, 256), jnp.int32),
            stop=pltpu.VMEM((8, 256), jnp.int32),
            encoded_high=pltpu.VMEM((256, D), BF16),
            encoded_low=pltpu.VMEM((256, D), BF16),
            expand=pltpu.VMEM((FRAMES, 256), BF16),
            hot=pltpu.VMEM((BINS, FRAMES), BF16),
            hidden=pltpu.VMEM((2, FRAMES + 16, D), F32),
            after=pltpu.VMEM((FRAMES + 16, D), F32),
            dafter=pltpu.VMEM((FRAMES + 16, D), F32),
            cols_a=pltpu.VMEM((FRAMES, 3 * D), BF16),
            cols_b=pltpu.VMEM((FRAMES, 3 * D), BF16),
            slope_a=pltpu.VMEM((FRAMES, D), F32),
            norm_a=pltpu.VMEM((FRAMES, D), F32),
            rstd_a=pltpu.VMEM((FRAMES, 1), F32),
            grad_a=pltpu.VMEM((FRAMES, D), BF16),
            grad_b=pltpu.VMEM((FRAMES, D), BF16),
            dcols3=pltpu.VMEM((T + 32, 3 * D), F32),
        ),
    )


def swapped(array):
    return lax.ppermute(array, SECTION, [(0, 1), (1, 0)])


def scattered_anyhow(arrays):
    ways = lax.axis_size(DP)
    shares = [a.shape[0] // ways for a in arrays]
    flat = jnp.concatenate([a.reshape(ways, -1) for a in arrays], axis=1)
    flat = lax.psum_scatter(flat, DP, scatter_dimension=0, tiled=True)[0]
    out, at = [], 0
    for a, share in zip(arrays, shares):
        size = share * a.shape[1]
        out.append(flat[at : at + size].reshape(share, a.shape[1]).astype(F32))
        at += size
    return out


def scatter_kernel(steps, cuts, count, lists, trades, given, *refs):
    n, m = len(cuts), len(trades)
    late = given < m
    sources, refs = refs[:count], refs[count:]
    traded, refs = refs[:given], refs[given:]
    outs, refs = refs[:count], refs[count:]
    arrived, refs = refs[:m], refs[m:]
    mine, landed = refs[:n], refs[n : n * (1 + steps)]
    load_sem, send_sem, recv_sem, *rest = refs[n * (1 + steps) :]
    if m:
        trade_send, trade_recv = rest[:2]
    if late:
        rounded = rest[2]
        traded = traded + (rounded,)
    me = lax.axis_index(DP)
    bits = [lax.rem(lax.div(me, 1 << k), 2) for k in range(steps)]
    partners = [me + (1 << k) * (1 - 2 * bits[k]) for k in range(steps)]
    def trade(i):
        return pltpu.make_async_remote_copy(
            src_ref=traded[i],
            dst_ref=arrived[i],
            send_sem=trade_send.at[i],
            recv_sem=trade_recv.at[i],
            device_id={SECTION: 1 - lax.axis_index(SECTION)},
            device_id_type=pl.DeviceIdType.MESH,
        )

    def every(k):
        return (slice(None),) * (steps - 1 - k)

    def source(i, bit):
        array, first, size = cuts[i]
        return sources[array].at[every(0) + (bit, slice(None), pl.ds(first, size))]

    def load(i):
        return pltpu.make_async_copy(source(i, bits[0]), mine[i], load_sem.at[i])

    def copy(i, k):
        if k == 0:
            out = source(i, 1 - bits[0])
        else:
            out = landed[i * steps + k - 1].at[every(k) + (1 - bits[k],)]
        return pltpu.make_async_remote_copy(
            src_ref=out,
            dst_ref=landed[i * steps + k],
            send_sem=send_sem.at[i, k],
            recv_sem=recv_sem.at[i, k],
            device_id={DP: partners[k]},
            device_id_type=pl.DeviceIdType.MESH,
        )

    def finish(i, k):
        copy(i, k).wait_recv()
        if k == 0:
            load(i).wait()
        there = landed[i * steps + k]
        for index in itertools.product(range(2), repeat=steps - 1 - k):
            if k == 0:
                stayed = mine[i][index]
            else:
                stayed = landed[i * steps + k - 1][index + (bits[k],)]
            total = there[index].astype(F32) + stayed.astype(F32)
            if k == steps - 1:
                array, first, size = cuts[i]
                outs[array][:, first : first + size] = total
            else:
                there[index] = total.astype(BF16)
        if k < steps - 1:
            copy(i, k + 1).start()

    def begin(i):
        copy(i, 0).start()
        load(i).start()

    def run(section, chosen):
        barrier = pltpu.get_barrier_semaphore()
        for partner in partners if chosen else ():
            pl.semaphore_signal(
                barrier, inc=1, device_id={DP: partner}, device_id_type=pl.DeviceIdType.MESH
            )
        if any(sender != section for sender in trades):
            pl.semaphore_signal(
                barrier,
                inc=1,
                device_id={SECTION: 1 - lax.axis_index(SECTION)},
                device_id_type=pl.DeviceIdType.MESH,
            )
        pl.semaphore_wait(barrier, (steps if chosen else 0) + (1 if section in trades else 0))
        size = len(chosen)
        for i in range(given):
            if trades[i] == section:
                trade(i).start()
        last = [x for x, i in enumerate(chosen) if cuts[i][0] == count - 1]
        for turn in range(-AHEAD, size + steps - 1):
            if turn + AHEAD < size:
                begin(chosen[turn + AHEAD])
            for k in range(steps):
                at = turn - k
                if 0 <= at < size:
                    finish(chosen[at], k)
                    if late and trades[-1] == section and k == steps - 1 and at == last[-1]:
                        rounded[...] = outs[count - 1][...].astype(BF16)
                        trade(m - 1).start()
        for i in chosen:
            for k in range(steps):
                copy(i, k).wait_send()
        for i in range(m):
            if trades[i] == section:
                trade(i).wait_send()
            else:
                trade(i).wait_recv()

    for section, chosen in enumerate(lists):
        if chosen or m:
            here = (lax.axis_index(SECTION) == section).astype(jnp.int32)
            each(here, functools.partial(one_time, run, section, chosen))


def one_time(run, section, chosen, _):
    run(section, chosen)


def scattered(arrays, name, collective, width, parts, traded, trades):
    ways = lax.axis_size(DP)
    steps = ways.bit_length() - 1
    if ways != 1 << steps or any(a.shape[0] // ways % 16 for a in arrays):
        sums = scattered_anyhow(arrays)
        traded = [*traded, sums[-1].astype(BF16)]
        return sums + [
            lax.ppermute(a, SECTION, [(s, 1 - s)]) for a, s in zip(traded, trades)
        ]
    shares = [a.shape[0] // ways for a in arrays]
    cuts = [
        (k, at, size)
        for k, a in enumerate(arrays)
        for at, size in pieces(a.shape[1], width if a.shape[0] > 1024 else 768)
    ]
    lists = [[i for k in part for i, cut in enumerate(cuts) if cut[0] == k] for part in parts]
    landed = [
        pltpu.VMEM((2,) * (steps - 1 - k) + (shares[array], size), BF16)
        for array, _, size in cuts
        for k in range(steps)
    ]
    mine = [pltpu.VMEM((2,) * (steps - 1) + (shares[array], size), BF16) for array, _, size in cuts]
    scratch = [
        *mine,
        *landed,
        pltpu.SemaphoreType.DMA((len(cuts),)),
        pltpu.SemaphoreType.DMA((len(cuts), steps)),
        pltpu.SemaphoreType.DMA((len(cuts), steps)),
    ]
    outs = [jax.ShapeDtypeStruct((share, a.shape[1]), F32) for share, a in zip(shares, arrays)]
    far, near = pl.BlockSpec(memory_space=pl.ANY), pl.BlockSpec(memory_space=pltpu.VMEM)
    out_specs = [near] * len(outs)
    scratch += [pltpu.SemaphoreType.DMA((len(trades),))] * 2
    sums = jax.ShapeDtypeStruct(outs[-1].shape, BF16)
    outs += [jax.ShapeDtypeStruct(a.shape, a.dtype) for a in traded]
    out_specs += [far] * len(traded)
    if len(trades) > len(traded):
        scratch.append(pltpu.VMEM(sums.shape, BF16))
        outs.append(sums)
        out_specs.append(near)
    return pl.pallas_call(
        functools.partial(
            scatter_kernel, steps, cuts, len(arrays), lists, tuple(trades), len(traded)
        ),
        name=name,
        in_specs=[far] * (len(arrays) + len(traded)),
        out_specs=out_specs,
        out_shape=outs,
        scratch_shapes=scratch,
        compiler_params=pltpu.CompilerParams(
            collective_id=collective, has_side_effects=True, vmem_limit_bytes=60 * 2**20
        ),
    )(
        *[a.reshape((2,) * steps + (share, a.shape[1])) for share, a in zip(shares, arrays)],
        *traded,
    )


def body(phonemes, phone_lengths, durations, pitch_bins, energy_bins, joint_weight, output_weight,
         widen_weight, narrow_weight, block_scales, block_shifts, predictor_convs,
         predictor_scales, predictor_shifts, predictor_outputs, pitch_table, energy_table,
         mel_weight, mel_cotangent, duration_cotangent, pitch_cotangent, energy_cotangent):
    first = lax.axis_index(SECTION) == 0
    n = phonemes.shape[0]
    frames = jnp.sum(durations, axis=1)
    block_weights = (joint_weight[0], output_weight[0], widen_weight[0], narrow_weight[0],
                     block_scales[0], block_shifts[0])
    weights = dict(zip(W_NAMES, block_weights))
    cot_duration = jnp.pad(duration_cotangent, ((0, 0), (0, SLOT - PHONES))).reshape(1, n * SLOT)
    cot_frames = jnp.concatenate([pitch_cotangent, energy_cotangent])
    encoded, encoded_lo = section_call(
        "encoder_forward",
        dict(counts=phone_lengths, phonemes=phonemes, **weights),
        dict(encoded=((n, PHONES, D), F32), encoded_lo=((n, PHONES, D), BF16)),
        (encoder_forward_branch(), None),
        smem=names(counts=1),
    )
    arrived = lax.ppermute(encoded_lo, SECTION, [(0, 1)])
    duration, preds, small, mel_own, mel_away, dencoded, dsent, *grads, pack, pack_far = section_call(
        "predictors_or_decoder",
        dict(
            frames=frames,
            counts=phone_lengths,
            encoded=encoded,
            arrived=arrived,
            durations=durations,
            pitch_bins=pitch_bins,
            energy_bins=energy_bins,
            convs=predictor_convs,
            scales=predictor_scales,
            shifts=predictor_shifts,
            readouts=predictor_outputs,
            pitch_table=pitch_table,
            energy_table=energy_table,
            mel_turned=mel_weight.T,
            mel_cotangent=mel_cotangent.transpose(0, 2, 1),
            cot_duration=cot_duration,
            cot_frames=cot_frames,
            **weights,
        ),
        dict(
            duration_pred=((1, n * SLOT), F32),
            frame_preds=((2 * n, FRAMES), F32),
            small=((16, FRAMES // 2), BF16),
            mel_own=((n, MELS, FRAMES // 2), F32),
            mel_away=((n, MELS, FRAMES // 2), BF16),
            dencoded=((n, PHONES, D), F32),
            dsent=((n, PHONES, D), BF16),
            **GRADS,
            pack=((D, NEAR_PACK), BF16),
            pack_far=((D, PACK - AT_TABLES), BF16),
        ),
        (predictors_branch(n), decoder_branch(n)),
        smem=names(frames=1, counts=1),
    )
    pack, returned = scattered([pack], "pack_sums", 1, 768, ((0,), ()), (dsent,), (1,))
    input_own, input_away, *grads = section_call(
        "encoder_backward",
        dict(
            counts=phone_lengths,
            phonemes=phonemes,
            grad_near=dencoded,
            grad_far=returned,
            **weights,
            **dict(zip(G_NAMES, grads)),
        ),
        dict(
            input_own=((n, PHONES // 2, D), F32),
            input_away=((n, PHONES // 2, D), BF16),
            **GRADS,
        ),
        (encoder_backward_branch(), None),
        smem=names(counts=1),
        kept=G_NAMES,
    )
    sums = dict(zip(G_NAMES, grads))
    order = names(g_widen=1, g_narrow=1, g_joint=1, g_output=1, g_vec=1)
    sums = scattered(
        [sums[n] for n in order] + [pack_far],
        "block_sums",
        2,
        128,
        (range(5), (5, 0, 1, 2, 3, 4)),
        (pack, small, input_away, mel_away),
        (0, 0, 0, 1, 1),
    )
    near_pack, small, input_away, mel_away, far_pack = sums[6:]
    own = dict(zip(order, sums))
    return assembled(
        n,
        sums[0].shape[0],
        dict(
            **own,
            pack=pack,
            pack_far=sums[5],
            duration=duration,
            preds=preds,
            mel_own=mel_own,
            input_own=input_own,
            near_pack=near_pack,
            small=small,
            input_away=input_away,
            mel_away=mel_away,
            far_pack=far_pack,
        ),
    )


def assemble_kernel(n, ins, outs, *refs):
    far, refs = refs[: len(ins)], refs[len(ins) :]
    outs_refs, (*near, sem) = refs[: len(outs)], refs[len(outs) :]
    copies = [
        pltpu.make_async_copy(a, b, sem.at[k]) for k, (a, b) in enumerate(zip(far, near))
    ]
    for copy in copies:
        copy.start()
    for copy in copies:
        copy.wait()
    r = Refs(ins + outs, [*near, *outs_refs])
    first = lax.axis_index(SECTION) == 0
    half, some = FRAMES // 2, PHONES // 2

    def choose(near, far):
        return jnp.where(first, near.astype(F32), far.astype(F32))

    for s in range(n):
        r.o_mel[s] = choose(r.mel_away[s], r.mel_own[s])
        r.o_input[s] = choose(r.input_own[s], r.input_away[s])
    small = r.small[...].astype(F32)
    preds = choose(r.preds[:, 0:half], small[0 : 2 * n, :])
    r.o_pitch[...] = preds[0:n]
    r.o_energy[...] = preds[n : 2 * n]
    for s in range(n):
        r.o_duration[s : s + 1, :] = choose(
            r.duration[:, s * SLOT : s * SLOT + some], small[2 * n + s : 2 * n + s + 1, 0:some]
        )
    r.o_joint[0] = r.g_joint[...]
    r.o_output[0] = r.g_output[...]
    r.o_widen[0] = r.g_widen[...]
    r.o_narrow[0] = r.g_narrow[...]
    share = r.pack.shape[0]
    block_vec = r.g_vec[...].T
    vec = choose(r.pack[:, AT_VECTORS:AT_TABLES], r.near_pack[:, AT_VECTORS:AT_TABLES]).T
    for k in range(2):
        r.o_block_scales[0, k : k + 1, :] = block_vec[2 * k : 2 * k + 1, 0:share]
        r.o_block_shifts[0, k : k + 1, :] = block_vec[2 * k + 1 : 2 * k + 2, 0:share]
        for p in range(3):
            at = (2 * p + k) * 3 * D
            r.o_convs[p, k] = choose(
                r.pack[:, at : at + 3 * D], r.near_pack[:, at : at + 3 * D]
            )
            row = 8 * p + 2 * k
            r.o_scales[p, k : k + 1, :] = vec[row : row + 1, 0:share]
            r.o_shifts[p, k : k + 1, :] = vec[row + 1 : row + 2, 0:share]
    for p in range(3):
        r.o_readouts[p : p + 1, :] = vec[8 * p + 4 : 8 * p + 5, 0:share]
    near = choose(r.pack[:, AT_TABLES:], r.near_pack[:, AT_TABLES:])
    far = choose(r.far_pack[...], r.pack_far[...])
    r.o_pitch_table[...] = near + far[:, 0:BINS]
    r.o_energy_table[...] = far[:, BINS : 2 * BINS]
    r.o_mel_weight[...] = far[:, 2 * BINS : 2 * BINS + MELS]


def assembled(n, widen_rows, ins):
    share = ins[names(pack=1)[0]].shape[0]
    narrow_rows = FF * share // D
    outs = dict(
        o_mel=(n, MELS, FRAMES // 2),
        o_duration=(n, PHONES // 2),
        o_pitch=(n, FRAMES // 2),
        o_energy=(n, FRAMES // 2),
        o_input=(n, PHONES // 2, D),
        o_joint=(1, share, 3 * D),
        o_output=(1, share, D),
        o_widen=(1, widen_rows, FF),
        o_narrow=(1, narrow_rows, D),
        o_block_scales=(1, 2, share),
        o_block_shifts=(1, 2, share),
        o_convs=(3, 2, share, 3 * D),
        o_scales=(3, 2, share),
        o_shifts=(3, 2, share),
        o_readouts=(3, share),
        o_pitch_table=(share, BINS),
        o_energy_table=(share, BINS),
        o_mel_weight=(share, MELS),
    )
    whole = pl.BlockSpec(memory_space=pltpu.VMEM)
    results = pl.pallas_call(
        functools.partial(assemble_kernel, n, list(ins), list(outs)),
        name="assemble",
        in_specs=[pl.BlockSpec(memory_space=pl.ANY)] * len(ins),
        out_specs=[whole] * len(outs),
        out_shape=[jax.ShapeDtypeStruct(shape, F32) for shape in outs.values()],
        scratch_shapes=[
            *[pltpu.VMEM(a.shape, a.dtype) for a in ins.values()],
            pltpu.SemaphoreType.DMA((len(ins),)),
        ],
        compiler_params=pltpu.CompilerParams(vmem_limit_bytes=61 * 2**20),
    )(*ins.values())
    results = list(results)
    results[0] = results[0].transpose(0, 2, 1)
    results[11] = results[11].transpose(0, 1, 3, 2)
    results[15], results[16] = results[15].T, results[16].T
    return tuple(results)


def solution(mesh):
    halves_of_rows = P(DP, SECTION)
    row, rows, blocks = P(DP), P(DP, None), P(DP, None, None)
    table, block_sums = P(SECTION, None, None), P(SECTION, DP, None)
    block_vectors, vectors, columns = P(SECTION, None, DP), P(None, None, DP), P(None, DP)
    return jax.shard_map(
        body,
        mesh=mesh,
        in_specs=(blocks, row, rows, rows, rows) + (table,) * 6 + (P(),) * 7
        + (blocks, rows, rows, rows),
        out_specs=(
            P(DP, SECTION, None),
            halves_of_rows,
            halves_of_rows,
            halves_of_rows,
            P(DP, SECTION, None),
            *(block_sums,) * 4,
            block_vectors,
            block_vectors,
            P(None, None, None, DP),
            vectors,
            vectors,
            columns,
            columns,
            columns,
            rows,
        ),
        check_vma=False,
    )
```

```python
import functools
import itertools
import math

import jax
import jax.numpy as jnp
from jax import lax
from jax.experimental import pallas as pl
from jax.experimental.pallas import tpu as pltpu
from jax.sharding import PartitionSpec as P

D = 256
HEAD = 128
FF = 1024
BINS = 256
MELS = 80
TAPS = 9
PHONES = 160
FRAMES = 1024
SLOT = 192
WIDE = TAPS * D
EPS = 1e-5
AT_VECTORS = 6 * 3 * D
AT_TABLES = AT_VECTORS + 128
AT_MEL = AT_TABLES + 2 * BINS
PACK = AT_MEL + 128
NEAR_PACK = AT_TABLES + BINS
C1 = math.sqrt(2.0 / math.pi)
C2 = C1 * 0.044715
SCALE = HEAD**-0.5
SECTION = "section"
DP = "dp"
LOG2E = math.log2(math.e)
F32 = jnp.float32
BF16 = jnp.bfloat16


def names(**kept):
    return tuple(kept)


def dot(a, b):
    return jnp.dot(a, b, preferred_element_type=F32)


def dot_nt(a, b):
    return lax.dot_general(a, b, (((1,), (1,)), ((), ())), preferred_element_type=F32)


def dot_tn(a, b):
    return lax.dot_general(a, b, (((0,), (0,)), ((), ())), preferred_element_type=F32)


def iota(shape, dim):
    return lax.broadcasted_iota(jnp.int32, shape, dim)


def gelu_pair(x):
    x2 = x * x
    h = 0.5 + 0.5 * jnp.tanh(x * (C1 + C2 * x2))
    value = x * h
    slope = h + value * (1.0 - h) * (2.0 * C1 + 6.0 * C2 * x2)
    return value, slope


def normed(r):
    mean = jnp.mean(r, axis=-1, keepdims=True)
    centred = r - mean
    rstd = lax.rsqrt(jnp.mean(centred * centred, axis=-1, keepdims=True) + EPS)
    return centred * rstd, rstd


def norm_back(t, n, rstd):
    return (
        t - jnp.mean(t, axis=-1, keepdims=True) - n * jnp.mean(t * n, axis=-1, keepdims=True)
    ) * rstd


def column_sum(x):
    return jnp.sum(x, axis=0, keepdims=True)


def aligned(i, size):
    return pl.ds(pl.multiple_of(i * size, size), size)


def each(count, body):
    def step(i, carry):
        body(i)
        return carry

    lax.fori_loop(0, count, step, 0)


class Layout:
    def __init__(self, segments, span, query):
        self.segments, self.span, self.query = segments, span, query
        self.rows = segments * span
        self.fewest = span // 2


ENC = Layout(4, SLOT, SLOT)
DEC = Layout(1, FRAMES, 256)
T = 256
AHEAD = 2


def pieces(length, size):
    return [(at, min(size, length - at)) for at in range(0, length, size)]


def block_scratch(layout, backward, single=False):
    L, S, n = layout.rows, layout.span, layout.segments
    shapes = dict(
        h_lo=pltpu.VMEM((L, D), BF16),
        joint=pltpu.VMEM((L, 3 * D), BF16),
        jointT=pltpu.VMEM((n, 3 * D, S), BF16),
        mixedT=pltpu.VMEM((n, D, S), BF16),
        first=pltpu.VMEM((L + 16, D), F32),
        cols=pltpu.VMEM((L, WIDE), BF16),
        slope=pltpu.VMEM((L, FF), F32),
        wide=pltpu.VMEM((2, T, D), F32),
        second=pltpu.VMEM((L, D), F32),
        widen=pltpu.VMEM((WIDE, FF), BF16),
        narrow=pltpu.VMEM((FF, D), BF16),
        sem=pltpu.SemaphoreType.DMA((6,)),
    )
    if backward:
        shapes.update(
            expo=pltpu.VMEM((n, 2, S, S), BF16),
            rinv=pltpu.VMEM((n, 2, 8, S), F32),
            n1=pltpu.VMEM((L, D), F32),
            r1=pltpu.VMEM((L, 1), F32),
            act=pltpu.VMEM((L, FF), BF16),
            dnar=pltpu.VMEM((max(L, FF), D), BF16),
            dwid=pltpu.VMEM((L, FF), BF16),
            dcols=pltpu.VMEM((T + 32, WIDE), F32),
            dfirst=pltpu.VMEM((L + 16, D), F32),
            datt=pltpu.VMEM((L, D), BF16),
            dmixT=pltpu.VMEM((n, D, S), BF16),
            inner=pltpu.VMEM((n, 2, 8, S), F32),
            djointT=pltpu.VMEM((n, 3 * D, S), BF16),
            joint_turned=pltpu.VMEM((3 * D, D), BF16),
            a_joint=pltpu.VMEM((3 * D, D), F32),
            a_output=pltpu.VMEM((D, D), F32),
            a_vec=pltpu.VMEM((8, D), F32),
        )
    if backward and single:
        shapes.update(widen_lo=pltpu.VMEM((WIDE, FF), BF16), narrow_lo=pltpu.VMEM((FF, D), BF16))
    elif backward:
        shapes.update(
            spare=pltpu.VMEM((WIDE - 2 * L, FF), BF16),
            a_widen=pltpu.VMEM((WIDE, FF), F32),
            a_narrow=pltpu.VMEM((FF, D), F32),
        )
    return shapes


def start_block(layout, b):
    edge = jnp.zeros((8, D), F32)
    b.first[0:8, :] = edge
    b.first[layout.rows + 8 : layout.rows + 16, :] = edge


def zero_accumulators(b, w):
    b.joint_turned[...] = w.joint[...].T
    b.a_joint[...] = jnp.zeros_like(b.a_joint)
    b.a_output[...] = jnp.zeros_like(b.a_output)
    b.a_vec[...] = jnp.zeros_like(b.a_vec)
    b.dcols[0:16, :] = jnp.zeros((16, WIDE), F32)
    if hasattr(b, "widen_lo"):
        return
    b.a_narrow[...] = jnp.zeros_like(b.a_narrow)

    def body(t, _):
        b.a_widen[aligned(t, D), :] = jnp.zeros((D, FF), F32)
        return 0

    lax.fori_loop(0, TAPS, body, 0)


def heads(h):
    return tuple(slice(k * D + h * HEAD, k * D + (h + 1) * HEAD) for k in range(3))


def span(start, size):
    if isinstance(start, int):
        return slice(start, start + size)
    return pl.ds(pl.multiple_of(start, math.gcd(size, 256)), size)


def tile_rows(k, extra=0, first=0):
    return pl.ds(pl.multiple_of(k * T + first, 8), T + extra)


def attention_forward(layout, b, w, counts, length):
    S, save = layout.span, hasattr(b, "expo")
    blocks = [(s, at, q) for s in range(layout.segments) for at, q in pieces(length, layout.query)]
    for s, at, q in blocks:
        rows = slice(s * S + at, s * S + at + q)
        value = dot(b.h_lo[rows, :], w.joint[...]).astype(BF16)
        b.joint[rows, :] = value
        b.jointT[s, :, at : at + q] = value.T
    chunks = pieces(length, D)
    items = [block + (h,) for block in blocks for h in range(2)]

    def score(i):
        s, at, q, h = items[i]
        query_at, key_at, _ = heads(h)
        side = slice((i % 2) * D, (i % 2) * D + q)
        top = None
        for c, size in chunks:
            scores = dot(
                b.joint[s * S + c : s * S + c + size, key_at], b.jointT[s, query_at, at : at + q]
            )
            if c + size > layout.fewest:
                scores = jnp.where(iota((size, q), 0) + c < counts[s], scores, -1e30)
            b.slope[c : c + size, side] = scores
            part = jnp.max(scores.reshape(size // 8, 8, q), axis=0)
            top = part if top is None else jnp.maximum(top, part)
        return jnp.max(top, axis=0, keepdims=True)

    tops = {0: score(0)}
    for i, (s, at, q, h) in enumerate(items):
        if i + 1 < len(items):
            tops[i + 1] = score(i + 1)
        query_at, _, value_at = heads(h)
        side = slice((i % 2) * D, (i % 2) * D + q)
        sums = mixed = None
        for c, size in chunks:
            expo = jnp.exp2((b.slope[c : c + size, side] - tops[i]) * (SCALE * LOG2E))
            part = jnp.sum(expo.reshape(size // 8, 8, q), axis=0)
            sums = part if sums is None else sums + part
            expo = expo.astype(BF16)
            if save:
                b.expo[s, h, c : c + size, at : at + q] = expo
            part = dot(b.jointT[s, value_at, c : c + size], expo)
            mixed = part if mixed is None else mixed + part
        rinv = 1.0 / column_sum(sums)
        b.mixedT[s, query_at, at : at + q] = (mixed * rinv).astype(BF16)
        if save:
            b.rinv[s, h, :, at : at + q] = jnp.broadcast_to(rinv, (8, q))
    for s, at, q in blocks:
        r0 = s * S + at
        attended = dot_tn(b.mixedT[s, :, at : at + q], w.output[...])
        n, rstd = normed(b.h_lo[r0 : r0 + q, :].astype(F32) + attended)
        keep = (iota((q, 1), 0) + at < counts[s]).astype(F32)
        b.first[r0 + 8 : r0 + 8 + q, :] = (n * w.scales[0:1, :] + w.shifts[0:1, :]) * keep
        if save:
            b.n1[r0 : r0 + q, :] = n
            b.r1[r0 : r0 + q, :] = rstd


def ffn_forward(b, w, length):
    save = hasattr(b, "expo")
    tiles = pieces(length, T)
    items = [(k, j) for k in range(len(tiles)) for j in range(4)]

    def unfold(k):
        r0, size = tiles[k]
        v = b.first[r0 : r0 + size + 16, :]
        for t in range(TAPS):
            b.cols[r0 : r0 + size, t * D : (t + 1) * D] = v[4 + t : 4 + t + size].astype(BF16)

    def widen(i):
        k, j = items[i]
        r0, size = tiles[k]
        b.wide[i % 2, 0:size, :] = dot(b.cols[r0 : r0 + size, :], b.widen[:, j * D : (j + 1) * D])

    unfold(0)
    widen(0)
    for i, (k, j) in enumerate(items):
        if j == 1 and k + 1 < len(tiles):
            unfold(k + 1)
        if i + 1 < len(items):
            widen(i + 1)
        r0, size = tiles[k]
        rows, at = slice(r0, r0 + size), slice(j * D, (j + 1) * D)
        value, slope = gelu_pair(b.wide[i % 2, 0:size, :])
        value = value.astype(BF16)
        if save:
            b.act[rows, at] = value
            b.slope[rows, at] = slope
        narrowed = dot(value, b.narrow[at, :])
        before = b.second[rows, :] if j else b.first[r0 + 8 : r0 + 8 + size, :]
        b.second[rows, :] = before + narrowed


def ffn_backward(b, w, length):
    b.dfirst[0 : length + 16, :] = jnp.zeros((length + 16, D), F32)
    for r0, size in pieces(length, T):
        rows = slice(r0, r0 + size)
        b.dcols[16 + size : 32 + size, :] = jnp.zeros((16, WIDE), F32)
        for j in range(4):
            at = slice(j * D, (j + 1) * D)
            b.dwid[rows, at] = (
                dot_nt(b.dnar[rows, :], b.narrow[at, :]) * b.slope[rows, at]
            ).astype(BF16)
        for t in range(TAPS):
            at = slice(t * D, (t + 1) * D)
            b.dcols[16 : 16 + size, at] = dot_nt(b.dwid[rows, :], b.widen[at, :])
        total = b.dcols[12 : 28 + size, 0:D]
        for t in range(1, TAPS):
            total = total + b.dcols[12 - t : 28 - t + size, t * D : (t + 1) * D]
        b.dfirst[r0 : r0 + size + 16, :] += total
        b.dfirst[r0 + 8 : r0 + 8 + size, :] += b.second[rows, :]


def ffn_weight_grads(b, length):
    for t in range(3):
        at = slice(t * 3 * D, (t + 1) * 3 * D)
        b.a_widen[at, :] += dot_tn(b.cols[0:length, at], b.dwid[0:length, :])
    b.a_narrow[...] += dot_tn(b.act[0:length, :], b.dnar[0:length, :])


def attention_backward(layout, b, w, counts, length, finish):
    S = layout.span
    blocks = [(s, at, q) for s in range(layout.segments) for at, q in pieces(length, layout.query)]
    chunks = pieces(length, D)
    for s, at, q in blocks:
        r0 = s * S + at
        rows, pad_rows, lanes = slice(r0, r0 + q), slice(r0 + 8, r0 + 8 + q), slice(at, at + q)
        keep = (iota((q, 1), 0) + at < counts[s]).astype(F32)
        dy = b.dfirst[pad_rows, :] * keep
        n = b.n1[rows, :]
        b.a_vec[0:1, :] += column_sum(dy * n)
        b.a_vec[1:2, :] += column_sum(dy)
        dsum = norm_back(dy * w.scales[0:1, :], n, b.r1[rows, :])
        b.dfirst[pad_rows, :] = dsum
        datt = dsum.astype(BF16)
        b.datt[rows, :] = datt
        dmix = dot_nt(w.output[...], datt)
        for h in range(2):
            head = heads(h)[0]
            part = (dmix[head, :] * b.rinv[s, h, 0:1, lanes]).astype(BF16)
            b.dmixT[s, head, lanes] = part
            inner = column_sum(part.astype(F32) * b.mixedT[s, head, lanes].astype(F32))
            b.inner[s, h, :, lanes] = jnp.broadcast_to(inner, (8, q))
    items = [block + (h,) for block in blocks for h in range(2)]

    def score(i):
        s, at, q, h = items[i]
        side = slice((i % 2) * D, (i % 2) * D + q)
        b.slope[0:length, side] = dot(
            b.joint[s * S : s * S + length, heads(h)[2]], b.dmixT[s, heads(h)[0], at : at + q]
        )

    score(0)
    for i, (s, at, q, h) in enumerate(items):
        if i + 1 < len(items):
            score(i + 1)
        query_at, key_at, _ = heads(h)
        lanes, side = slice(at, at + q), slice((i % 2) * D, (i % 2) * D + q)
        dquery = None
        for c, size in chunks:
            expo = b.expo[s, h, c : c + size, lanes].astype(F32)
            ds = expo * (b.slope[c : c + size, side] - b.inner[s, h, 0:1, lanes])
            ds = ds.astype(BF16)
            part = dot(b.jointT[s, key_at, c : c + size], ds)
            dquery = part if dquery is None else dquery + part
            b.cols[s * S + at : s * S + at + q, h * FRAMES + c : h * FRAMES + c + size] = ds.T
        b.djointT[s, query_at, lanes] = (dquery * SCALE).astype(BF16)
    for s in range(layout.segments):
        rows = slice(s * S, s * S + length)
        for h in range(2):
            query_at, key_at, value_at = heads(h)
            for c, size in chunks:
                lanes = slice(c, c + size)
                dkey = dot(
                    b.jointT[s, query_at, 0:length],
                    b.cols[rows, h * FRAMES + c : h * FRAMES + c + size],
                )
                b.djointT[s, key_at, lanes] = (dkey * SCALE).astype(BF16)
                dvalue = dot_nt(b.dmixT[s, query_at, 0:length], b.expo[s, h, lanes, 0:length])
                b.djointT[s, value_at, lanes] = dvalue.astype(BF16)
        b.a_output[...] += dot(b.mixedT[s, :, 0:length], b.datt[rows, :])
        b.a_joint[...] += dot(b.djointT[s, :, 0:length], b.h_lo[rows, :])
    for s, at, q in blocks:
        dh = dot_tn(b.djointT[s, :, at : at + q], b.joint_turned[...])
        finish(s, at, q, dh + b.dfirst[s * S + at + 8 : s * S + at + 8 + q, :])


def second_norm_back(b, w, r0, size, dy, n, rstd):
    b.a_vec[2:3, :] += column_sum(dy * n)
    b.a_vec[3:4, :] += column_sum(dy)
    dsecond = norm_back(dy * w.scales[1:2, :], n, rstd)
    b.second[r0 : r0 + size, :] = dsecond
    b.dnar[r0 : r0 + size, :] = dsecond.astype(BF16)


class Refs:
    def __init__(self, names, refs):
        for name, ref in zip(names, refs):
            setattr(self, name, ref)


WEIGHTS = names(joint=1, output=1, widen_far=1, narrow_far=1, scales=1, shifts=1)
FAR = names(w_widen_far=1, w_narrow_far=1, g_widen=1, g_narrow=1)


def large_copies(b, o):
    if hasattr(b, "widen_lo"):
        narrow = b.narrow_lo
        parts = [(b.widen_lo, first, size) for first, size in pieces(WIDE, 3 * D)]
    else:
        size = b.act.shape[0]
        narrow = b.dnar.at[pl.ds(0, FF)]
        parts = [(b.act, 0, size), (b.dwid, 0, size), (b.spare, 0, WIDE - 2 * size)]
    copies, at = [pltpu.make_async_copy(narrow, o.g_narrow, b.sem.at[2])], 0
    for k, (buffer, first, size) in enumerate(parts):
        there = o.g_widen.at[pl.ds(at, size)]
        copies.append(
            pltpu.make_async_copy(buffer.at[pl.ds(first, size)], there, b.sem.at[3 + k])
        )
        at += size
    return copies


def send_large_grads(b, o):
    narrow, *widen = large_copies(b, o)
    b.dnar[0:FF, :] = b.a_narrow[...].astype(BF16)
    narrow.start()
    at = 0
    for copy, buffer in zip(widen, (b.act, b.dwid, b.spare)):
        size = buffer.shape[0]
        buffer[...] = b.a_widen[at : at + size, :].astype(BF16)
        copy.start()
        at += size


def make_large_grads(b, o, length):
    narrow, *widen = large_copies(b, o)
    for copy, (at, size) in zip(widen, pieces(WIDE, 3 * D)):
        part = dot_tn(b.cols[0:length, at : at + size], b.dwid[0:length, :])
        b.widen_lo[at : at + size, :] = part.astype(BF16)
        copy.start()
    b.narrow_lo[...] = dot_tn(b.act[0:length, :], b.dnar[0:length, :]).astype(BF16)
    narrow.start()


def store_block_grads(b, o):
    o.g_joint[...] = b.a_joint[...].T.astype(BF16)
    o.g_output[...] = b.a_output[...].astype(BF16)
    rows = jnp.concatenate([b.a_vec[...], jnp.zeros((120, D), F32)], axis=0)
    o.g_vec[...] = rows.T.astype(BF16)
    for copy in large_copies(b, o):
        copy.wait()


def start_weights(b, w):
    pltpu.make_async_copy(w.widen_far, b.widen, b.sem.at[0]).start()
    pltpu.make_async_copy(w.narrow_far, b.narrow, b.sem.at[1]).start()


def wait_weights(b, w):
    pltpu.make_async_copy(w.widen_far, b.widen, b.sem.at[0]).wait()
    pltpu.make_async_copy(w.narrow_far, b.narrow, b.sem.at[1]).wait()


GRADS = dict(
    g_joint=((D, 3 * D), BF16),
    g_output=((D, D), BF16),
    g_widen=((WIDE, FF), BF16),
    g_narrow=((FF, D), BF16),
    g_vec=((D, 128), BF16),
)


def expansion(start, stop, first_row, size):
    row = iota((size, 256), 0) + first_row
    return ((row >= start) & (row < stop)).astype(F32).astype(BF16)


def hot_columns(bins, count, first_lane, size):
    live = iota((1, size), 1) + first_lane < count
    return ((iota((BINS, size), 0) == bins) & live).astype(F32).astype(BF16)


def span_ends(durations):
    upper = (iota((256, 256), 0) <= iota((256, 256), 1)).astype(F32).astype(BF16)
    return dot(durations.astype(F32).astype(BF16), upper).astype(jnp.int32)


def decoder_kernel(sequences, r):
    b, w, o = r, Refs(WEIGHTS, [getattr(r, "w_" + n) for n in WEIGHTS]), r
    layout = DEC
    start_weights(b, w)
    zero_accumulators(b, w)
    start_block(layout, b)
    r.a_mel[...] = jnp.zeros_like(r.a_mel)
    r.a_table[...] = jnp.zeros_like(r.a_table)
    r.durations_pad[...] = jnp.zeros_like(r.durations_pad)
    r.durations_pad[0:sequences, 0:PHONES] = r.durations[...]
    stop = span_ends(r.durations_pad[...])
    r.stop[...] = stop
    r.start[...] = stop - r.durations_pad[...]
    r.encoded_pad[...] = jnp.zeros_like(r.encoded_pad)

    def sequence(s, length):
        count = r.frames[s]
        counts = [count]
        r.encoded_pad[0:PHONES, :] = r.arrived[s]
        start, stop = r.start[pl.ds(s, 1), :], r.stop[pl.ds(s, 1), :]
        tiles = pieces(length, T)
        for r0, size in tiles:
            rows = slice(r0, r0 + size)
            expand = expansion(start, stop, r0, size)
            r.expand[rows, :] = expand
            hot_p = hot_columns(r.pitch_bins[pl.ds(s, 1), rows], count, r0, size)
            hot_e = hot_columns(r.energy_bins[pl.ds(s, 1), rows], count, r0, size)
            r.hot[0:BINS, rows] = hot_p
            r.hot[BINS:, rows] = hot_e
            adapted = dot(expand, r.encoded_pad[...])
            adapted = adapted + dot_tn(hot_p, r.pitch_table[...])
            adapted = adapted + dot_tn(hot_e, r.energy_table[...])
            b.h_lo[rows, :] = adapted.astype(BF16)
        attention_forward(layout, b, w, counts, length)
        b.first[length + 8 : length + 16, :] = jnp.zeros((8, D), F32)
        ffn_forward(b, w, length)
        for r0, size in tiles:
            rows = slice(r0, r0 + size)
            n, rstd = normed(b.second[rows, :])
            keep = (iota((size, 1), 0) + r0 < count).astype(F32)
            decoded = ((n * w.scales[1:2, :] + w.shifts[1:2, :]) * keep).astype(BF16)
            spectrum = dot_nt(r.mel_turned[...], decoded)
            if r0 < FRAMES // 2:
                o.mel_away[s, :, rows] = spectrum.astype(BF16)
            else:
                o.mel_own[s, :, r0 - FRAMES // 2 : r0 - FRAMES // 2 + size] = spectrum
            cotangent = r.mel_cotangent[s, :, rows]
            r.a_mel[...] += dot(cotangent, decoded)
            dy = dot_tn(cotangent, r.mel_turned[...]) * keep
            second_norm_back(b, w, r0, size, dy, n, rstd)
        ffn_backward(b, w, length)
        ffn_weight_grads(b, length)

        def finish(_, at, q, dh):
            b.datt[at : at + q, :] = dh.astype(BF16)

        attention_backward(layout, b, w, counts, length, finish)
        dadapted = b.datt[0:length, :]
        r.a_table[...] += dot(r.hot[:, 0:length], dadapted)
        o.dsent[s] = dot_tn(r.expand[0:length, :], dadapted)[0:PHONES].astype(BF16)

    def one(s):
        sequence(s, FRAMES)

    wait_weights(b, w)
    each(sequences, one)
    send_large_grads(b, o)
    store_block_grads(b, o)
    r.pack_far[:, 0 : 2 * BINS] = r.a_table[...].T.astype(BF16)
    r.pack_far[:, 2 * BINS :] = jnp.zeros((D, 128), BF16)
    r.pack_far[:, 2 * BINS : 2 * BINS + MELS] = r.a_mel[...].T.astype(BF16)


def section_call(name, inputs, outputs, branches, smem=(), kept=()):
    shapes = {n: (a.shape, a.dtype) for n, a in inputs.items()}

    def kernel(*refs):
        place = dict(zip(inputs, refs))
        target = dict(zip(outputs, refs[len(inputs) :]))

        def run(body, ins, outs, scratch):
            near_ins = [n for n in ins if n not in FAR and n not in smem]
            near_outs = [n for n in outs if n not in FAR]
            local = {n: pltpu.VMEM(*shapes[n]) for n in near_ins}
            local.update({n: pltpu.VMEM(*outputs[n]) for n in near_outs})
            local.update(scratch)
            local.update(
                sem_in=pltpu.SemaphoreType.DMA((len(near_ins),)),
                sem_out=pltpu.SemaphoreType.DMA((len(near_outs),)),
            )

            def scoped(*values):
                r = Refs(list(local), values)
                for n in ins:
                    if n not in near_ins:
                        setattr(r, n, place[n])
                for n in outs:
                    if n not in near_outs:
                        setattr(r, n, target[n])
                copies = [
                    pltpu.make_async_copy(place[n], getattr(r, n), r.sem_in.at[k])
                    for k, n in enumerate(near_ins)
                ]
                for copy in copies:
                    copy.start()
                for copy in copies:
                    copy.wait()
                body(r)
                copies = [
                    pltpu.make_async_copy(getattr(r, n), target[n], r.sem_out.at[k])
                    for k, n in enumerate(near_outs)
                ]
                for copy in copies:
                    copy.start()
                for copy in copies:
                    copy.wait()

            pl.run_scoped(scoped, *local.values())

        for section, branch in enumerate(branches):
            if branch is not None:
                here = (lax.axis_index(SECTION) == section).astype(jnp.int32)
                each(here, lambda _: run(*branch))

    index_in = list(inputs)
    return pl.pallas_call(
        kernel,
        name=name,
        in_specs=[
            pl.BlockSpec(memory_space=pltpu.SMEM if n in smem else pl.ANY) for n in inputs
        ],
        out_specs=[pl.BlockSpec(memory_space=pl.ANY)] * len(outputs),
        out_shape=[jax.ShapeDtypeStruct(*outputs[n]) for n in outputs],
        input_output_aliases={index_in.index(n): k for k, n in enumerate(outputs) if n in kept},
        compiler_params=pltpu.CompilerParams(vmem_limit_bytes=61 * 2**20),
    )(*inputs.values())


W_NAMES = tuple("w_" + n for n in WEIGHTS)
G_NAMES = tuple(GRADS)


def decoder_branch(sequences):
    scratch = dict(
        block_scratch(DEC, True),
        a_mel=pltpu.VMEM((MELS, D), F32),
        a_table=pltpu.VMEM((2 * BINS, D), F32),
        durations_pad=pltpu.VMEM((8, 256), jnp.int32),
        start=pltpu.VMEM((8, 256), jnp.int32),
        stop=pltpu.VMEM((8, 256), jnp.int32),
        encoded_pad=pltpu.VMEM((256, D), BF16),
        expand=pltpu.VMEM((FRAMES, 256), BF16),
        hot=pltpu.VMEM((2 * BINS, FRAMES), BF16),
    )
    ins = names(frames=1, arrived=1, durations=1, pitch_bins=1, energy_bins=1, pitch_table=1,
                energy_table=1, mel_turned=1, mel_cotangent=1)
    outs = names(mel_own=1, mel_away=1, dsent=1, pack_far=1)
    return functools.partial(decoder_kernel, sequences), ins + W_NAMES, outs + G_NAMES, scratch


def load_segments(b, phonemes):
    b.h_lo[...] = jnp.zeros_like(b.h_lo)
    for s in range(ENC.segments):
        b.h_lo[s * SLOT : s * SLOT + PHONES, :] = phonemes[s]


def slot_keep(counts, r0, size):
    row = iota((size, 1), 0) + r0
    kept = row < counts[0]
    for s in range(1, ENC.segments):
        kept = kept | ((row >= s * SLOT) & (row < s * SLOT + counts[s]))
    return kept.astype(F32)


def encoder_forward_kernel(r):
    b, w = r, Refs(WEIGHTS, [getattr(r, "w_" + n) for n in WEIGHTS])
    start_weights(b, w)
    counts = [r.counts[s] for s in range(ENC.segments)]
    start_block(ENC, b)
    load_segments(b, r.phonemes)
    attention_forward(ENC, b, w, counts, SLOT)
    wait_weights(b, w)
    ffn_forward(b, w, ENC.rows)
    for r0, size in pieces(ENC.rows, T):
        n, _ = normed(b.second[r0 : r0 + size, :])
        encoded = (n * w.scales[1:2, :] + w.shifts[1:2, :]) * slot_keep(counts, r0, size)
        b.second[r0 : r0 + size, :] = encoded
    for s in range(ENC.segments):
        encoded = b.second[s * SLOT : s * SLOT + PHONES, :]
        r.encoded[s] = encoded
        r.encoded_lo[s] = encoded.astype(BF16)


def encoder_backward_kernel(r):
    b, w, o = r, Refs(WEIGHTS, [getattr(r, "w_" + n) for n in WEIGHTS]), r
    start_weights(b, w)
    counts = [r.counts[s] for s in range(ENC.segments)]
    zero_accumulators(b, w)
    start_block(ENC, b)
    load_segments(b, r.phonemes)
    attention_forward(ENC, b, w, counts, SLOT)
    wait_weights(b, w)
    ffn_forward(b, w, ENC.rows)
    b.n1_grad[...] = jnp.zeros_like(b.n1_grad)
    for s in range(ENC.segments):
        b.n1_grad[s * SLOT : s * SLOT + PHONES, :] = r.grad_near[s] + r.grad_far[s].astype(F32)
    for r0, size in pieces(ENC.rows, T):
        n, rstd = normed(b.second[r0 : r0 + size, :])
        dy = b.n1_grad[r0 : r0 + size, :] * slot_keep(counts, r0, size)
        second_norm_back(b, w, r0, size, dy, n, rstd)
    ffn_backward(b, w, ENC.rows)
    make_large_grads(b, o, ENC.rows)

    def finish(s, at, q, dh):
        o.input_own[s] = dh[0 : PHONES // 2]
        o.input_away[s] = dh[PHONES // 2 : PHONES].astype(BF16)

    attention_backward(ENC, b, w, counts, SLOT, finish)
    store_block_grads(b, o)


def encoder_forward_branch():
    return (
        encoder_forward_kernel,
        names(counts=1, phonemes=1) + W_NAMES,
        names(encoded=1, encoded_lo=1),
        block_scratch(ENC, False),
    )


def encoder_backward_branch():
    return (
        encoder_backward_kernel,
        names(counts=1, phonemes=1, grad_near=1, grad_far=1) + W_NAMES,
        names(input_own=1, input_away=1) + G_NAMES,
        dict(block_scratch(ENC, True, True), n1_grad=pltpu.VMEM((ENC.rows, D), F32)),
    )


def halves(x):
    high = x.astype(BF16)
    return high, (x - high.astype(F32)).astype(BF16)


def predict(r, p, rows, keep, keep_row, hidden, cotangent, estimate):
    tiles = rows // T
    conv_a, conv_b = r.convs.at[p, 0], r.convs.at[p, 1]
    scale_a, scale_b = r.scales[p, 0:1, :], r.scales[p, 1:2, :]
    shift_a, shift_b = r.shifts[p, 0:1, :], r.shifts[p, 1:2, :]
    readout = r.readouts[pl.ds(p, 1), :]
    edge = jnp.zeros((8, D), F32)
    r.after[0:8, :] = edge
    r.after[rows + 8 : rows + 16, :] = edge

    def unfold(source, target, k):
        v = source[tile_rows(k, 16), :]
        for t in range(3):
            target[tile_rows(k), t * D : (t + 1) * D] = v[7 + t : 7 + t + T].astype(BF16)

    def fold(target, gradient, conv, k):
        r.dcols3[16 : 16 + T, :] = dot_nt(gradient, conv[...])
        total = r.dcols3[9 : 25 + T, 0:D]
        for t in range(1, 3):
            total = total + r.dcols3[9 - t : 25 - t + T, t * D : (t + 1) * D]
        target[tile_rows(k, 16), :] += total

    def clear(target):
        def body(k):
            target[tile_rows(k), :] = jnp.zeros((T, D), F32)

        each(tiles, body)
        target[rows : rows + 16, :] = jnp.zeros((16, D), F32)

    def first_half(k):
        at = tile_rows(k)
        unfold(hidden, r.cols_a, k)
        value, slope = gelu_pair(dot(r.cols_a[at, :], conv_a[...]))
        n, rstd = normed(value)
        r.slope_a[at, :] = slope
        r.norm_a[at, :] = n
        r.rstd_a[at, :] = rstd
        r.after[tile_rows(k, 0, 8), :] = (n * scale_a + shift_a) * keep(k * T, T)

    each(tiles, first_half)
    clear(r.dafter)
    weighted = readout * scale_b
    weighted_mean = jnp.mean(weighted, axis=1, keepdims=True)
    high, low = halves(readout)
    row = iota((16, D), 0)
    two = jnp.where(row == 0, high.astype(F32), jnp.where(row == 1, low.astype(F32), 0.0))
    two = two.astype(BF16)

    def second_half(k):
        at = span(k * T, T)
        unfold(r.after, r.cols_b, k)
        value, slope = gelu_pair(dot(r.cols_b[at, :], conv_b[...]))
        n, rstd = normed(value)
        after = n * scale_b + shift_b
        high, low = halves(after)
        with_high, with_low = dot_nt(two, high), dot_nt(two, low)
        guess = with_high[0:1] + with_high[1:2] + with_low[0:1]
        estimate[:, at] = guess * keep_row(k * T, T)
        column = jnp.broadcast_to(cotangent[:, at], (128, T)).T
        column = jnp.concatenate([column, column], axis=1) * keep(k * T, T)
        r.a_vec[p, 2:3, :] += readout * column_sum(column * n)
        r.a_vec[p, 3:4, :] += readout * column_sum(column)
        r.a_vec[p, 4:5, :] += column_sum(column * after)
        inner = jnp.mean(weighted * n, axis=1, keepdims=True)
        gradient = (column * (weighted - weighted_mean - n * inner) * rstd * slope).astype(BF16)
        r.grad_b[at, :] = gradient
        fold(r.dafter, gradient, conv_b, k)

    each(tiles, second_half)
    clear(hidden)

    def back(k):
        at = tile_rows(k)
        dy = r.dafter[tile_rows(k, 0, 8), :] * keep(k * T, T)
        n = r.norm_a[at, :]
        r.a_vec[p, 0:1, :] += column_sum(dy * n)
        r.a_vec[p, 1:2, :] += column_sum(dy)
        gradient = norm_back(dy * scale_a, n, r.rstd_a[at, :]) * r.slope_a[at, :]
        gradient = gradient.astype(BF16)
        r.grad_a[at, :] = gradient
        fold(hidden, gradient, conv_a, k)

    each(tiles, back)
    r.a_conv[p, 0] += dot_tn(r.grad_a[0:rows, :], r.cols_a[0:rows, :])
    r.a_conv[p, 1] += dot_tn(r.grad_b[0:rows, :], r.cols_b[0:rows, :])


def predictor_kernel(sequences, r):
    r.a_conv[...] = jnp.zeros_like(r.a_conv)
    r.a_vec[...] = jnp.zeros_like(r.a_vec)
    r.a_table[...] = jnp.zeros_like(r.a_table)
    r.dcols3[0:16, :] = jnp.zeros((16, 3 * D), F32)
    r.dcols3[16 + T :, :] = jnp.zeros((16, 3 * D), F32)
    r.durations_pad[...] = jnp.zeros_like(r.durations_pad)
    r.durations_pad[0:sequences, 0:PHONES] = r.durations[...]
    stop = span_ends(r.durations_pad[...])
    r.stop[...] = stop
    r.start[...] = stop - r.durations_pad[...]
    counts = [r.counts[s] for s in range(sequences)]
    slots = sequences * SLOT
    r.hidden[0, 0 : slots + 16, :] = jnp.zeros((slots + 16, D), F32)
    for s in range(sequences):
        r.hidden[0, s * SLOT + 8 : s * SLOT + 8 + PHONES, :] = r.encoded[s]

    def keep_slots(r0, size):
        return slot_keep(counts, r0, size)

    def keep_slots_row(r0, size):
        lane = iota((1, size), 1) + r0
        kept = lane < counts[0]
        for s in range(1, sequences):
            kept = kept | ((lane >= s * SLOT) & (lane < s * SLOT + counts[s]))
        return kept.astype(F32)

    predict(
        r, 0, slots, keep_slots, keep_slots_row, r.hidden.at[0], r.cot_duration, r.duration_pred
    )
    for s in range(sequences):
        r.dencoded[s] = r.hidden[0, s * SLOT + 8 : s * SLOT + 8 + PHONES, :]
    r.encoded_high[...] = jnp.zeros_like(r.encoded_high)
    r.encoded_low[...] = jnp.zeros_like(r.encoded_low)

    def one(s):
        count = r.frames[s]
        high, low = halves(r.encoded[s])
        r.encoded_high[0:PHONES, :] = high
        r.encoded_low[0:PHONES, :] = low
        start, stop = r.start[pl.ds(s, 1), :], r.stop[pl.ds(s, 1), :]
        edge = jnp.zeros((8, D), F32)
        for k in range(2):
            r.hidden[k, 0:8, :] = edge
            r.hidden[k, FRAMES + 8 : FRAMES + 16, :] = edge

        def embed(k):
            at = span(k * T, T)
            expand = expansion(start, stop, k * T, T)
            r.expand[at, :] = expand
            hot = hot_columns(r.pitch_bins[pl.ds(s, 1), at], count, k * T, T)
            r.hot[:, at] = hot
            frames = dot(expand, r.encoded_high[...]) + dot(expand, r.encoded_low[...])
            r.hidden[0, tile_rows(k, 0, 8), :] = frames
            pitched = frames + dot_tn(hot, r.pitch_table[...])
            r.hidden[1, tile_rows(k, 0, 8), :] = pitched

        each(FRAMES // T, embed)

        def keep(r0, size):
            return (iota((size, 1), 0) + r0 < count).astype(F32)

        def keep_row(r0, size):
            return (iota((1, size), 1) + r0 < count).astype(F32)

        def both(k):
            line = pl.ds(k * sequences + s, 1)
            predict(
                r, k + 1, FRAMES, keep, keep_row, r.hidden.at[k],
                r.cot_frames.at[line], r.frame_preds.at[line],
            )

        each(2, both)
        high, low = halves(r.hidden[1, 8 : FRAMES + 8, :])
        r.a_table[...] += dot(r.hot[...], high) + dot(r.hot[...], low)
        high, low = halves(r.hidden[0, 8 : FRAMES + 8, :] + r.hidden[1, 8 : FRAMES + 8, :])
        dencoded = dot_tn(r.expand[...], high) + dot_tn(r.expand[...], low)
        r.dencoded[s] = r.dencoded[s] + dencoded[0:PHONES]

    each(sequences, one)
    some = PHONES // 2
    r.away[...] = jnp.zeros_like(r.away)
    r.away[0 : 2 * sequences, :] = r.frame_preds[:, FRAMES // 2 :]
    for s in range(sequences):
        line = r.duration_pred[:, s * SLOT + some : s * SLOT + PHONES]
        r.away[2 * sequences + s : 2 * sequences + s + 1, 0:some] = line
    r.small[...] = r.away[...].astype(BF16)
    for p in range(3):
        for k in range(2):
            at = (2 * p + k) * 3 * D
            r.pack[:, at : at + 3 * D] = r.a_conv[p, k].astype(BF16)
    rows = jnp.concatenate([r.a_vec[p] for p in range(3)] + [jnp.zeros((104, D), F32)], axis=0)
    r.pack[:, AT_VECTORS:AT_TABLES] = rows.T.astype(BF16)
    r.pack[:, AT_TABLES : AT_TABLES + BINS] = r.a_table[...].T.astype(BF16)


def predictors_branch(sequences):
    return (
        functools.partial(predictor_kernel, sequences),
        names(frames=1, counts=1, encoded=1, durations=1, pitch_bins=1, convs=1, scales=1,
              shifts=1, readouts=1, pitch_table=1, cot_duration=1, cot_frames=1),
        names(duration_pred=1, frame_preds=1, small=1, dencoded=1, pack=1),
        dict(
            away=pltpu.VMEM((16, FRAMES // 2), F32),
            a_conv=pltpu.VMEM((3, 2, D, 3 * D), F32),
            a_vec=pltpu.VMEM((3, 8, D), F32),
            a_table=pltpu.VMEM((BINS, D), F32),
            durations_pad=pltpu.VMEM((8, 256), jnp.int32),
            start=pltpu.VMEM((8, 256), jnp.int32),
            stop=pltpu.VMEM((8, 256), jnp.int32),
            encoded_high=pltpu.VMEM((256, D), BF16),
            encoded_low=pltpu.VMEM((256, D), BF16),
            expand=pltpu.VMEM((FRAMES, 256), BF16),
            hot=pltpu.VMEM((BINS, FRAMES), BF16),
            hidden=pltpu.VMEM((2, FRAMES + 16, D), F32),
            after=pltpu.VMEM((FRAMES + 16, D), F32),
            dafter=pltpu.VMEM((FRAMES + 16, D), F32),
            cols_a=pltpu.VMEM((FRAMES, 3 * D), BF16),
            cols_b=pltpu.VMEM((FRAMES, 3 * D), BF16),
            slope_a=pltpu.VMEM((FRAMES, D), F32),
            norm_a=pltpu.VMEM((FRAMES, D), F32),
            rstd_a=pltpu.VMEM((FRAMES, 1), F32),
            grad_a=pltpu.VMEM((FRAMES, D), BF16),
            grad_b=pltpu.VMEM((FRAMES, D), BF16),
            dcols3=pltpu.VMEM((T + 32, 3 * D), F32),
        ),
    )


def swapped(array):
    return lax.ppermute(array, SECTION, [(0, 1), (1, 0)])


def scattered_anyhow(arrays):
    ways = lax.axis_size(DP)
    shares = [a.shape[0] // ways for a in arrays]
    flat = jnp.concatenate([a.reshape(ways, -1) for a in arrays], axis=1)
    flat = lax.psum_scatter(flat, DP, scatter_dimension=0, tiled=True)[0]
    out, at = [], 0
    for a, share in zip(arrays, shares):
        size = share * a.shape[1]
        out.append(flat[at : at + size].reshape(share, a.shape[1]).astype(F32))
        at += size
    return out


def scatter_kernel(steps, cuts, count, lists, trades, given, *refs):
    n, m = len(cuts), len(trades)
    late = given < m
    sources, refs = refs[:count], refs[count:]
    traded, refs = refs[:given], refs[given:]
    outs, refs = refs[:count], refs[count:]
    arrived, refs = refs[:m], refs[m:]
    mine, landed = refs[:n], refs[n : n * (1 + steps)]
    load_sem, send_sem, recv_sem, *rest = refs[n * (1 + steps) :]
    if m:
        trade_send, trade_recv = rest[:2]
    if late:
        rounded = rest[2]
        traded = traded + (rounded,)
    me = lax.axis_index(DP)
    bits = [lax.rem(lax.div(me, 1 << k), 2) for k in range(steps)]
    partners = [me + (1 << k) * (1 - 2 * bits[k]) for k in range(steps)]
    def trade(i):
        return pltpu.make_async_remote_copy(
            src_ref=traded[i],
            dst_ref=arrived[i],
            send_sem=trade_send.at[i],
            recv_sem=trade_recv.at[i],
            device_id={SECTION: 1 - lax.axis_index(SECTION)},
            device_id_type=pl.DeviceIdType.MESH,
        )

    def every(k):
        return (slice(None),) * (steps - 1 - k)

    def source(i, bit):
        array, first, size = cuts[i]
        return sources[array].at[every(0) + (bit, slice(None), pl.ds(first, size))]

    def load(i):
        return pltpu.make_async_copy(source(i, bits[0]), mine[i], load_sem.at[i])

    def copy(i, k):
        if k == 0:
            out = source(i, 1 - bits[0])
        else:
            out = landed[i * steps + k - 1].at[every(k) + (1 - bits[k],)]
        return pltpu.make_async_remote_copy(
            src_ref=out,
            dst_ref=landed[i * steps + k],
            send_sem=send_sem.at[i, k],
            recv_sem=recv_sem.at[i, k],
            device_id={DP: partners[k]},
            device_id_type=pl.DeviceIdType.MESH,
        )

    def finish(i, k):
        copy(i, k).wait_recv()
        if k == 0:
            load(i).wait()
        there = landed[i * steps + k]
        for index in itertools.product(range(2), repeat=steps - 1 - k):
            if k == 0:
                stayed = mine[i][index]
            else:
                stayed = landed[i * steps + k - 1][index + (bits[k],)]
            total = there[index].astype(F32) + stayed.astype(F32)
            if k == steps - 1:
                array, first, size = cuts[i]
                outs[array][:, first : first + size] = total
            else:
                there[index] = total.astype(BF16)
        if k < steps - 1:
            copy(i, k + 1).start()

    def begin(i):
        copy(i, 0).start()
        load(i).start()

    def run(section, chosen):
        barrier = pltpu.get_barrier_semaphore()
        for partner in partners if chosen else ():
            pl.semaphore_signal(
                barrier, inc=1, device_id={DP: partner}, device_id_type=pl.DeviceIdType.MESH
            )
        if any(sender != section for sender in trades):
            pl.semaphore_signal(
                barrier,
                inc=1,
                device_id={SECTION: 1 - lax.axis_index(SECTION)},
                device_id_type=pl.DeviceIdType.MESH,
            )
        pl.semaphore_wait(barrier, (steps if chosen else 0) + (1 if section in trades else 0))
        size = len(chosen)
        for i in range(given):
            if trades[i] == section:
                trade(i).start()
        last = [x for x, group in enumerate(chosen) for i in group if cuts[i][0] == count - 1]
        for turn in range(-AHEAD, size + steps - 1):
            if turn + AHEAD < size:
                for i in chosen[turn + AHEAD]:
                    begin(i)
            for k in range(steps):
                at = turn - k
                if 0 <= at < size:
                    for i in chosen[at]:
                        finish(i, k)
                    if late and trades[-1] == section and k == steps - 1 and at == last[-1]:
                        rounded[...] = outs[count - 1][...].astype(BF16)
                        trade(m - 1).start()
        for i in itertools.chain(*chosen):
            for k in range(steps):
                copy(i, k).wait_send()
        for i in range(m):
            if trades[i] == section:
                trade(i).wait_send()
            else:
                trade(i).wait_recv()

    for section, chosen in enumerate(lists):
        if chosen or m:
            here = (lax.axis_index(SECTION) == section).astype(jnp.int32)
            each(here, functools.partial(one_time, run, section, chosen))


def one_time(run, section, chosen, _):
    run(section, chosen)


def scattered(arrays, name, collective, width, parts, traded, trades):
    ways = lax.axis_size(DP)
    steps = ways.bit_length() - 1
    if ways != 1 << steps or any(a.shape[0] // ways % 16 for a in arrays):
        sums = scattered_anyhow(arrays)
        traded = [*traded, sums[-1].astype(BF16)]
        return sums + [
            lax.ppermute(a, SECTION, [(s, 1 - s)]) for a, s in zip(traded, trades)
        ]
    shares = [a.shape[0] // ways for a in arrays]
    cuts = [
        (k, at, size)
        for k, a in enumerate(arrays)
        for at, size in pieces(a.shape[1], width if a.shape[0] > 1024 else 768)
    ]
    lists = []
    for part in parts:
        turns = [[i] for i, cut in enumerate(cuts) if cut[0] == 0 and 0 in part]
        others = [i for i, cut in enumerate(cuts) if cut[0] > 0 and cut[0] in part]
        for x, i in enumerate(others):
            turns[x % len(turns)].append(i)
        lists.append(turns)
    landed = [
        pltpu.VMEM((2,) * (steps - 1 - k) + (shares[array], size), BF16)
        for array, _, size in cuts
        for k in range(steps)
    ]
    mine = [pltpu.VMEM((2,) * (steps - 1) + (shares[array], size), BF16) for array, _, size in cuts]
    scratch = [
        *mine,
        *landed,
        pltpu.SemaphoreType.DMA((len(cuts),)),
        pltpu.SemaphoreType.DMA((len(cuts), steps)),
        pltpu.SemaphoreType.DMA((len(cuts), steps)),
    ]
    outs = [jax.ShapeDtypeStruct((share, a.shape[1]), F32) for share, a in zip(shares, arrays)]
    far, near = pl.BlockSpec(memory_space=pl.ANY), pl.BlockSpec(memory_space=pltpu.VMEM)
    out_specs = [near] * len(outs)
    scratch += [pltpu.SemaphoreType.DMA((len(trades),))] * 2
    sums = jax.ShapeDtypeStruct(outs[-1].shape, BF16)
    outs += [jax.ShapeDtypeStruct(a.shape, a.dtype) for a in traded]
    out_specs += [far] * len(traded)
    if len(trades) > len(traded):
        scratch.append(pltpu.VMEM(sums.shape, BF16))
        outs.append(sums)
        out_specs.append(near)
    return pl.pallas_call(
        functools.partial(
            scatter_kernel, steps, cuts, len(arrays), lists, tuple(trades), len(traded)
        ),
        name=name,
        in_specs=[far] * (len(arrays) + len(traded)),
        out_specs=out_specs,
        out_shape=outs,
        scratch_shapes=scratch,
        compiler_params=pltpu.CompilerParams(
            collective_id=collective, has_side_effects=True, vmem_limit_bytes=60 * 2**20
        ),
    )(
        *[a.reshape((2,) * steps + (share, a.shape[1])) for share, a in zip(shares, arrays)],
        *traded,
    )


def body(phonemes, phone_lengths, durations, pitch_bins, energy_bins, joint_weight, output_weight,
         widen_weight, narrow_weight, block_scales, block_shifts, predictor_convs,
         predictor_scales, predictor_shifts, predictor_outputs, pitch_table, energy_table,
         mel_weight, mel_cotangent, duration_cotangent, pitch_cotangent, energy_cotangent):
    first = lax.axis_index(SECTION) == 0
    n = phonemes.shape[0]
    frames = jnp.sum(durations, axis=1)
    block_weights = (joint_weight[0], output_weight[0], widen_weight[0], narrow_weight[0],
                     block_scales[0], block_shifts[0])
    weights = dict(zip(W_NAMES, block_weights))
    cot_duration = jnp.pad(duration_cotangent, ((0, 0), (0, SLOT - PHONES))).reshape(1, n * SLOT)
    cot_frames = jnp.concatenate([pitch_cotangent, energy_cotangent])
    encoded, encoded_lo = section_call(
        "encoder_forward",
        dict(counts=phone_lengths, phonemes=phonemes, **weights),
        dict(encoded=((n, PHONES, D), F32), encoded_lo=((n, PHONES, D), BF16)),
        (encoder_forward_branch(), None),
        smem=names(counts=1),
    )
    arrived = lax.ppermute(encoded_lo, SECTION, [(0, 1)])
    duration, preds, small, mel_own, mel_away, dencoded, dsent, *grads, pack, pack_far = section_call(
        "predictors_or_decoder",
        dict(
            frames=frames,
            counts=phone_lengths,
            encoded=encoded,
            arrived=arrived,
            durations=durations,
            pitch_bins=pitch_bins,
            energy_bins=energy_bins,
            convs=predictor_convs,
            scales=predictor_scales,
            shifts=predictor_shifts,
            readouts=predictor_outputs,
            pitch_table=pitch_table,
            energy_table=energy_table,
            mel_turned=mel_weight.T,
            mel_cotangent=mel_cotangent.transpose(0, 2, 1),
            cot_duration=cot_duration,
            cot_frames=cot_frames,
            **weights,
        ),
        dict(
            duration_pred=((1, n * SLOT), F32),
            frame_preds=((2 * n, FRAMES), F32),
            small=((16, FRAMES // 2), BF16),
            mel_own=((n, MELS, FRAMES // 2), F32),
            mel_away=((n, MELS, FRAMES // 2), BF16),
            dencoded=((n, PHONES, D), F32),
            dsent=((n, PHONES, D), BF16),
            **GRADS,
            pack=((D, NEAR_PACK), BF16),
            pack_far=((D, PACK - AT_TABLES), BF16),
        ),
        (predictors_branch(n), decoder_branch(n)),
        smem=names(frames=1, counts=1),
    )
    pack, returned = scattered([pack], "pack_sums", 1, 768, ((0,), ()), (dsent,), (1,))
    input_own, input_away, *grads = section_call(
        "encoder_backward",
        dict(
            counts=phone_lengths,
            phonemes=phonemes,
            grad_near=dencoded,
            grad_far=returned,
            **weights,
            **dict(zip(G_NAMES, grads)),
        ),
        dict(
            input_own=((n, PHONES // 2, D), F32),
            input_away=((n, PHONES // 2, D), BF16),
            **GRADS,
        ),
        (encoder_backward_branch(), None),
        smem=names(counts=1),
        kept=G_NAMES,
    )
    sums = dict(zip(G_NAMES, grads))
    order = names(g_widen=1, g_narrow=1, g_joint=1, g_output=1, g_vec=1)
    sums = scattered(
        [sums[n] for n in order] + [pack_far],
        "block_sums",
        2,
        128,
        (range(5), range(6)),
        (pack, small, input_away, mel_away),
        (0, 0, 0, 1, 1),
    )
    near_pack, small, input_away, mel_away, far_pack = sums[6:]
    own = dict(zip(order, sums))
    return assembled(
        n,
        sums[0].shape[0],
        dict(
            **own,
            pack=pack,
            pack_far=sums[5],
            duration=duration,
            preds=preds,
            mel_own=mel_own,
            input_own=input_own,
            near_pack=near_pack,
            small=small,
            input_away=input_away,
            mel_away=mel_away,
            far_pack=far_pack,
        ),
    )


def assemble_kernel(n, ins, outs, *refs):
    far, refs = refs[: len(ins)], refs[len(ins) :]
    outs_refs, (*near, sem) = refs[: len(outs)], refs[len(outs) :]
    copies = [
        pltpu.make_async_copy(a, b, sem.at[k]) for k, (a, b) in enumerate(zip(far, near))
    ]
    for copy in copies:
        copy.start()
    for copy in copies:
        copy.wait()
    r = Refs(ins + outs, [*near, *outs_refs])
    first = lax.axis_index(SECTION) == 0
    half, some = FRAMES // 2, PHONES // 2

    def choose(near, far):
        return jnp.where(first, near.astype(F32), far.astype(F32))

    for s in range(n):
        r.o_mel[s] = choose(r.mel_away[s], r.mel_own[s])
        r.o_input[s] = choose(r.input_own[s], r.input_away[s])
    small = r.small[...].astype(F32)
    preds = choose(r.preds[:, 0:half], small[0 : 2 * n, :])
    r.o_pitch[...] = preds[0:n]
    r.o_energy[...] = preds[n : 2 * n]
    for s in range(n):
        r.o_duration[s : s + 1, :] = choose(
            r.duration[:, s * SLOT : s * SLOT + some], small[2 * n + s : 2 * n + s + 1, 0:some]
        )
    r.o_joint[0] = r.g_joint[...]
    r.o_output[0] = r.g_output[...]
    r.o_widen[0] = r.g_widen[...]
    r.o_narrow[0] = r.g_narrow[...]
    share = r.pack.shape[0]
    block_vec = r.g_vec[...].T
    vec = choose(r.pack[:, AT_VECTORS:AT_TABLES], r.near_pack[:, AT_VECTORS:AT_TABLES]).T
    for k in range(2):
        r.o_block_scales[0, k : k + 1, :] = block_vec[2 * k : 2 * k + 1, 0:share]
        r.o_block_shifts[0, k : k + 1, :] = block_vec[2 * k + 1 : 2 * k + 2, 0:share]
        for p in range(3):
            at = (2 * p + k) * 3 * D
            r.o_convs[p, k] = choose(
                r.pack[:, at : at + 3 * D], r.near_pack[:, at : at + 3 * D]
            )
            row = 8 * p + 2 * k
            r.o_scales[p, k : k + 1, :] = vec[row : row + 1, 0:share]
            r.o_shifts[p, k : k + 1, :] = vec[row + 1 : row + 2, 0:share]
    for p in range(3):
        r.o_readouts[p : p + 1, :] = vec[8 * p + 4 : 8 * p + 5, 0:share]
    near = choose(r.pack[:, AT_TABLES:], r.near_pack[:, AT_TABLES:])
    far = choose(r.far_pack[...], r.pack_far[...])
    r.o_pitch_table[...] = near + far[:, 0:BINS]
    r.o_energy_table[...] = far[:, BINS : 2 * BINS]
    r.o_mel_weight[...] = far[:, 2 * BINS : 2 * BINS + MELS]


def assembled(n, widen_rows, ins):
    share = ins[names(pack=1)[0]].shape[0]
    narrow_rows = FF * share // D
    outs = dict(
        o_mel=(n, MELS, FRAMES // 2),
        o_duration=(n, PHONES // 2),
        o_pitch=(n, FRAMES // 2),
        o_energy=(n, FRAMES // 2),
        o_input=(n, PHONES // 2, D),
        o_joint=(1, share, 3 * D),
        o_output=(1, share, D),
        o_widen=(1, widen_rows, FF),
        o_narrow=(1, narrow_rows, D),
        o_block_scales=(1, 2, share),
        o_block_shifts=(1, 2, share),
        o_convs=(3, 2, share, 3 * D),
        o_scales=(3, 2, share),
        o_shifts=(3, 2, share),
        o_readouts=(3, share),
        o_pitch_table=(share, BINS),
        o_energy_table=(share, BINS),
        o_mel_weight=(share, MELS),
    )
    whole = pl.BlockSpec(memory_space=pltpu.VMEM)
    results = pl.pallas_call(
        functools.partial(assemble_kernel, n, list(ins), list(outs)),
        name="assemble",
        in_specs=[pl.BlockSpec(memory_space=pl.ANY)] * len(ins),
        out_specs=[whole] * len(outs),
        out_shape=[jax.ShapeDtypeStruct(shape, F32) for shape in outs.values()],
        scratch_shapes=[
            *[pltpu.VMEM(a.shape, a.dtype) for a in ins.values()],
            pltpu.SemaphoreType.DMA((len(ins),)),
        ],
        compiler_params=pltpu.CompilerParams(vmem_limit_bytes=61 * 2**20),
    )(*ins.values())
    results = list(results)
    results[0] = results[0].transpose(0, 2, 1)
    results[11] = results[11].transpose(0, 1, 3, 2)
    results[15], results[16] = results[15].T, results[16].T
    return tuple(results)


def solution(mesh):
    halves_of_rows = P(DP, SECTION)
    row, rows, blocks = P(DP), P(DP, None), P(DP, None, None)
    table, block_sums = P(SECTION, None, None), P(SECTION, DP, None)
    block_vectors, vectors, columns = P(SECTION, None, DP), P(None, None, DP), P(None, DP)
    return jax.shard_map(
        body,
        mesh=mesh,
        in_specs=(blocks, row, rows, rows, rows) + (table,) * 6 + (P(),) * 7
        + (blocks, rows, rows, rows),
        out_specs=(
            P(DP, SECTION, None),
            halves_of_rows,
            halves_of_rows,
            halves_of_rows,
            P(DP, SECTION, None),
            *(block_sums,) * 4,
            block_vectors,
            block_vectors,
            P(None, None, None, DP),
            vectors,
            vectors,
            columns,
            columns,
            columns,
            rows,
        ),
        check_vma=False,
    )
```
